256 devices in a mesh: mode: 8 (over x, core), elem: 32 (over z, y).
Axes of the slice: x: 4, y: 4, z: 8, core: 2. Of those that a mesh axis runs over, the one named last changes fastest.
Arguments:
- forcing: float32 [128, 81, 4096], P('mode', None, 'elem'), may hold values from -300 to 300
- metric: float32 [4, 81, 4096], P(None, None, 'elem'), as said below
- edge_map: int32 [4096, 32], P('elem'), may hold values from 0 to 2112, as said below
- shared_rows: int32 [12288], P('elem'), may hold values from 0 to 2112, as said below
- partner_masks: int32 [12288], P('elem'), may hold values from 1 to 16, as said below
- penalty: float32 [67616], P('elem'), may hold values from 50 to 500
Outputs:
- pressure: float32 [128, 81, 4096], P('mode', None, 'elem')
The draws below stay inside these ranges and needn't reach their ends.
Inputs may be any that keep to these rules, and one draw needn't show every extreme that they name: `edge_map`: entries index skeleton nodes of the element's own device; an element's 32 entries are distinct, and every skeleton node of a device is named by some element of it. `shared_rows`: each device's 384 slots name distinct skeleton nodes on the perimeter of that device's patch of elements. `partner_masks`: every entry has exactly one bit set. Along each device's slots the pattern is constant over four runs in order, of lengths 8 * 8 + 1, 65, 127 and 127. The partner device of a slot holds the same pattern at that slot. `metric`: at every node the first, second and fourth components are positive and the third's magnitude is at most half the geometric mean of the first two.
All inputs are finite; a program needn't handle non-finite values.
Results may differ from the reference program's by a relative error of at most 0.0003.
Values sent between devices are 32-bit elements; how exact they have to be, the bound alone decides.
No kernel may reach another device: no remote copies, remote signals or barrier semaphores. Data moves between devices by JAX's collectives and lax.ppermute only.
A program may use at most 64 MiB of HBM per device.

```python
import math
import jax
import jax.numpy as jnp
import numpy as np
from jax import lax

ORDER = 8
EX = 16
EY = 8
ITERS = 2
E_DEV = 128
ELEMS = 4096
NODES = 81
CYCLE = 32
SKEL = 2113
NSKEL = 67616
SH = 384
NSH = 12288
PLANES = 128
N_ELEM = 32


def grid_tables():
    extent_first = ORDER * EX + 1
    extent_second = ORDER * EY + 1
    grid_first, grid_second = np.meshgrid(np.arange(extent_first), np.arange(extent_second), indexing='ij')
    on_skeleton = (grid_first % ORDER == 0) | (grid_second % ORDER == 0)
    ranking = np.cumsum(on_skeleton.reshape(-1)) - 1
    cycle_first = np.concatenate([np.arange(ORDER + 1), np.arange(ORDER + 1), np.zeros(ORDER - 1, np.int64), np.full(ORDER - 1, ORDER)])
    cycle_second = np.concatenate([np.zeros(ORDER + 1, np.int64), np.full(ORDER + 1, ORDER), np.arange(1, ORDER), np.arange(1, ORDER)])
    element_ids = np.arange(EX * EY)
    node_first = ORDER * (element_ids // EY)[:, None] + cycle_first[None, :]
    node_second = ORDER * (element_ids % EY)[:, None] + cycle_second[None, :]
    cycle_rank = ranking[node_first * extent_second + node_second]
    along_second = np.arange(extent_second)
    along_first = np.arange(1, extent_first - 1)
    side_low_first = ranking[along_second]
    side_high_first = ranking[(extent_first - 1) * extent_second + along_second]
    side_low_second = ranking[along_first * extent_second]
    side_high_second = ranking[along_first * extent_second + extent_second - 1]
    sides = [side_low_first, side_high_first, side_low_second, side_high_second]
    return (cycle_rank.astype(np.int32), [np.asarray(side, np.int32) for side in sides])


def numbering(key):
    base = jax.random.fold_in(key, 101)
    device_ids = jnp.arange(N_ELEM, dtype=jnp.int32)
    return jax.vmap(lambda device: jax.random.permutation(jax.random.fold_in(base, device), SKEL))(device_ids).astype(jnp.int32)


def patch_layout(key):
    total_bits = int(N_ELEM).bit_length() - 1
    bits_first = (total_bits + 1) // 2
    bits_second = total_bits // 2
    count_first = 2 ** bits_first
    count_second = 2 ** bits_second
    steps_first = np.arange(count_first)
    steps_second = np.arange(count_second)
    gray_first = steps_first ^ steps_first >> 1
    gray_second = steps_second ^ steps_second >> 1
    code = gray_first[:, None] * count_second + gray_second[None, :]
    code_bits = np.stack([code >> level & 1 for level in range(total_bits)], axis=-1).astype(np.int32)
    bit_order = jax.random.permutation(jax.random.fold_in(key, 1011), total_bits).astype(jnp.int32)
    offset = jax.random.randint(jax.random.fold_in(key, 1013), (), 0, N_ELEM, jnp.int32)
    powers = jnp.left_shift(jnp.int32(1), bit_order)
    device = jnp.sum(jnp.asarray(code_bits) * powers[None, None, :], axis=-1).astype(jnp.int32)
    device = jnp.bitwise_xor(device, offset)
    even_first = jnp.asarray(np.broadcast_to((steps_first % 2 == 0)[:, None], (count_first, count_second)))
    even_second = jnp.asarray(np.broadcast_to((steps_second % 2 == 0)[None, :], (count_first, count_second)))
    before_first = jnp.roll(device, 1, axis=0)
    after_first = jnp.roll(device, -1, axis=0)
    before_second = jnp.roll(device, 1, axis=1)
    after_second = jnp.roll(device, -1, axis=1)
    masks = jnp.stack([jnp.bitwise_xor(device, jnp.where(even_first, before_first, after_first)), jnp.bitwise_xor(device, jnp.where(even_first, after_first, before_first)), jnp.bitwise_xor(device, jnp.where(even_second, before_second, after_second)), jnp.bitwise_xor(device, jnp.where(even_second, after_second, before_second))], axis=-1).reshape(-1, 4)
    position_of = jnp.zeros((N_ELEM,), jnp.int32).at[device.reshape(-1)].set(jnp.arange(N_ELEM, dtype=jnp.int32))
    return (masks[position_of], even_first.reshape(-1)[position_of], even_second.reshape(-1)[position_of])


def draw_edge_map(key, part):
    orders = numbering(key)
    cycle_rank, sides = grid_tables()
    return orders[:, jnp.asarray(cycle_rank)].reshape(ELEMS, CYCLE)


def draw_shared_rows(key, part):
    orders = numbering(key)
    masks, even_first, even_second = patch_layout(key)
    cycle_rank, sides = grid_tables()
    low_first, high_first, low_second, high_second = [jnp.asarray(side)[None, :] for side in sides]
    first_even = even_first[:, None]
    second_even = even_second[:, None]
    ranks = jnp.concatenate([jnp.where(first_even, low_first, high_first), jnp.where(first_even, high_first, low_first), jnp.where(second_even, low_second, high_second), jnp.where(second_even, high_second, low_second)], axis=1)
    return jnp.take_along_axis(orders, ranks, axis=1).reshape(NSH)


def draw_partner_masks(key, part):
    masks, even_first, even_second = patch_layout(key)
    run_lengths = [ORDER * EY + 1, ORDER * EY + 1, ORDER * EX - 1, ORDER * EX - 1]
    runs = [jnp.broadcast_to(masks[:, index:index + 1], (N_ELEM, run_lengths[index])) for index in range(4)]
    return jnp.concatenate(runs, axis=1).reshape(NSH).astype(jnp.int32)


def draw_metric(key, part):
    key = jax.random.fold_in(key, 3)
    keys = jax.random.split(key, 5)
    shape = (NODES, ELEMS)
    stretch_first = jnp.exp(jax.random.uniform(keys[0], shape, jnp.float32, math.log(0.5), math.log(2.0)))
    stretch_second = jnp.exp(jax.random.uniform(keys[1], shape, jnp.float32, math.log(0.5), math.log(2.0)))
    shear = jax.random.uniform(keys[2], shape, jnp.float32, -0.5, 0.5)
    element_scale = jnp.exp(jax.random.uniform(keys[3], (1, ELEMS), jnp.float32, math.log(0.5), math.log(2.0)))
    mass = jnp.exp(jax.random.uniform(keys[4], shape, jnp.float32, math.log(0.1), math.log(1.0))) * element_scale
    cross_term = shear * jnp.sqrt(stretch_first * stretch_second) * element_scale
    return jnp.stack([stretch_first * element_scale, stretch_second * element_scale, cross_term, mass]).astype(jnp.float32)


def block_scale(key, extent, pieces, smallest, largest):
    gain = 1.0
    for axis_at, shards_of in pieces:
        steps = jax.random.uniform(jax.random.fold_in(jax.random.fold_in(key, 6), axis_at), (shards_of,), jnp.float32, smallest / len(pieces), largest / len(pieces))
        gain = gain * jnp.repeat(jnp.exp(steps), extent[axis_at] // shards_of).reshape((-1,) + (1,) * (len(extent) - 1 - axis_at))
    return gain


def bell_draw(stream_key, extent, width, reach, cuts=(), kind=jnp.bfloat16):
    array = width * jax.random.normal(stream_key, extent, jnp.float32)
    if cuts:
        array = array * block_scale(stream_key, extent, cuts, -0.22, 0.18)
    return jnp.clip(array, -reach, reach).astype(kind)


def setup_inputs(seed: int = 0) -> dict:
    arg_keys = jax.random.split(jax.random.key(seed), 7)
    return {
        "forcing": bell_draw(arg_keys[0], (PLANES, NODES, ELEMS), 50.0, 300.0, ((0, 8), (2, 32)), jnp.float32),
        "metric": draw_metric(jax.random.fold_in(arg_keys[6], 71), 0),
        "edge_map": draw_edge_map(jax.random.fold_in(arg_keys[6], 71), 0),
        "shared_rows": draw_shared_rows(jax.random.fold_in(arg_keys[6], 71), 0),
        "partner_masks": draw_partner_masks(jax.random.fold_in(arg_keys[6], 71), 0),
        "penalty": jnp.clip(jnp.exp(math.log(500.0) - 2.3025851 * jax.random.uniform(arg_keys[5], (NSKEL,), jnp.float32) ** block_scale(arg_keys[5], (NSKEL,), ((0, 32),), -0.2, 0.2)), 50.0, 500.0),
    }


plane_spacing = 0.25


def legendre_table(points, poly_order):
    table = np.zeros((points.shape[0], poly_order + 1))
    table[:, 0] = 1.0
    table[:, 1] = points
    for degree in range(2, poly_order + 1):
        table[:, degree] = ((2 * degree - 1) * points * table[:, degree - 1] - (degree - 1) * table[:, degree - 2]) / degree
    return table


def lobatto_derivative(poly_order):
    node_count = poly_order + 1
    points = np.cos(np.pi * np.arange(node_count) / poly_order)
    for newton_step in range(100):
        table = legendre_table(points, poly_order)
        points = points - (points * table[:, poly_order] - table[:, poly_order - 1]) / (node_count * table[:, poly_order])
    points = np.sort(points)
    top_values = legendre_table(points, poly_order)[:, poly_order]
    identity = np.eye(node_count)
    differ = points[:, None] - points[None, :] + identity
    matrix = top_values[:, None] / (top_values[None, :] * differ)
    matrix = matrix * (1.0 - identity)
    matrix[0, 0] = -poly_order * node_count / 4.0
    matrix[poly_order, poly_order] = poly_order * node_count / 4.0
    return matrix


def fourier_tables(planes):
    positions = jnp.arange(planes, dtype=jnp.int32)
    wavenumber = positions // 2
    phases = ((wavenumber[:, None] * positions[None, :]) % planes).astype(jnp.float32) * (2.0 * math.pi / planes)
    cosine = jnp.cos(phases)
    sine_table = jnp.sin(phases)
    is_even = (positions % 2 == 0)[:, None]
    nyquist = (positions == 1)[:, None]
    alternate = (1 - 2 * (positions % 2)).astype(jnp.float32)[None, :]
    forward = jnp.where(nyquist, alternate, jnp.where(is_even, cosine, -sine_table)) / planes
    backward = jnp.where(is_even, 2.0 * cosine, -2.0 * sine_table)
    backward = jnp.where(nyquist, alternate, backward)
    backward = jnp.where((positions == 0)[:, None], 1.0, backward)
    return forward, backward.T


def helmholtz_shift(rows_global, planes):
    wavenumber = (rows_global // 2).astype(jnp.float32)
    spanwise = wavenumber * (2.0 * math.pi / (planes * plane_spacing))
    spanwise = jnp.where(rows_global == 1, math.pi / plane_spacing, spanwise)
    return spanwise * spanwise


def cycle_of(values_grid):
    last_node = values_grid.shape[-2] - 1
    return jnp.concatenate([values_grid[..., :, 0, :], values_grid[..., :, last_node, :], values_grid[..., 0, 1:last_node, :], values_grid[..., last_node, 1:last_node, :]], axis=-2)


def element_of(interior, boundary):
    node_count = interior.shape[-2] + 2
    side_bottom = boundary[..., 0:node_count, :]
    side_top = boundary[..., node_count:2 * node_count, :]
    side_left = boundary[..., 2 * node_count:3 * node_count - 2, :]
    side_right = boundary[..., 3 * node_count - 2:, :]
    middle = jnp.concatenate([side_left[..., None, :, :], interior, side_right[..., None, :, :]], axis=-3)
    return jnp.concatenate([side_bottom[..., :, None, :], middle, side_top[..., :, None, :]], axis=-2)


def element_apply(values_grid, metric, shift_row, derivative):
    grad_first = jnp.einsum("ik,...kje->...ije", derivative, values_grid, precision=lax.Precision.HIGHEST)
    grad_second = jnp.einsum("jk,...ike->...ije", derivative, values_grid, precision=lax.Precision.HIGHEST)
    flux_first = metric[0] * grad_first + metric[2] * grad_second
    flux_second = metric[2] * grad_first + metric[1] * grad_second
    result = jnp.einsum("ki,...kje->...ije", derivative, flux_first, precision=lax.Precision.HIGHEST)
    result = result + jnp.einsum("kj,...ike->...ije", derivative, flux_second, precision=lax.Precision.HIGHEST)
    return result + shift_row * metric[3] * values_grid


def element_diagonal(metric, derivative):
    squared = derivative * derivative
    term_first = jnp.einsum("ki,...kje->...ije", squared, metric[0], precision=lax.Precision.HIGHEST)
    term_second = jnp.einsum("kj,...ike->...ije", squared, metric[1], precision=lax.Precision.HIGHEST)
    corner = jnp.diagonal(derivative)
    cross_term = 2.0 * (corner[:, None] * corner[None, :])[:, :, None] * metric[2]
    return term_first + term_second + cross_term


def reference(forcing, metric, edge_map, shared_rows, partner_masks, penalty):
    derivative = jnp.asarray(lobatto_derivative(ORDER), jnp.float32)
    nodes_side = ORDER + 1
    devices = N_ELEM
    forward, backward = fourier_tables(PLANES)
    geometry = metric.reshape(4, nodes_side, nodes_side, devices, E_DEV).transpose(0, 3, 1, 2, 4)
    node_map = edge_map.reshape(devices, E_DEV, CYCLE).transpose(0, 2, 1)
    slot_rows = shared_rows.reshape(devices, SH)
    device_ids = jnp.arange(devices, dtype=jnp.int32)
    partners = jnp.bitwise_xor(device_ids[:, None], partner_masks.reshape(devices, SH))
    slot_ids = jnp.broadcast_to(jnp.arange(SH, dtype=jnp.int32)[None, :], (devices, SH))
    local_penalty = penalty.reshape(devices, SKEL)
    weights = jnp.ones((devices, SKEL), jnp.float32).at[device_ids[:, None], slot_rows].set(0.5)

    def gather_cycle(skeleton):
        return jax.vmap(lambda values, positions: values[positions])(skeleton, node_map)

    def scatter_cycle(cycle_values):
        return jax.vmap(lambda values, positions: jnp.zeros((SKEL,), jnp.float32).at[positions].add(values))(cycle_values, node_map)

    def share_rows(skeleton):
        slot_values = jnp.take_along_axis(skeleton, slot_rows, axis=1)
        received = slot_values[partners, slot_ids]
        return skeleton.at[device_ids[:, None], slot_rows].add(received)

    def assemble(values_grid, addition):
        return values_grid[:, 1:ORDER, 1:ORDER, :], share_rows(scatter_cycle(cycle_of(values_grid)) + addition)

    lap_interior, lap_skeleton = assemble(element_diagonal(geometry, derivative), local_penalty)
    mass_interior, mass_skeleton = assemble(geometry[3], 0.0)

    def operate(interior, skeleton, shift_row):
        values_grid = element_of(interior, gather_cycle(skeleton))
        result = element_apply(values_grid, geometry, shift_row, derivative)
        return assemble(result, local_penalty * skeleton)

    def inner_product(left_pair, right_pair):
        return jnp.sum(left_pair[0] * right_pair[0]) + jnp.sum(left_pair[1] * right_pair[1] * weights)

    def solve_row(arguments):
        source, shift_row = arguments
        right_side = assemble(source, 0.0)
        diag_interior = lap_interior + shift_row * mass_interior
        diag_skeleton = lap_skeleton + shift_row * mass_skeleton
        residual = right_side
        precond = (residual[0] / diag_interior, residual[1] / diag_skeleton)
        search = precond
        solution = (jnp.zeros_like(right_side[0]), jnp.zeros_like(right_side[1]))
        current = inner_product(residual, precond)
        for iteration in range(ITERS):
            applied = operate(search[0], search[1], shift_row)
            step_size = current / inner_product(search, applied)
            solution = (solution[0] + step_size * search[0], solution[1] + step_size * search[1])
            residual = (residual[0] - step_size * applied[0], residual[1] - step_size * applied[1])
            if iteration + 1 < ITERS:
                precond = (residual[0] / diag_interior, residual[1] / diag_skeleton)
                following = inner_product(residual, precond)
                conjugate = following / current
                search = (precond[0] + conjugate * search[0], precond[1] + conjugate * search[1])
                current = following
        return element_of(solution[0], gather_cycle(solution[1]))

    coefficients = jnp.dot(forward, forcing.reshape(PLANES, -1), precision=lax.Precision.HIGHEST)
    coefficients = coefficients.reshape(PLANES, nodes_side, nodes_side, devices, E_DEV).transpose(0, 3, 1, 2, 4)
    shifts = helmholtz_shift(jnp.arange(PLANES, dtype=jnp.int32), PLANES)
    solutions = lax.map(solve_row, (coefficients, shifts))
    solutions = solutions.transpose(0, 2, 3, 1, 4).reshape(PLANES, -1)
    pressure = jnp.dot(backward, solutions, precision=lax.Precision.HIGHEST)
    return pressure.reshape(PLANES, NODES, ELEMS)
```

```python
import math

import jax
import jax.numpy as jnp
import numpy as np
from jax import lax
from jax.experimental import pallas as pl
from jax.experimental.pallas import tpu as pltpu
from jax.sharding import PartitionSpec as P

ORDER = 8
SIDE = ORDER + 1
NODES = SIDE * SIDE
CYCLE = 32
INNER = (ORDER - 1) ** 2
ROWS = 16
LANES = 128
PLANES = 128
MODES = 8
ELEMS_AXIS = 32
SKEL = 2113
LOW = 256
HIGH = 9
TILES = 2 * HIGH
SLOTS = 384
SLOT_TILES = SLOTS // LANES
BLOCK = 9
PACKED = MODES * BLOCK
SCALARS = 5
SPACING = 0.25
F32 = jnp.float32
BF16 = jnp.bfloat16
HIGHEST = lax.Precision.HIGHEST
VMEM_LIMIT = 56 * 1024 * 1024


def legendre_table(points, poly_order):
    table = np.zeros((points.shape[0], poly_order + 1))
    table[:, 0] = 1.0
    table[:, 1] = points
    for degree in range(2, poly_order + 1):
        table[:, degree] = (
            (2 * degree - 1) * points * table[:, degree - 1] - (degree - 1) * table[:, degree - 2]
        ) / degree
    return table


def lobatto_derivative(poly_order):
    node_count = poly_order + 1
    points = np.cos(np.pi * np.arange(node_count) / poly_order)
    for newton_step in range(100):
        table = legendre_table(points, poly_order)
        points = points - (points * table[:, poly_order] - table[:, poly_order - 1]) / (
            node_count * table[:, poly_order]
        )
    points = np.sort(points)
    top_values = legendre_table(points, poly_order)[:, poly_order]
    identity = np.eye(node_count)
    differ = points[:, None] - points[None, :] + identity
    matrix = top_values[:, None] / (top_values[None, :] * differ)
    matrix = matrix * (1.0 - identity)
    matrix[0, 0] = -poly_order * node_count / 4.0
    matrix[poly_order, poly_order] = poly_order * node_count / 4.0
    return matrix


def fourier_tables():
    positions = np.arange(PLANES)
    phases = ((positions // 2)[:, None] * positions[None, :] % PLANES) * (2.0 * np.pi / PLANES)
    cosine, sine = np.cos(phases), np.sin(phases)
    even = (positions % 2 == 0)[:, None]
    nyquist = (positions == 1)[:, None]
    alternate = (1.0 - 2.0 * (positions % 2))[None, :]
    forward = np.where(nyquist, alternate, np.where(even, cosine, -sine)) / PLANES
    backward = np.where(nyquist, alternate, np.where(even, 2.0 * cosine, -2.0 * sine))
    backward = np.where((positions == 0)[:, None], 1.0, backward)
    return forward.astype(np.float32), backward.T.astype(np.float32)


DERIVATIVE = lobatto_derivative(ORDER).astype(np.float32)
CYCLE_NODES = (
    [i * SIDE for i in range(SIDE)]
    + [i * SIDE + ORDER for i in range(SIDE)]
    + [j for j in range(1, ORDER)]
    + [ORDER * SIDE + j for j in range(1, ORDER)]
)
INNER_NODES = [i * SIDE + j for i in range(1, ORDER) for j in range(1, ORDER)]


def diagonal_tables():
    squared = (DERIVATIVE * DERIVATIVE).astype(np.float64)
    first = np.kron(squared.T, np.eye(SIDE))
    second = np.kron(np.eye(SIDE), squared.T)
    corner = np.diagonal(DERIVATIVE)
    cross = 2.0 * np.outer(corner, corner).reshape(NODES, 1)
    cross = np.broadcast_to(cross, (NODES, LANES))
    return np.concatenate([first, second], axis=1).astype(np.float32), cross.astype(np.float32)


def helmholtz_shift(rows_global):
    wavenumber = (rows_global // 2).astype(F32)
    spanwise = wavenumber * (2.0 * math.pi / (PLANES * SPACING))
    spanwise = jnp.where(rows_global == 1, math.pi / SPACING, spanwise)
    return spanwise * spanwise


def row_block(index):
    return slice(index * ROWS, (index + 1) * ROWS)


def lane_block(index):
    return slice(index * LANES, (index + 1) * LANES)


def pieces(value):
    top = value.astype(BF16).astype(F32)
    return top, value - top


def one_hot_columns(low_columns):
    lanes = lax.broadcasted_iota(jnp.int32, (low_columns.shape[0], LOW), 1)
    return jnp.where(low_columns == lanes, 1.0, 0.0).astype(BF16)


def one_hot_rows(low_rows):
    sublanes = lax.broadcasted_iota(jnp.int32, (LOW, low_rows.shape[1]), 0)
    return jnp.where(low_rows == sublanes, 1.0, 0.0).astype(BF16)


def masked_store(value, high_row, left_ref, column):
    top, rest = pieces(value)
    for high in range(HIGH):
        here = high_row == high
        left_ref[row_block(high), lane_block(column)] = jnp.where(here, top, 0.0).astype(BF16)
        left_ref[row_block(HIGH + high), lane_block(column)] = jnp.where(here, rest, 0.0).astype(BF16)


def scatter_sum(left, right):
    both = jnp.dot(left, right, preferred_element_type=F32)
    return both[: HIGH * ROWS] + both[HIGH * ROWS :]


def scatter_cycle(load, edge, edge_rows, left_ref, right_ref):
    low = jnp.bitwise_and(edge, LOW - 1)
    high_rows = jnp.right_shift(edge_rows, 8)
    for slot in range(CYCLE):
        right_ref[lane_block(slot), :] = one_hot_columns(low[:, slot : slot + 1])
        masked_store(load(slot), high_rows[slot : slot + 1, :], left_ref, slot)
    return scatter_sum(left_ref[...], right_ref[...])


def scatter_slots(load, shared, shared_rows, left_ref, right_ref):
    low = jnp.bitwise_and(shared, LOW - 1)
    high_rows = jnp.right_shift(shared_rows, 8)
    for tile in range(SLOT_TILES):
        right_ref[lane_block(tile), :] = one_hot_columns(low[:, tile : tile + 1])
        masked_store(load(tile), high_rows[tile : tile + 1, :], left_ref, tile)
    return scatter_sum(left_ref[:, :SLOTS], right_ref[:SLOTS, :])


def stack_pieces(skeleton):
    top, rest = pieces(skeleton)
    return jnp.concatenate([top.astype(BF16), rest.astype(BF16)], axis=0)


def gather_tile(stacked, rows):
    low = jnp.bitwise_and(rows, LOW - 1)
    high = jnp.right_shift(rows, 8)
    found = jnp.dot(stacked, one_hot_rows(low), preferred_element_type=F32)
    total = None
    for index in range(HIGH):
        part = found[row_block(index), :] + found[row_block(HIGH + index), :]
        part = jnp.where(high == index, part, 0.0)
        total = part if total is None else total + part
    return total


def gather_cycle(skeleton, edge_rows, store):
    stacked = stack_pieces(skeleton)
    for pair in range(CYCLE // 2):
        rows = jnp.concatenate(
            [edge_rows[2 * pair : 2 * pair + 1, :], edge_rows[2 * pair + 1 : 2 * pair + 2, :]], axis=1
        )
        total = gather_tile(stacked, rows)
        store(2 * pair, total[:, :LANES])
        store(2 * pair + 1, total[:, LANES:])


def gather_slots(skeleton, shared_rows):
    stacked = stack_pieces(skeleton)
    return [gather_tile(stacked, shared_rows[tile : tile + 1, :]) for tile in range(SLOT_TILES)]


def read_skeleton(packed_ref):
    return jnp.concatenate(
        [
            jnp.concatenate([packed_ref[INNER + 2 * high], packed_ref[INNER + 2 * high + 1]], axis=1)
            for high in range(HIGH)
        ],
        axis=0,
    )


def write_skeleton(packed_ref, skeleton):
    for high in range(HIGH):
        packed_ref[INNER + 2 * high] = skeleton[row_block(high), :LANES]
        packed_ref[INNER + 2 * high + 1] = skeleton[row_block(high), LANES:]


def clear_tail(packed_ref):
    for index in range(INNER + TILES, PACKED):
        packed_ref[index] = jnp.zeros((ROWS, LANES), F32)


def fold(value):
    return value[:, :LANES] + value[:, LANES:]


def per_tile(penalty_ref):
    return jnp.concatenate(
        [jnp.broadcast_to(penalty_ref[high : high + 1, :], (ROWS, LOW)) for high in range(HIGH)], axis=0
    )


def skeleton_sum(product):
    total = None
    for high in range(HIGH):
        part = fold(product[row_block(high), :])
        total = part if total is None else total + part
    return total


def pack_kernel(forcing_ref, edge_ref, out_ref, left_ref, right_ref):
    edge = edge_ref[...]
    edge_rows = edge.T
    for index, node in enumerate(INNER_NODES):
        out_ref[index] = forcing_ref[:, node, :]
    skeleton = scatter_cycle(
        lambda slot: forcing_ref[:, CYCLE_NODES[slot], :], edge, edge_rows, left_ref, right_ref
    )
    write_skeleton(out_ref, skeleton)
    clear_tail(out_ref)


def transform_kernel(matrix_ref, in_ref, out_ref):
    matrix = matrix_ref[...]
    for index in range(BLOCK):
        block = in_ref[:, index].reshape(PLANES, LANES)
        mixed = jnp.dot(matrix, block, precision=HIGHEST, preferred_element_type=F32)
        out_ref[:, index] = mixed.reshape(MODES, ROWS, LANES)


def diagonal_kernel(
    metric_ref, table_ref, cross_ref, edge_ref, penalty_ref, shared_ref, inner_ref, skeleton_ref, slots_ref,
    cells_ref, left_ref, right_ref,
):
    both = jnp.concatenate([metric_ref[0], metric_ref[1]], axis=0)
    terms = jnp.dot(table_ref[...], both, precision=HIGHEST, preferred_element_type=F32)
    cells_ref[0] = terms + cross_ref[...] * metric_ref[2]
    cells_ref[1] = metric_ref[3]
    for index, node in enumerate(INNER_NODES):
        inner_ref[0, index : index + 1, :] = cells_ref[0, node : node + 1, :]
        inner_ref[1, index : index + 1, :] = cells_ref[1, node : node + 1, :]
    edge = edge_ref[...]
    edge_rows = edge.T
    sublanes = lax.broadcasted_iota(jnp.int32, (ROWS, LANES), 0)

    def load(slot):
        node = CYCLE_NODES[slot]
        laplace = jnp.broadcast_to(cells_ref[0, node : node + 1, :], (ROWS, LANES))
        mass = jnp.broadcast_to(cells_ref[1, node : node + 1, :], (ROWS, LANES))
        return jnp.where(sublanes == 0, laplace, jnp.where(sublanes == 1, mass, 0.0))

    skeleton = scatter_cycle(load, edge, edge_rows, left_ref, right_ref)
    wide = lax.broadcasted_iota(jnp.int32, (HIGH * ROWS, LOW), 0)
    skeleton = skeleton + jnp.where(jnp.bitwise_and(wide, ROWS - 1) == 0, per_tile(penalty_ref), 0.0)
    skeleton_ref[...] = skeleton
    for tile, value in enumerate(gather_slots(skeleton, shared_ref[...])):
        slots_ref[tile] = value[:8]


def slots_kernel(packed_ref, shared_ref, extra_ref, out_ref):
    for tile, value in enumerate(gather_slots(read_skeleton(packed_ref), shared_ref[...])):
        out_ref[tile, :ROWS, :] = value
        out_ref[tile, ROWS:, :] = extra_ref[tile]


def select_arrived(masks, tile, arrived):
    chosen = arrived[0]
    row = masks[tile : tile + 1, :]
    for level in range(1, len(arrived)):
        moving = jnp.bitwise_and(jnp.right_shift(row, level), 1) == 1
        chosen = jnp.where(moving, arrived[level], chosen)
    return chosen


def derivative_line(values, transposed):
    results = []
    for out in range(SIDE):
        total = None
        for k in range(SIDE):
            weight = float(DERIVATIVE[k, out] if transposed else DERIVATIVE[out, k])
            if weight == 0.0:
                continue
            part = weight * values[k]
            total = part if total is None else total + part
        results.append(total)
    return results


def gradients(cells_ref, first_ref, metric_ref, rows, visit):
    for j in range(SIDE):
        line = derivative_line([cells_ref[k * SIDE + j, rows, :] for k in range(SIDE)], False)
        for i in range(SIDE):
            first_ref[i * SIDE + j] = line[i]
    for i in range(SIDE):
        line = derivative_line([cells_ref[i * SIDE + k, rows, :] for k in range(SIDE)], False)
        seconds = []
        for j in range(SIDE):
            node = i * SIDE + j
            m0, m1, m2 = [metric_ref[c, node : node + 1, :] for c in range(3)]
            g1, g2 = first_ref[node], line[j]
            p1 = m0 * g1 + m2 * g2
            p2 = m2 * g1 + m1 * g2
            visit(node, g1, g2, p1, p2)
            seconds.append(p2)
        yield i, seconds


def apply_operator(cells_ref, result_ref, first_ref, energy_ref, metric_ref, shift_ref):
    @pl.loop(0, 2)
    def half(part):
        rows = pl.ds(pl.multiple_of(part * 8, 8), 8)
        shift = shift_ref[rows, :]

        def visit(node, g1, g2, p1, p2):
            first_ref[node] = p1

        for i, seconds in gradients(cells_ref, first_ref, metric_ref, rows, visit):
            line = derivative_line(seconds, True)
            for j in range(SIDE):
                node = i * SIDE + j
                mass = shift * metric_ref[3, node : node + 1, :]
                result_ref[node, rows, :] = line[j] + mass * cells_ref[node, rows, :]
        energy = jnp.zeros((8, LANES), F32)
        for j in range(SIDE):
            line = derivative_line([first_ref[k * SIDE + j] for k in range(SIDE)], True)
            for i in range(SIDE):
                node = i * SIDE + j
                value = result_ref[node, rows, :] + line[i]
                result_ref[node, rows, :] = value
                energy = energy + value * cells_ref[node, rows, :]
        energy_ref[rows, :] = energy


def apply_energy(cells_ref, first_ref, energy_ref, metric_ref, shift_ref):
    @pl.loop(0, 2)
    def half(part):
        rows = pl.ds(pl.multiple_of(part * 8, 8), 8)
        shift = shift_ref[rows, :]
        sums = [jnp.zeros((8, LANES), F32)]

        def visit(node, g1, g2, p1, p2):
            value = cells_ref[node, rows, :]
            mass = shift * metric_ref[3, node : node + 1, :]
            sums[0] = sums[0] + (g1 * p1 + g2 * p2 + mass * value * value)

        for i, seconds in gradients(cells_ref, first_ref, metric_ref, rows, visit):
            pass
        energy_ref[rows, :] = sums[0]


def first_kernel(
    packed_ref, a0, a1, a2, a3, a4, masks_ref, shared_ref, shared_columns_ref, edge_ref, metric_ref, inner_ref,
    diagonal_ref, penalty_ref, shift_ref, search_ref, applied_ref, inverse_ref, slots_ref, sums_ref,
    left_ref, right_ref, cells_ref, result_ref, first_ref, energy_ref,
):
    arrived_refs = [a0, a1, a2, a3, a4]
    masks = masks_ref[...]
    shared_rows = shared_ref[...]
    shared_columns = shared_columns_ref[...]
    shift = shift_ref[...]

    def load_right(tile):
        return select_arrived(masks, tile, [ref[tile, :ROWS, :] for ref in arrived_refs])

    def load_extra(tile):
        chosen = select_arrived(masks, tile, [ref[tile, ROWS:, :] for ref in arrived_refs])
        return jnp.concatenate([chosen, jnp.zeros_like(chosen)], axis=0)

    local = read_skeleton(packed_ref)
    right_side = local + scatter_slots(load_right, shared_columns, shared_rows, left_ref, right_ref)
    diagonal = diagonal_ref[...] + scatter_slots(
        load_extra, shared_columns, shared_rows, left_ref, right_ref
    )
    parts = []
    for high in range(HIGH):
        block = diagonal[row_block(high), :]
        wide_shift = jnp.concatenate([shift, shift], axis=1)
        parts.append(block[0:1, :] + wide_shift * block[1:2, :])
    inverse = 1.0 / jnp.concatenate(parts, axis=0)
    search = right_side * inverse
    write_skeleton(search_ref, search)
    write_skeleton(inverse_ref, inverse)
    clear_tail(search_ref)
    start = skeleton_sum(local * search)
    for index, node in enumerate(INNER_NODES):
        value = packed_ref[index]
        inverted = 1.0 / (inner_ref[0, index : index + 1, :] + shift * inner_ref[1, index : index + 1, :])
        scaled = value * inverted
        inverse_ref[index] = inverted
        search_ref[index] = scaled
        cells_ref[node] = scaled
        start = start + value * scaled

    def store(slot, value):
        cells_ref[CYCLE_NODES[slot]] = value

    edge = edge_ref[...]
    edge_rows = edge.T
    gather_cycle(search, edge_rows, store)
    apply_operator(cells_ref, result_ref, first_ref, energy_ref, metric_ref, shift_ref)
    for index, node in enumerate(INNER_NODES):
        applied_ref[index] = result_ref[node]
    weighted = per_tile(penalty_ref) * search
    applied = weighted + scatter_cycle(
        lambda slot: result_ref[CYCLE_NODES[slot]], edge, edge_rows, left_ref, right_ref
    )
    write_skeleton(applied_ref, applied)
    for tile, value in enumerate(gather_slots(applied, shared_rows)):
        slots_ref[tile] = value
    sums_ref[0] = energy_ref[...] + skeleton_sum(weighted * search)
    sums_ref[1] = start


def second_kernel(
    packed_ref, search_ref, applied_ref, inverse_ref, sums_ref, a0, a1, a2, a3, a4, masks_ref, shared_ref,
    shared_columns_ref, edge_ref, metric_ref, penalty_ref, shift_ref, change_ref, message_ref,
    left_ref, right_ref, cells_ref, first_ref, energy_ref,
):
    arrived_refs = [a0, a1, a2, a3, a4]
    masks = masks_ref[...]

    def load(tile):
        return select_arrived(masks, tile, [ref[tile] for ref in arrived_refs])

    local = read_skeleton(applied_ref)
    search = read_skeleton(search_ref)
    full = local + scatter_slots(load, shared_columns_ref[...], shared_ref[...], left_ref, right_ref)
    change = full * read_skeleton(inverse_ref) - search
    write_skeleton(change_ref, change)
    clear_tail(change_ref)
    crossed = skeleton_sum(local * change)
    sourced = skeleton_sum(read_skeleton(packed_ref) * change)
    for index, node in enumerate(INNER_NODES):
        value = applied_ref[index]
        moved = value * inverse_ref[index] - search_ref[index]
        change_ref[index] = moved
        cells_ref[node] = moved
        crossed = crossed + value * moved
        sourced = sourced + packed_ref[index] * moved

    def store(slot, value):
        cells_ref[CYCLE_NODES[slot]] = value

    gather_cycle(change, edge_ref[...].T, store)
    apply_energy(cells_ref, first_ref, energy_ref, metric_ref, shift_ref)
    energy = energy_ref[...] + skeleton_sum(per_tile(penalty_ref) * change * change)
    sublanes = lax.broadcasted_iota(jnp.int32, (ROWS, LANES), 0)
    lanes = lax.broadcasted_iota(jnp.int32, (ROWS, LANES), 1)
    spread = jnp.zeros((ROWS, LANES), F32)
    for index, value in enumerate([sums_ref[0], crossed, energy, sums_ref[1], sourced]):
        column = jnp.sum(value, axis=1, keepdims=True)
        spread = jnp.where(lanes == sublanes + index * ROWS, column, spread)
    message = jnp.sum(spread, axis=0, keepdims=True)
    message_ref[...] = jnp.broadcast_to(message, message_ref.shape)


def combine_kernel(matrix_ref, scalars_ref, search_ref, change_ref, out_ref, block_ref):
    sublanes = lax.broadcasted_iota(jnp.int32, (ROWS, LANES), 0)
    lanes = lax.broadcasted_iota(jnp.int32, (ROWS, LANES), 1)
    for mode in range(MODES):
        total = jnp.sum(scalars_ref[mode], axis=0, keepdims=True)
        g00, g01, g11, h0, h1 = [
            jnp.sum(jnp.where(lanes == sublanes + index * ROWS, total, 0.0), axis=1, keepdims=True)
            for index in range(SCALARS)
        ]
        ratio = g01 / g00
        pivot = g11 - ratio * g01
        second = jnp.where(pivot > 0.0, (h1 - ratio * h0) / pivot, 0.0)
        first = h0 / g00 - ratio * second
        for index in range(BLOCK):
            block_ref[index, row_block(mode), :] = (
                first * search_ref[mode, index] + second * change_ref[mode, index]
            )
    matrix = matrix_ref[...]
    for index in range(BLOCK):
        mixed = jnp.dot(matrix, block_ref[index], precision=HIGHEST, preferred_element_type=F32)
        out_ref[:, index] = mixed.reshape(MODES, ROWS, LANES)


def unpack_kernel(packed_ref, edge_ref, out_ref):
    for index, node in enumerate(INNER_NODES):
        out_ref[:, node, :] = packed_ref[index]

    def store(slot, value):
        out_ref[:, CYCLE_NODES[slot], :] = value

    gather_cycle(read_skeleton(packed_ref), edge_ref[...].T, store)


def call(kernel, out_shapes, scratch, *operands):
    return pl.pallas_call(
        kernel,
        out_shape=out_shapes,
        scratch_shapes=scratch,
        compiler_params=pltpu.CompilerParams(vmem_limit_bytes=VMEM_LIMIT),
    )(*operands)


def shape(*dims):
    return jax.ShapeDtypeStruct(dims, F32)


def swap_blocks(packed):
    blocks = packed.reshape(MODES, BLOCK, ROWS, LANES)
    return lax.all_to_all(blocks, "mode", split_axis=0, concat_axis=0, tiled=True)


def exchange(slots):
    count = lax.axis_size("elem")
    return [
        lax.ppermute(slots, "elem", [(i, i ^ 1 << level) for i in range(count)])
        for level in range(count.bit_length() - 1)
    ]


def body(forcing, metric, edge_map, shared_rows, partner_masks, penalty):
    forward, backward = [jnp.asarray(table) for table in fourier_tables()]
    table, cross = [jnp.asarray(part) for part in diagonal_tables()]
    rows_global = lax.axis_index("mode") * ROWS + jnp.arange(ROWS, dtype=jnp.int32)
    shift = jnp.broadcast_to(helmholtz_shift(rows_global)[:, None], (ROWS, LANES))
    shared = shared_rows.reshape(SLOT_TILES, LANES)
    shared_columns = shared.T
    masks = partner_masks.reshape(SLOT_TILES, LANES)
    penalties = jnp.pad(penalty, (0, HIGH * LOW - SKEL), constant_values=1.0).reshape(HIGH, LOW)
    left = pltpu.VMEM((2 * HIGH * ROWS, CYCLE * LANES), BF16)
    right = pltpu.VMEM((CYCLE * LANES, LOW), BF16)
    left_slots = pltpu.VMEM((2 * HIGH * ROWS, SLOTS), BF16)
    right_slots = pltpu.VMEM((SLOTS, LOW), BF16)
    cells = pltpu.VMEM((NODES, ROWS, LANES), F32)
    first = pltpu.VMEM((NODES, 8, LANES), F32)
    energy = pltpu.VMEM((ROWS, LANES), F32)

    packed = call(pack_kernel, shape(PACKED, ROWS, LANES), [left, right], forcing, edge_map)
    gathered = swap_blocks(packed)
    inner, diagonal, extra = call(
        diagonal_kernel,
        [shape(2, INNER, LANES), shape(HIGH * ROWS, LOW), shape(SLOT_TILES, 8, LANES)],
        [pltpu.VMEM((2, NODES, LANES), F32), left, right],
        metric, table, cross, edge_map, penalties, shared,
    )
    mixed = call(transform_kernel, shape(MODES, BLOCK, ROWS, LANES), [], forward, gathered)
    source = swap_blocks(mixed).reshape(PACKED, ROWS, LANES)
    slots = call(slots_kernel, shape(SLOT_TILES, ROWS + 8, LANES), [], source, shared, extra)
    search, applied, inverse, slots, sums = call(
        first_kernel,
        [
            shape(PACKED, ROWS, LANES), shape(INNER + TILES, ROWS, LANES), shape(INNER + TILES, ROWS, LANES),
            shape(SLOT_TILES, ROWS, LANES), shape(2, ROWS, LANES),
        ],
        [left, right, cells, cells, first, energy],
        source, *exchange(slots), masks, shared, shared_columns, edge_map, metric, inner, diagonal, penalties, shift,
    )
    search_blocks = swap_blocks(search)
    change, message = call(
        second_kernel,
        [shape(PACKED, ROWS, LANES), shape(MODES * ELEMS_AXIS, LANES)],
        [left_slots, right_slots, cells, first, energy],
        source, search, applied, inverse, sums, *exchange(slots), masks, shared, shared_columns, edge_map, metric,
        penalties, shift,
    )
    change_blocks = swap_blocks(change)
    scalars = lax.all_to_all(message, ("mode", "elem"), split_axis=0, concat_axis=0, tiled=True)
    mixed = call(
        combine_kernel, shape(MODES, BLOCK, ROWS, LANES), [pltpu.VMEM((BLOCK, PLANES, LANES), F32)],
        backward, scalars.reshape(MODES, ELEMS_AXIS, LANES), search_blocks, change_blocks,
    )
    result = swap_blocks(mixed).reshape(PACKED, ROWS, LANES)
    return call(unpack_kernel, shape(ROWS, NODES, LANES), [], result, edge_map)


def solution(mesh):
    placed = (
        P("mode", None, "elem"),
        P(None, None, "elem"),
        P("elem", None),
        P("elem"),
        P("elem"),
        P("elem"),
    )
    return jax.shard_map(
        body, mesh=mesh, in_specs=placed, out_specs=P("mode", None, "elem"), check_vma=False
    )
```

```python
import math

import jax
import jax.numpy as jnp
import numpy as np
from jax import lax
from jax.experimental import pallas as pl
from jax.experimental.pallas import tpu as pltpu
from jax.sharding import PartitionSpec as P

ORDER = 8
SIDE = ORDER + 1
NODES = SIDE * SIDE
CYCLE = 32
INNER = (ORDER - 1) ** 2
ROWS = 16
LANES = 128
PLANES = 128
MODES = 8
ELEMS_AXIS = 32
SKEL = 2113
LOW = 256
HIGH = 9
TILES = 2 * HIGH
SLOTS = 384
SLOT_TILES = SLOTS // LANES
BLOCK = 9
SHARE = BLOCK + SLOT_TILES
GROUP = 7
TAIL = 4
SCALARS = 5
SPACING = 0.25
F32 = jnp.float32
BF16 = jnp.bfloat16
HIGHEST = lax.Precision.HIGHEST
VMEM_LIMIT = 32 * 1024 * 1024


def legendre_table(points, poly_order):
    table = np.zeros((points.shape[0], poly_order + 1))
    table[:, 0] = 1.0
    table[:, 1] = points
    for degree in range(2, poly_order + 1):
        table[:, degree] = (
            (2 * degree - 1) * points * table[:, degree - 1] - (degree - 1) * table[:, degree - 2]
        ) / degree
    return table


def lobatto_derivative(poly_order):
    node_count = poly_order + 1
    points = np.cos(np.pi * np.arange(node_count) / poly_order)
    for newton_step in range(100):
        table = legendre_table(points, poly_order)
        points = points - (points * table[:, poly_order] - table[:, poly_order - 1]) / (
            node_count * table[:, poly_order]
        )
    points = np.sort(points)
    top_values = legendre_table(points, poly_order)[:, poly_order]
    identity = np.eye(node_count)
    differ = points[:, None] - points[None, :] + identity
    matrix = top_values[:, None] / (top_values[None, :] * differ)
    matrix = matrix * (1.0 - identity)
    matrix[0, 0] = -poly_order * node_count / 4.0
    matrix[poly_order, poly_order] = poly_order * node_count / 4.0
    return matrix


def fourier_tables():
    positions = np.arange(PLANES)
    phases = ((positions // 2)[:, None] * positions[None, :] % PLANES) * (2.0 * np.pi / PLANES)
    cosine, sine = np.cos(phases), np.sin(phases)
    even = (positions % 2 == 0)[:, None]
    nyquist = (positions == 1)[:, None]
    alternate = (1.0 - 2.0 * (positions % 2))[None, :]
    forward = np.where(nyquist, alternate, np.where(even, cosine, -sine)) / PLANES
    backward = np.where(nyquist, alternate, np.where(even, 2.0 * cosine, -2.0 * sine))
    backward = np.where((positions == 0)[:, None], 1.0, backward)
    return forward.astype(np.float32), backward.T.astype(np.float32)


DERIVATIVE = lobatto_derivative(ORDER).astype(np.float32)
CYCLE_NODES = (
    [i * SIDE for i in range(SIDE)]
    + [i * SIDE + ORDER for i in range(SIDE)]
    + [j for j in range(1, ORDER)]
    + [ORDER * SIDE + j for j in range(1, ORDER)]
)
INNER_NODES = [i * SIDE + j for i in range(1, ORDER) for j in range(1, ORDER)]


def diagonal_tables():
    squared = (DERIVATIVE * DERIVATIVE).astype(np.float64)
    first = np.kron(squared.T, np.eye(SIDE))
    second = np.kron(np.eye(SIDE), squared.T)
    corner = np.diagonal(DERIVATIVE)
    cross = 2.0 * np.outer(corner, corner).reshape(NODES, 1)
    cross = np.broadcast_to(cross, (NODES, LANES))
    return np.concatenate([first, second], axis=1).astype(np.float32), cross.astype(np.float32)


def helmholtz_shift(rows_global):
    wavenumber = (rows_global // 2).astype(F32)
    spanwise = wavenumber * (2.0 * math.pi / (PLANES * SPACING))
    spanwise = jnp.where(rows_global == 1, math.pi / SPACING, spanwise)
    return spanwise * spanwise


def row_block(index):
    return slice(index * ROWS, (index + 1) * ROWS)


def lane_block(index):
    return slice(index * LANES, (index + 1) * LANES)


def pieces(value):
    top = value.astype(BF16).astype(F32)
    return top, value - top


def one_hot_columns(low_columns):
    lanes = lax.broadcasted_iota(jnp.int32, (low_columns.shape[0], LOW), 1)
    return jnp.where(low_columns == lanes, 1.0, 0.0).astype(BF16)


def one_hot_rows(low_rows):
    sublanes = lax.broadcasted_iota(jnp.int32, (LOW, low_rows.shape[1]), 0)
    return jnp.where(low_rows == sublanes, 1.0, 0.0).astype(BF16)


def masked_store(value, high_row, left_ref, column):
    top, rest = pieces(value)
    for high in range(HIGH):
        here = high_row == high
        left_ref[row_block(high), lane_block(column)] = jnp.where(here, top, 0.0).astype(BF16)
        left_ref[row_block(HIGH + high), lane_block(column)] = jnp.where(here, rest, 0.0).astype(BF16)


def scatter_sum(left, right):
    both = jnp.dot(left, right, preferred_element_type=F32)
    return both[: HIGH * ROWS] + both[HIGH * ROWS :]


def scatter_cycle(load, edge_rows, left_ref, right_ref):
    low = jnp.bitwise_and(edge_rows.T, LOW - 1)
    high_rows = jnp.right_shift(edge_rows, 8)
    for slot in range(CYCLE):
        right_ref[lane_block(slot), :] = one_hot_columns(low[:, slot : slot + 1])
        masked_store(load(slot), high_rows[slot : slot + 1, :], left_ref, slot)
    return scatter_sum(left_ref[...], right_ref[...])


def scatter_slots(load, shared_rows, left_ref, right):
    high_rows = jnp.right_shift(shared_rows, 8)
    for tile in range(SLOT_TILES):
        masked_store(load(tile), high_rows[tile : tile + 1, :], left_ref, tile)
    return scatter_sum(left_ref[:, :SLOTS], right)


def stack_pieces(skeleton):
    top, rest = pieces(skeleton)
    return jnp.concatenate([top.astype(BF16), rest.astype(BF16)], axis=0)


def gather_tile(stacked, rows):
    low = jnp.bitwise_and(rows, LOW - 1)
    high = jnp.right_shift(rows, 8)
    found = jnp.dot(stacked, one_hot_rows(low), preferred_element_type=F32)
    total = None
    for index in range(HIGH):
        part = found[row_block(index), :] + found[row_block(HIGH + index), :]
        part = jnp.where(high == index, part, 0.0)
        total = part if total is None else total + part
    return total


def gather_cycle(skeleton, edge_rows, store):
    stacked = stack_pieces(skeleton)
    for pair in range(CYCLE // 2):
        rows = jnp.concatenate(
            [edge_rows[2 * pair : 2 * pair + 1, :], edge_rows[2 * pair + 1 : 2 * pair + 2, :]], axis=1
        )
        total = gather_tile(stacked, rows)
        store(2 * pair, total[:, :LANES])
        store(2 * pair + 1, total[:, LANES:])


def gather_slots(skeleton, shared_rows):
    stacked = stack_pieces(skeleton)
    return [gather_tile(stacked, shared_rows[tile : tile + 1, :]) for tile in range(SLOT_TILES)]


def sent_place(index):
    return index // BLOCK, index % BLOCK


def tail_place(index):
    return min(index // 2, MODES - 1), index - 2 * min(index // 2, MODES - 1)


def result_place(index):
    block, row = tail_place(index)
    return block, row + GROUP if row < 2 else row - 2


def read_skeleton(load):
    return jnp.concatenate(
        [jnp.concatenate([load(2 * high), load(2 * high + 1)], axis=1) for high in range(HIGH)], axis=0
    )


def write_skeleton(skeleton, store):
    for high in range(HIGH):
        store(2 * high, skeleton[row_block(high), :LANES])
        store(2 * high + 1, skeleton[row_block(high), LANES:])


def write_place(ref, place):
    def store(index, value):
        block, row = place(index)
        ref[block, row] = value

    return store


def fold(value):
    return value[:, :LANES] + value[:, LANES:]


def per_tile(penalty_ref):
    return jnp.concatenate(
        [jnp.broadcast_to(penalty_ref[high : high + 1, :], (ROWS, LOW)) for high in range(HIGH)], axis=0
    )


def skeleton_sum(product):
    total = None
    for high in range(HIGH):
        part = fold(product[row_block(high), :])
        total = part if total is None else total + part
    return total


def select_arrived(masks, tile, arrived):
    chosen = arrived[0]
    row = masks[tile : tile + 1, :]
    for level in range(1, len(arrived)):
        moving = jnp.bitwise_and(jnp.right_shift(row, level), 1) == 1
        chosen = jnp.where(moving, arrived[level], chosen)
    return chosen


def derivative_line(values, transposed):
    results = []
    for out in range(SIDE):
        total = None
        for k in range(SIDE):
            weight = float(DERIVATIVE[k, out] if transposed else DERIVATIVE[out, k])
            if weight == 0.0:
                continue
            part = weight * values[k]
            total = part if total is None else total + part
        results.append(total)
    return results


def gradients(cells_ref, first_ref, metric_ref, rows, visit):
    for j in range(SIDE):
        line = derivative_line([cells_ref[k * SIDE + j, rows, :] for k in range(SIDE)], False)
        for i in range(SIDE):
            first_ref[i * SIDE + j] = line[i]
    for i in range(SIDE):
        line = derivative_line([cells_ref[i * SIDE + k, rows, :] for k in range(SIDE)], False)
        seconds = []
        for j in range(SIDE):
            node = i * SIDE + j
            m0, m1, m2 = [metric_ref[c, node : node + 1, :] for c in range(3)]
            g1, g2 = first_ref[node], line[j]
            p1 = m0 * g1 + m2 * g2
            p2 = m2 * g1 + m1 * g2
            visit(node, g1, g2, p1, p2)
            seconds.append(p2)
        yield i, seconds


def apply_operator(cells_ref, result_ref, first_ref, energy_ref, metric_ref, shift_ref):
    @pl.loop(0, 2)
    def half(part):
        rows = pl.ds(pl.multiple_of(part * 8, 8), 8)
        shift = shift_ref[rows, :]

        def visit(node, g1, g2, p1, p2):
            first_ref[node] = p1

        for i, seconds in gradients(cells_ref, first_ref, metric_ref, rows, visit):
            line = derivative_line(seconds, True)
            for j in range(SIDE):
                node = i * SIDE + j
                mass = shift * metric_ref[3, node : node + 1, :]
                result_ref[node, rows, :] = line[j] + mass * cells_ref[node, rows, :]
        energy = jnp.zeros((8, LANES), F32)
        for j in range(SIDE):
            line = derivative_line([first_ref[k * SIDE + j] for k in range(SIDE)], True)
            for i in range(SIDE):
                node = i * SIDE + j
                value = result_ref[node, rows, :] + line[i]
                result_ref[node, rows, :] = value
                energy = energy + value * cells_ref[node, rows, :]
        energy_ref[rows, :] = energy


def apply_energy(cells_ref, first_ref, energy_ref, metric_ref, shift_ref):
    @pl.loop(0, 2)
    def half(part):
        rows = pl.ds(pl.multiple_of(part * 8, 8), 8)
        shift = shift_ref[rows, :]
        sums = [jnp.zeros((8, LANES), F32)]

        def visit(node, g1, g2, p1, p2):
            value = cells_ref[node, rows, :]
            mass = shift * metric_ref[3, node : node + 1, :]
            sums[0] = sums[0] + (g1 * p1 + g2 * p2 + mass * value * value)

        for i, seconds in gradients(cells_ref, first_ref, metric_ref, rows, visit):
            pass
        energy_ref[rows, :] = sums[0]


def pack_kernel(forcing_ref, edge_ref, shared_ref, out_ref, slots_ref, left_ref, right_ref):
    store = write_place(out_ref, sent_place)
    for index, node in enumerate(INNER_NODES):
        store(index, forcing_ref[node])
    for index in range(INNER + TILES, MODES * BLOCK):
        store(index, jnp.zeros((ROWS, LANES), F32))
    skeleton = scatter_cycle(lambda slot: forcing_ref[CYCLE_NODES[slot]], edge_ref[...], left_ref, right_ref)
    write_skeleton(skeleton, lambda index, value: store(INNER + index, value))
    for tile, value in enumerate(gather_slots(skeleton, shared_ref[...])):
        slots_ref[tile] = value


def diagonal_kernel(
    metric_ref, table_ref, cross_ref, edge_ref, penalty_ref, shared_ref, columns_ref, slots_ref,
    inner_ref, skeleton_ref, message_ref, right_slots_ref, cells_ref, left_ref, right_ref,
):
    both = jnp.concatenate([metric_ref[0], metric_ref[1]], axis=0)
    terms = jnp.dot(table_ref[...], both, precision=HIGHEST, preferred_element_type=F32)
    cells_ref[0] = terms + cross_ref[...] * metric_ref[2]
    cells_ref[1] = metric_ref[3]
    for index, node in enumerate(INNER_NODES):
        inner_ref[0, index : index + 1, :] = cells_ref[0, node : node + 1, :]
        inner_ref[1, index : index + 1, :] = cells_ref[1, node : node + 1, :]
    sublanes = lax.broadcasted_iota(jnp.int32, (ROWS, LANES), 0)

    def load(slot):
        node = CYCLE_NODES[slot]
        laplace = jnp.broadcast_to(cells_ref[0, node : node + 1, :], (ROWS, LANES))
        mass = jnp.broadcast_to(cells_ref[1, node : node + 1, :], (ROWS, LANES))
        return jnp.where(sublanes == 0, laplace, jnp.where(sublanes == 1, mass, 0.0))

    skeleton = scatter_cycle(load, edge_ref[...], left_ref, right_ref)
    wide = lax.broadcasted_iota(jnp.int32, (HIGH * ROWS, LOW), 0)
    skeleton = skeleton + jnp.where(jnp.bitwise_and(wide, ROWS - 1) == 0, per_tile(penalty_ref), 0.0)
    skeleton_ref[...] = skeleton
    low = jnp.bitwise_and(columns_ref[...], LOW - 1)
    for tile, value in enumerate(gather_slots(skeleton, shared_ref[...])):
        message_ref[tile, :ROWS, :] = slots_ref[tile]
        message_ref[tile, ROWS:, :] = value[:8]
        right_slots_ref[lane_block(tile), :] = one_hot_columns(low[:, tile : tile + 1])


def transform_kernel(matrix_ref, share_ref, in_ref, a0, a1, a2, a3, a4, masks_ref, out_ref, extra_ref):
    matrix = matrix_ref[...]
    arrived_refs = [a0, a1, a2, a3, a4]
    masks = masks_ref[...]
    for index in range(BLOCK):
        block = in_ref[:, index].reshape(PLANES, LANES)
        mixed = jnp.dot(matrix, block, precision=HIGHEST, preferred_element_type=F32)
        out_ref[:, index] = mixed.reshape(MODES, ROWS, LANES)
    share = share_ref[...]
    for tile in range(SLOT_TILES):
        chosen = select_arrived(masks, tile, [ref[tile] for ref in arrived_refs])
        mixed = jnp.dot(share, chosen[:ROWS], precision=HIGHEST, preferred_element_type=F32)
        out_ref[:, BLOCK + tile] = mixed.reshape(MODES, ROWS, LANES)
        extra_ref[tile] = chosen[ROWS:]


def first_kernel(
    source_ref, extra_ref, shared_ref, right_slots_ref, edge_ref, metric_ref, inner_ref, diagonal_ref,
    penalty_ref, shift_ref, pairs_ref, kept_ref, slots_ref, sums_ref,
    left_ref, right_ref, cells_ref, result_ref, first_ref, energy_ref,
):
    shared_rows = shared_ref[...]
    right_slots = right_slots_ref[...]
    shift = shift_ref[...]
    edge_rows = edge_ref[...]

    def load_right(tile):
        total = source_ref[0, BLOCK + tile]
        for mode in range(1, MODES):
            total = total + source_ref[mode, BLOCK + tile]
        return total

    def load_extra(tile):
        return jnp.concatenate([extra_ref[tile], jnp.zeros((8, LANES), F32)], axis=0)

    def source(index):
        block, row = sent_place(index)
        return source_ref[block, row]

    local = read_skeleton(lambda index: source(INNER + index))
    right_side = local + scatter_slots(load_right, shared_rows, left_ref, right_slots)
    diagonal = diagonal_ref[...] + scatter_slots(load_extra, shared_rows, left_ref, right_slots)
    wide_shift = jnp.concatenate([shift, shift], axis=1)
    parts = []
    for high in range(HIGH):
        block = diagonal[row_block(high), :]
        parts.append(block[0:1, :] + wide_shift * block[1:2, :])
    inverse = 1.0 / jnp.concatenate(parts, axis=0)
    search = right_side * inverse
    kept_ref[0] = local
    kept_ref[1] = inverse
    kept_ref[2] = search
    start = skeleton_sum(local * search)
    for index, node in enumerate(INNER_NODES):
        value = source(index)
        inverted = 1.0 / (inner_ref[0, index : index + 1, :] + shift * inner_ref[1, index : index + 1, :])
        scaled = value * inverted
        pairs_ref[index // GROUP, index % GROUP] = scaled
        pairs_ref[index // GROUP, GROUP + index % GROUP] = inverted
        cells_ref[node] = scaled
        start = start + value * scaled

    def store(slot, value):
        cells_ref[CYCLE_NODES[slot]] = value

    gather_cycle(search, edge_rows, store)
    apply_operator(cells_ref, result_ref, first_ref, energy_ref, metric_ref, shift_ref)
    weighted = per_tile(penalty_ref) * search
    applied = weighted + scatter_cycle(
        lambda slot: result_ref[CYCLE_NODES[slot]], edge_rows, left_ref, right_ref
    )
    kept_ref[3] = applied
    for tile, value in enumerate(gather_slots(applied, shared_rows)):
        slots_ref[tile] = value
    crossed = jnp.zeros((ROWS, LANES), F32)
    sourced = jnp.zeros((ROWS, LANES), F32)
    for index, node in enumerate(INNER_NODES):
        value = result_ref[node]
        moved = value * pairs_ref[index // GROUP, GROUP + index % GROUP] - cells_ref[node]
        pairs_ref[index // GROUP, GROUP + index % GROUP] = moved
        crossed = crossed + value * moved
        sourced = sourced + source(index) * moved
    for row in range(2 * GROUP):
        pairs_ref[MODES - 1, row] = jnp.zeros((ROWS, LANES), F32)
    sums_ref[0] = energy_ref[...] + skeleton_sum(weighted * search)
    sums_ref[1] = crossed
    sums_ref[2] = start
    sums_ref[3] = sourced


def second_kernel(
    pairs_ref, kept_ref, sums_ref, a0, a1, a2, a3, a4, masks_ref, shared_ref, right_slots_ref, edge_ref,
    metric_ref, penalty_ref, shift_ref, change_ref, message_ref, left_ref, cells_ref, first_ref, energy_ref,
):
    arrived_refs = [a0, a1, a2, a3, a4]
    masks = masks_ref[...]

    def load(tile):
        return select_arrived(masks, tile, [ref[tile] for ref in arrived_refs])

    local, inverse, search, applied = [kept_ref[index] for index in range(4)]
    full = applied + scatter_slots(load, shared_ref[...], left_ref, right_slots_ref[...])
    change = full * inverse - search
    change_ref[...] = change
    crossed = sums_ref[1] + skeleton_sum(applied * change)
    sourced = sums_ref[3] + skeleton_sum(local * change)
    for index, node in enumerate(INNER_NODES):
        cells_ref[node] = pairs_ref[index // GROUP, GROUP + index % GROUP]

    def store(slot, value):
        cells_ref[CYCLE_NODES[slot]] = value

    gather_cycle(change, edge_ref[...], store)
    apply_energy(cells_ref, first_ref, energy_ref, metric_ref, shift_ref)
    energy = energy_ref[...] + skeleton_sum(per_tile(penalty_ref) * change * change)
    sublanes = lax.broadcasted_iota(jnp.int32, (ROWS, LANES), 0)
    lanes = lax.broadcasted_iota(jnp.int32, (ROWS, LANES), 1)
    spread = jnp.zeros((ROWS, LANES), F32)
    for index, value in enumerate([sums_ref[0], crossed, energy, sums_ref[2], sourced]):
        column = jnp.sum(value, axis=1, keepdims=True)
        spread = jnp.where(lanes == sublanes + index * ROWS, column, spread)
    message = jnp.sum(spread, axis=0, keepdims=True)
    message_ref[...] = jnp.broadcast_to(message, message_ref.shape)


def scale_kernel(scalars_ref, kept_ref, change_ref, out_ref):
    sublanes = lax.broadcasted_iota(jnp.int32, (ROWS, LANES), 0)
    lanes = lax.broadcasted_iota(jnp.int32, (ROWS, LANES), 1)
    total = jnp.sum(scalars_ref[...], axis=0, keepdims=True)
    g00, g01, g11, h0, h1 = [
        jnp.sum(jnp.where(lanes == sublanes + index * ROWS, total, 0.0), axis=1, keepdims=True)
        for index in range(SCALARS)
    ]
    ratio = g01 / g00
    pivot = g11 - ratio * g01
    second = jnp.where(pivot > 0.0, (h1 - ratio * h0) / pivot, 0.0)
    first = h0 / g00 - ratio * second
    for mode in range(MODES - 1):
        out_ref[mode, 2] = jnp.where(lanes < LANES // 2, first, second)
        out_ref[mode, 3] = jnp.zeros((ROWS, LANES), F32)
    for high in range(HIGH):
        value = first * kept_ref[2, row_block(high), :] + second * change_ref[row_block(high), :]
        for part in range(2):
            block, row = tail_place(2 * high + part)
            out_ref[block, row] = value[:, lane_block(part)]


def combine_kernel(matrix_ref, last_ref, tail_ref, pairs_ref, out_ref, block_ref):
    last = last_ref[...]
    for mode in range(MODES):
        first = tail_ref[mode, 2, :, 0:1]
        second = tail_ref[mode, 2, :, LANES // 2 : LANES // 2 + 1]
        for index in range(GROUP):
            value = first * pairs_ref[mode, index] + second * pairs_ref[mode, GROUP + index]
            if index < 2:
                value = value + last * tail_ref[mode, 2 + index]
            block_ref[index, row_block(mode), :] = value
        for index in range(2):
            block_ref[GROUP + index, row_block(mode), :] = tail_ref[mode, index]
    matrix = matrix_ref[...]
    for index in range(BLOCK):
        mixed = jnp.dot(matrix, block_ref[index], precision=HIGHEST, preferred_element_type=F32)
        out_ref[:, index] = mixed.reshape(MODES, ROWS, LANES)


def unpack_kernel(packed_ref, edge_ref, out_ref):
    for index, node in enumerate(INNER_NODES):
        out_ref[node] = packed_ref[index // GROUP, index % GROUP]

    def load(index):
        block, row = result_place(index)
        return packed_ref[block, row]

    def store(slot, value):
        out_ref[CYCLE_NODES[slot]] = value

    gather_cycle(read_skeleton(load), edge_ref[...], store)


def call(kernel, out_shapes, scratch, *operands):
    return pl.pallas_call(
        kernel,
        out_shape=out_shapes,
        scratch_shapes=scratch,
        compiler_params=pltpu.CompilerParams(vmem_limit_bytes=VMEM_LIMIT),
    )(*operands)


def shape(*dims):
    return jax.ShapeDtypeStruct(dims, F32)


def swap_blocks(blocks, axis="mode"):
    return lax.all_to_all(blocks, axis, split_axis=0, concat_axis=0, tiled=True)


def exchange(slots):
    count = lax.axis_size("elem")
    return [
        lax.ppermute(slots, "elem", [(i, i ^ 1 << level) for i in range(count)])
        for level in range(count.bit_length() - 1)
    ]


def body(forcing, metric, edge_map, shared_rows, partner_masks, penalty):
    forward, backward = [jnp.asarray(table) for table in fourier_tables()]
    table, cross = [jnp.asarray(part) for part in diagonal_tables()]
    mode = lax.axis_index("mode")
    rows_global = mode * ROWS + jnp.arange(ROWS, dtype=jnp.int32)
    shift = jnp.broadcast_to(helmholtz_shift(rows_global)[:, None], (ROWS, LANES))
    last = jnp.broadcast_to(jnp.where(mode == MODES - 1, 1.0, 0.0), (ROWS, LANES)).astype(F32)
    share = lax.dynamic_slice(forward, (0, mode * ROWS), (PLANES, ROWS))
    edge_rows = edge_map.T
    shared = shared_rows.reshape(SLOT_TILES, LANES)
    masks = partner_masks.reshape(SLOT_TILES, LANES)
    penalties = jnp.pad(penalty, (0, HIGH * LOW - SKEL), constant_values=1.0).reshape(HIGH, LOW)
    left = pltpu.VMEM((2 * HIGH * ROWS, CYCLE * LANES), BF16)
    right = pltpu.VMEM((CYCLE * LANES, LOW), BF16)
    left_slots = pltpu.VMEM((2 * HIGH * ROWS, SLOTS), BF16)
    cells = pltpu.VMEM((NODES, ROWS, LANES), F32)
    first = pltpu.VMEM((NODES, 8, LANES), F32)
    energy = pltpu.VMEM((ROWS, LANES), F32)
    wide = (HIGH * ROWS, LOW)

    packed, slots = call(
        pack_kernel, [shape(MODES, BLOCK, ROWS, LANES), shape(SLOT_TILES, ROWS, LANES)], [left, right],
        forcing.transpose(1, 0, 2), edge_rows, shared,
    )
    gathered = swap_blocks(packed)
    inner, diagonal, message, right_slots = call(
        diagonal_kernel,
        [
            shape(2, INNER, LANES), shape(*wide), shape(SLOT_TILES, ROWS + 8, LANES),
            jax.ShapeDtypeStruct((SLOTS, LOW), BF16),
        ],
        [pltpu.VMEM((2, NODES, LANES), F32), left, right],
        metric, table, cross, edge_rows, penalties, shared, shared.T, slots,
    )
    mixed, extra = call(
        transform_kernel, [shape(MODES, SHARE, ROWS, LANES), shape(SLOT_TILES, 8, LANES)], [],
        forward, share, gathered, *exchange(message), masks,
    )
    source = swap_blocks(mixed)
    pairs, kept, slots, sums = call(
        first_kernel,
        [
            shape(MODES, 2 * GROUP, ROWS, LANES), shape(4, *wide), shape(SLOT_TILES, ROWS, LANES),
            shape(4, ROWS, LANES),
        ],
        [left, right, cells, cells, first, energy],
        source, extra, shared, right_slots, edge_rows, metric, inner, diagonal, penalties, shift,
    )
    pair_blocks = swap_blocks(pairs)
    change, message = call(
        second_kernel,
        [shape(*wide), shape(ELEMS_AXIS, LANES)],
        [left_slots, cells, first, energy],
        pairs, kept, sums, *exchange(slots), masks, shared, right_slots, edge_rows, metric, penalties, shift,
    )
    message, pair_blocks = lax.optimization_barrier((message, pair_blocks))
    scalars = swap_blocks(message, "elem")
    tail = call(scale_kernel, shape(MODES, TAIL, ROWS, LANES), [], scalars, kept, change)
    mixed = call(
        combine_kernel, shape(MODES, BLOCK, ROWS, LANES), [pltpu.VMEM((BLOCK, PLANES, LANES), F32)],
        backward, last, swap_blocks(tail), pair_blocks,
    )
    result = call(unpack_kernel, shape(NODES, ROWS, LANES), [], swap_blocks(mixed), edge_rows)
    return result.transpose(1, 0, 2)


def solution(mesh):
    placed = (
        P("mode", None, "elem"),
        P(None, None, "elem"),
        P("elem", None),
        P("elem"),
        P("elem"),
        P("elem"),
    )
    return jax.shard_map(
        body, mesh=mesh, in_specs=placed, out_specs=P("mode", None, "elem"), check_vma=False
    )
```

```python
import functools
import math

import jax
import jax.numpy as jnp
import numpy as np
from jax import lax
from jax.experimental import pallas as pl
from jax.experimental.pallas import tpu as pltpu
from jax.sharding import PartitionSpec as P

ORDER = 8
SIDE = ORDER + 1
NODES = SIDE * SIDE
CYCLE = 32
INNER = (ORDER - 1) ** 2
ROWS = 16
LANES = 128
PLANES = 128
MODES = 8
ELEMS_AXIS = 32
SKEL = 2113
LOW = 256
HIGH = 9
TILES = 2 * HIGH
SLOTS = 384
SLOT_TILES = SLOTS // LANES
BLOCK = 9
SHARE = BLOCK + SLOT_TILES
SCALARS = 5
STEP_ORDER = [4, 5, 7, 2, 6, 3, 1]
SPACING = 0.25
F32 = jnp.float32
BF16 = jnp.bfloat16
HIGHEST = lax.Precision.HIGHEST
VMEM_LIMIT = 32 * 1024 * 1024
FIRST_LIMIT = 56 * 1024 * 1024


def legendre_table(points, poly_order):
    table = np.zeros((points.shape[0], poly_order + 1))
    table[:, 0] = 1.0
    table[:, 1] = points
    for degree in range(2, poly_order + 1):
        table[:, degree] = (
            (2 * degree - 1) * points * table[:, degree - 1] - (degree - 1) * table[:, degree - 2]
        ) / degree
    return table


def lobatto_derivative(poly_order):
    node_count = poly_order + 1
    points = np.cos(np.pi * np.arange(node_count) / poly_order)
    for newton_step in range(100):
        table = legendre_table(points, poly_order)
        points = points - (points * table[:, poly_order] - table[:, poly_order - 1]) / (
            node_count * table[:, poly_order]
        )
    points = np.sort(points)
    top_values = legendre_table(points, poly_order)[:, poly_order]
    identity = np.eye(node_count)
    differ = points[:, None] - points[None, :] + identity
    matrix = top_values[:, None] / (top_values[None, :] * differ)
    matrix = matrix * (1.0 - identity)
    matrix[0, 0] = -poly_order * node_count / 4.0
    matrix[poly_order, poly_order] = poly_order * node_count / 4.0
    return matrix


def fourier_tables():
    positions = np.arange(PLANES)
    phases = ((positions // 2)[:, None] * positions[None, :] % PLANES) * (2.0 * np.pi / PLANES)
    cosine, sine = np.cos(phases), np.sin(phases)
    even = (positions % 2 == 0)[:, None]
    nyquist = (positions == 1)[:, None]
    alternate = (1.0 - 2.0 * (positions % 2))[None, :]
    forward = np.where(nyquist, alternate, np.where(even, cosine, -sine)) / PLANES
    backward = np.where(nyquist, alternate, np.where(even, 2.0 * cosine, -2.0 * sine))
    backward = np.where((positions == 0)[:, None], 1.0, backward)
    return forward.astype(np.float32), backward.T.astype(np.float32)


DERIVATIVE64 = lobatto_derivative(ORDER)
DERIVATIVE = DERIVATIVE64.astype(np.float32)
CYCLE_NODES = (
    [i * SIDE for i in range(SIDE)]
    + [i * SIDE + ORDER for i in range(SIDE)]
    + [j for j in range(1, ORDER)]
    + [ORDER * SIDE + j for j in range(1, ORDER)]
)
INNER_NODES = [i * SIDE + j for i in range(1, ORDER) for j in range(1, ORDER)]


def diagonal_tables():
    squared = (DERIVATIVE * DERIVATIVE).astype(np.float64)
    first = np.kron(squared.T, np.eye(SIDE))
    second = np.kron(np.eye(SIDE), squared.T)
    corner = np.diagonal(DERIVATIVE)
    cross = 2.0 * np.outer(corner, corner).reshape(NODES, 1)
    cross = np.broadcast_to(cross, (NODES, LANES))
    return np.concatenate([first, second], axis=1).astype(np.float32), cross.astype(np.float32)


def helmholtz_shift():
    rows_global = lax.axis_index("mode") * ROWS + lax.broadcasted_iota(jnp.int32, (ROWS, LANES), 0)
    wavenumber = jnp.right_shift(rows_global, 1).astype(F32)
    spanwise = wavenumber * (2.0 * math.pi / (PLANES * SPACING))
    spanwise = jnp.where(rows_global == 1, math.pi / SPACING, spanwise)
    return spanwise * spanwise


def row_block(index):
    return slice(index * ROWS, (index + 1) * ROWS)


def lane_block(index):
    return slice(index * LANES, (index + 1) * LANES)


def pieces(value):
    top = value.astype(BF16).astype(F32)
    return top, value - top


def one_hot_rows(low_rows):
    sublanes = lax.broadcasted_iota(jnp.int32, (LOW, low_rows.shape[1]), 0)
    return jnp.where(low_rows == sublanes, 1.0, 0.0).astype(BF16)


def masked_store(value, high_row, left_ref, column):
    top, rest = pieces(value)
    for high in range(HIGH):
        here = high_row == high
        left_ref[row_block(high), lane_block(column)] = jnp.where(here, top, 0.0).astype(BF16)
        left_ref[row_block(HIGH + high), lane_block(column)] = jnp.where(here, rest, 0.0).astype(BF16)


def scatter_sum(left, selectors):
    contract = (((1,), (1,)), ((), ()))
    both = lax.dot_general(left, selectors, contract, preferred_element_type=F32)
    return both[: HIGH * ROWS] + both[HIGH * ROWS :]


def one_hot_cycle(edge_rows, selectors_ref):
    low = jnp.bitwise_and(edge_rows, LOW - 1)
    for slot in range(CYCLE):
        selectors_ref[:, lane_block(slot)] = one_hot_rows(low[slot : slot + 1, :])


def scatter_cycle(load, edge_rows, left_ref, selectors_ref):
    high_rows = jnp.right_shift(edge_rows, 8)
    for slot in range(CYCLE):
        masked_store(load(slot), high_rows[slot : slot + 1, :], left_ref, slot)
    return scatter_sum(left_ref[...], selectors_ref[...])


def slot_selectors(shared_rows):
    low = jnp.bitwise_and(shared_rows, LOW - 1)
    return jnp.concatenate(
        [one_hot_rows(low[tile : tile + 1, :]) for tile in range(SLOT_TILES)], axis=1
    )


def four_pieces(first, second):
    sublanes = lax.broadcasted_iota(jnp.int32, (ROWS, first.shape[1]), 0)
    first_top, first_rest = pieces(first)
    second_top, second_rest = pieces(second)
    rest = jnp.where(sublanes == 2, first_rest, jnp.where(sublanes == 3, second_rest, 0.0))
    return jnp.where(sublanes == 0, first_top, jnp.where(sublanes == 1, second_top, rest))


def masked_store_four(value, high_row, left_ref, column):
    for high in range(HIGH):
        part = jnp.where(high_row == high, value, 0.0).astype(BF16)
        left_ref[row_block(high), lane_block(column)] = part


def two_rows(total, high):
    base = high * ROWS
    first = total[base : base + 1, :] + total[base + 2 : base + 3, :]
    second = total[base + 1 : base + 2, :] + total[base + 3 : base + 4, :]
    return first, second


def scatter_slots(load, shared_rows, left_ref, right):
    high_rows = jnp.right_shift(shared_rows, 8)
    for tile in range(SLOT_TILES):
        masked_store(load(tile), high_rows[tile : tile + 1, :], left_ref, tile)
    return scatter_sum(left_ref[:, :SLOTS], right)


def stack_pieces(skeleton):
    top, rest = pieces(skeleton)
    return jnp.concatenate([top.astype(BF16), rest.astype(BF16)], axis=0)


def gather_tile(stacked, rows, keep=None):
    low = jnp.bitwise_and(rows, LOW - 1)
    high = jnp.right_shift(rows, 8)
    selector = one_hot_rows(low)
    if keep is not None:
        keep(selector)
    found = jnp.dot(stacked, selector, preferred_element_type=F32)
    total = None
    for index in range(HIGH):
        part = found[row_block(index), :] + found[row_block(HIGH + index), :]
        part = jnp.where(high == index, part, 0.0)
        total = part if total is None else total + part
    return total


def keep_columns(selectors_ref, column, selector):
    selectors_ref[:, column * LANES : (column + 2) * LANES] = selector


def gather_cycle(skeleton, edge_rows, store, selectors_ref=None):
    stacked = stack_pieces(skeleton)
    for pair in range(CYCLE // 2):
        rows = jnp.concatenate(
            [edge_rows[2 * pair : 2 * pair + 1, :], edge_rows[2 * pair + 1 : 2 * pair + 2, :]], axis=1
        )
        keep = None
        if selectors_ref is not None:
            keep = functools.partial(keep_columns, selectors_ref, 2 * pair)
        total = gather_tile(stacked, rows, keep)
        store(2 * pair, total[:, :LANES])
        store(2 * pair + 1, total[:, LANES:])


def gather_slots(skeleton, shared_rows):
    stacked = stack_pieces(skeleton)
    return [gather_tile(stacked, shared_rows[tile : tile + 1, :]) for tile in range(SLOT_TILES)]


def sent_place(index):
    return index // BLOCK, index % BLOCK


def read_skeleton(load):
    return jnp.concatenate(
        [jnp.concatenate([load(2 * high), load(2 * high + 1)], axis=1) for high in range(HIGH)], axis=0
    )


def write_skeleton(skeleton, store):
    for high in range(HIGH):
        store(2 * high, skeleton[row_block(high), :LANES])
        store(2 * high + 1, skeleton[row_block(high), LANES:])


def write_place(ref, place):
    def store(index, value):
        block, row = place(index)
        ref[block, row] = value

    return store


def fold(value):
    return value[:, :LANES] + value[:, LANES:]


def per_tile(penalty_ref):
    return jnp.concatenate(
        [jnp.broadcast_to(penalty_ref[high : high + 1, :], (ROWS, LOW)) for high in range(HIGH)], axis=0
    )


def skeleton_sum(product):
    total = None
    for high in range(HIGH):
        part = fold(product[row_block(high), :])
        total = part if total is None else total + part
    return total


def select_arrived(masks, tile, arrived):
    chosen = arrived[0]
    row = masks[tile : tile + 1, :]
    for level in range(1, len(arrived)):
        moving = jnp.bitwise_and(jnp.right_shift(row, level), 1) == 1
        chosen = jnp.where(moving, arrived[level], chosen)
    return chosen


def weighted_sum(weights, values):
    total = None
    for weight, value in zip(weights, values):
        if weight == 0.0:
            continue
        part = float(weight) * value
        total = part if total is None else total + part
    return total


def derivative_line(values, transposed):
    matrix = DERIVATIVE64.T if transposed else DERIVATIVE64
    half = SIDE // 2
    evens = [values[k] + values[ORDER - k] for k in range(half)] + [values[half]]
    odds = [values[k] - values[ORDER - k] for k in range(half)]
    results = [None] * SIDE
    for out in range(half):
        near, far = matrix[out, :half], matrix[out, :half:-1]
        even = weighted_sum(np.float32(np.append(0.5 * (near + far), matrix[out, half])), evens)
        odd = weighted_sum(np.float32(0.5 * (near - far)), odds)
        results[out] = odd + even
        results[ORDER - out] = odd - even
    results[half] = weighted_sum(np.float32(matrix[half, :half]), odds)
    return results


def gradients(cells_ref, first_ref, metric_ref, rows, visit):
    for j in range(SIDE):
        line = derivative_line([cells_ref[k * SIDE + j, rows, :] for k in range(SIDE)], False)
        for i in range(SIDE):
            first_ref[i * SIDE + j] = line[i]
    for i in range(SIDE):
        line = derivative_line([cells_ref[i * SIDE + k, rows, :] for k in range(SIDE)], False)
        seconds = []
        for j in range(SIDE):
            node = i * SIDE + j
            m0, m1, m2 = [metric_ref[node, c : c + 1, :] for c in range(3)]
            g1, g2 = first_ref[node], line[j]
            p1 = m0 * g1 + m2 * g2
            p2 = m2 * g1 + m1 * g2
            visit(node, g1, g2, p1, p2)
            seconds.append(p2)
        yield i, seconds


def apply_operator(cells_ref, result_ref, first_ref, energy_ref, metric_ref, shift_ref):
    @pl.loop(0, 2)
    def half(part):
        rows = pl.ds(pl.multiple_of(part * 8, 8), 8)
        shift = shift_ref[rows, :]

        def visit(node, g1, g2, p1, p2):
            first_ref[node] = p1

        for i, seconds in gradients(cells_ref, first_ref, metric_ref, rows, visit):
            line = derivative_line(seconds, True)
            for j in range(SIDE):
                node = i * SIDE + j
                mass = shift * metric_ref[node, 3:4, :]
                result_ref[node, rows, :] = line[j] + mass * cells_ref[node, rows, :]
        energy = jnp.zeros((8, LANES), F32)
        for j in range(SIDE):
            line = derivative_line([first_ref[k * SIDE + j] for k in range(SIDE)], True)
            for i in range(SIDE):
                node = i * SIDE + j
                value = result_ref[node, rows, :] + line[i]
                result_ref[node, rows, :] = value
                energy = energy + value * cells_ref[node, rows, :]
        energy_ref[rows, :] = energy


def apply_energy(cells_ref, first_ref, energy_ref, metric_ref, shift_ref):
    @pl.loop(0, 2)
    def half(part):
        rows = pl.ds(pl.multiple_of(part * 8, 8), 8)
        shift = shift_ref[rows, :]
        sums = [jnp.zeros((8, LANES), F32)]

        def visit(node, g1, g2, p1, p2):
            value = cells_ref[node, rows, :]
            mass = shift * metric_ref[node, 3:4, :]
            sums[0] = sums[0] + (g1 * p1 + g2 * p2 + mass * value * value)

        for i, seconds in gradients(cells_ref, first_ref, metric_ref, rows, visit):
            pass
        energy_ref[rows, :] = sums[0]


def diagonal_slots(
    metric_ref, table_ref, cross_ref, penalty_ref, edge_rows, shared_rows, right_ref,
    inner_ref, skeleton_ref, padded_ref, cells_ref, left_ref,
):
    both = jnp.concatenate([metric_ref[:, 0, :], metric_ref[:, 1, :]], axis=0)
    terms = jnp.dot(table_ref[...], both, precision=HIGHEST, preferred_element_type=F32)
    cells_ref[0] = terms + cross_ref[...] * metric_ref[:, 2, :]
    cells_ref[1] = metric_ref[:, 3, :]
    padded_ref[...] = jnp.ones((HIGH, LOW), F32)
    for high in range(HIGH):
        count = min(LOW, SKEL - high * LOW)
        line = penalty_ref[pl.ds(high * LOW, count)]
        padded_ref[high : high + 1, :count] = line.reshape(1, count)
    for index, node in enumerate(INNER_NODES):
        inner_ref[0, index : index + 1, :] = cells_ref[0, node : node + 1, :]
        inner_ref[1, index : index + 1, :] = cells_ref[1, node : node + 1, :]
    high_rows = jnp.right_shift(edge_rows, 8)
    for slot in range(CYCLE):
        node = CYCLE_NODES[slot]
        value = four_pieces(cells_ref[0, node : node + 1, :], cells_ref[1, node : node + 1, :])
        masked_store_four(value, high_rows[slot : slot + 1, :], left_ref, slot)
    contract = (((1,), (1,)), ((), ()))
    total = lax.dot_general(
        left_ref[: HIGH * ROWS, :], right_ref[...], contract, preferred_element_type=F32
    )
    stacked = []
    for high in range(HIGH):
        laplace, mass = two_rows(total, high)
        laplace = laplace + padded_ref[high : high + 1, :]
        skeleton_ref[0, high : high + 1, :] = laplace
        skeleton_ref[1, high : high + 1, :] = mass
        stacked.append(four_pieces(laplace, mass).astype(BF16))
    stacked = jnp.concatenate(stacked, axis=0)
    results = []
    for tile in range(SLOT_TILES):
        rows = shared_rows[tile : tile + 1, :]
        low = jnp.bitwise_and(rows, LOW - 1)
        high_row = jnp.right_shift(rows, 8)
        found = jnp.dot(stacked, one_hot_rows(low), preferred_element_type=F32)
        value = jnp.zeros((ROWS, LANES), F32)
        for high in range(HIGH):
            value = value + jnp.where(high_row == high, found[row_block(high), :], 0.0)
        results.append(two_rows(value, 0))
    return results


def pack_kernel(
    forcing_hbm, edge_hbm, shared_hbm, metric_hbm, penalty_hbm, table_hbm, cross_hbm,
    out_hbm, message_hbm, inner_hbm, skeleton_hbm, padded_hbm,
    forcing_ref, edge_ref, shared_ref, metric_ref, penalty_ref, table_ref, cross_ref,
    packed_ref, message_ref, inner_ref, skeleton_ref, padded_ref,
    cells_ref, left_ref, right_ref, in_semaphores, out_semaphores,
):
    ins = [
        pltpu.make_async_copy(source, target, in_semaphores.at[index])
        for index, (source, target) in enumerate(
            [
                (edge_hbm, edge_ref), (shared_hbm, shared_ref), (forcing_hbm, forcing_ref),
                (metric_hbm, metric_ref), (table_hbm, table_ref), (cross_hbm, cross_ref),
                (penalty_hbm, penalty_ref),
            ]
        )
    ]
    for copy in ins:
        copy.start()
    outs = []

    def send(source, target):
        copy = pltpu.make_async_copy(source, target, out_semaphores.at[len(outs)])
        copy.start()
        outs.append(copy)

    width = ORDER - 1
    for index in range(TILES, MODES * BLOCK - INNER):
        packed_ref[index] = jnp.zeros((ROWS, LANES), F32)
    ins[0].wait()
    edge_rows = edge_ref[...]
    one_hot_cycle(edge_rows, right_ref)
    ins[1].wait()
    shared_rows = shared_ref[...]
    ins[2].wait()
    for line in range(width):
        send(forcing_ref.at[pl.ds((line + 1) * SIDE + 1, width)], out_hbm.at[pl.ds(line * width, width)])
    for copy in ins[3:]:
        copy.wait()
    pairs = diagonal_slots(
        metric_ref, table_ref, cross_ref, penalty_ref, edge_rows, shared_rows, right_ref,
        inner_ref, skeleton_ref, padded_ref, cells_ref, left_ref,
    )
    send(inner_ref, inner_hbm)
    send(skeleton_ref, skeleton_hbm)
    send(padded_ref, padded_hbm)
    skeleton = scatter_cycle(lambda slot: forcing_ref[CYCLE_NODES[slot]], edge_rows, left_ref, right_ref)

    def store(index, value):
        packed_ref[index] = value

    write_skeleton(skeleton, store)
    send(packed_ref, out_hbm.at[pl.ds(INNER, MODES * BLOCK - INNER)])
    for tile, value in enumerate(gather_slots(skeleton, shared_rows)):
        laplace, mass = pairs[tile]
        message_ref[tile, :ROWS, :] = value
        message_ref[tile, ROWS:, :] = jnp.zeros((8, LANES), F32)
        message_ref[tile, ROWS : ROWS + 1, :] = laplace
        message_ref[tile, ROWS + 1 : ROWS + 2, :] = mass
    send(message_ref, message_hbm)
    for copy in outs:
        copy.wait()


def place(index):
    return pl.ds(pl.multiple_of(index * ROWS, ROWS), ROWS)


def relative_rows(matrix_ref, mode):
    parts = [matrix_ref[place(jnp.bitwise_xor(mode, step)), :] for step in range(MODES)]
    return jnp.concatenate(parts, axis=0)


def transform_kernel(
    matrix_ref, in_ref, a0, a1, a2, a3, a4, masks_ref, o0, o1, o2, o3, o4, o5, o6, o7, extra_ref, slots_ref
):
    mode = lax.axis_index("mode")
    outs = [o0, o1, o2, o3, o4, o5, o6, o7]
    matrix = relative_rows(matrix_ref, mode)
    slots_ref[...] = jnp.zeros(slots_ref.shape, F32)
    arrived_refs = [a0, a1, a2, a3, a4]
    masks = masks_ref[...]
    for index in range(BLOCK):
        block = in_ref[:, index].reshape(PLANES, LANES)
        mixed = jnp.dot(matrix, block, precision=HIGHEST, preferred_element_type=F32)
        for step, out_ref in enumerate(outs):
            out_ref[index] = mixed[row_block(step), :]
    for tile in range(SLOT_TILES):
        chosen = select_arrived(masks, tile, [ref[tile] for ref in arrived_refs])
        slots_ref[tile, place(mode), :] = chosen[:ROWS]
        mixed = jnp.dot(matrix, slots_ref[tile], precision=HIGHEST, preferred_element_type=F32)
        for step, out_ref in enumerate(outs):
            out_ref[BLOCK + tile] = mixed[row_block(step), :]
        extra_ref[tile] = chosen[ROWS:]


def first_kernel(
    i4, i5, i7, i2, i6, i3, i1, i0, extra_ref, shared_ref, edge_ref, metric_ref,
    inner_ref, diagonal_ref, penalty_ref, search_ref, change_ref, kept_ref, slots_ref, sums_ref,
    left_ref, right_ref, source_ref, cells_ref, result_ref, first_ref, energy_ref, shift_ref,
):
    mode = lax.axis_index("mode")
    ins = [i0, i1, i2, i3, i4, i5, i6, i7]
    for step, in_ref in enumerate(ins):
        source_ref[jnp.bitwise_xor(mode, step)] = in_ref[:BLOCK]
    shared_rows = shared_ref[...]
    right_slots = slot_selectors(shared_rows)
    shift = helmholtz_shift()
    shift_ref[...] = shift
    edge_rows = edge_ref[...]

    def load_right(tile):
        total = ins[0][BLOCK + tile]
        for in_ref in ins[1:]:
            total = total + in_ref[BLOCK + tile]
        return total

    def source(index):
        block, row = sent_place(index)
        return source_ref[block, row]

    high_rows = jnp.right_shift(shared_rows, 8)
    for tile in range(SLOT_TILES):
        value = four_pieces(extra_ref[tile, 0:1, :], extra_ref[tile, 1:2, :])
        masked_store_four(value, high_rows[tile : tile + 1, :], left_ref, tile)
    contract = (((1,), (1,)), ((), ()))
    added = lax.dot_general(
        left_ref[: HIGH * ROWS, :SLOTS], right_slots, contract, preferred_element_type=F32
    )
    wide_shift = jnp.concatenate([shift, shift], axis=1)
    parts = []
    for high in range(HIGH):
        laplace, mass = two_rows(added, high)
        laplace = laplace + diagonal_ref[0, high : high + 1, :]
        mass = mass + diagonal_ref[1, high : high + 1, :]
        parts.append(1.0 / (laplace + wide_shift * mass))
    inverse = jnp.concatenate(parts, axis=0)
    local = read_skeleton(lambda index: source(INNER + index))
    right_side = local + scatter_slots(load_right, shared_rows, left_ref, right_slots)
    search = right_side * inverse
    kept_ref[0] = local
    kept_ref[1] = inverse
    kept_ref[2] = search
    start = skeleton_sum(local * search)
    for index, node in enumerate(INNER_NODES):
        value = source(index)
        inverted = 1.0 / (inner_ref[0, index : index + 1, :] + shift * inner_ref[1, index : index + 1, :])
        scaled = value * inverted
        search_ref[index] = scaled
        change_ref[index] = inverted
        cells_ref[node] = scaled
        start = start + value * scaled

    def store(slot, value):
        cells_ref[CYCLE_NODES[slot]] = value

    gather_cycle(search, edge_rows, store, right_ref)
    apply_operator(cells_ref, result_ref, first_ref, energy_ref, metric_ref, shift_ref)
    weighted = per_tile(penalty_ref) * search
    applied = weighted + scatter_cycle(
        lambda slot: result_ref[CYCLE_NODES[slot]], edge_rows, left_ref, right_ref
    )
    kept_ref[3] = applied
    for tile, value in enumerate(gather_slots(applied, shared_rows)):
        slots_ref[tile] = value
    crossed = jnp.zeros((ROWS, LANES), F32)
    sourced = jnp.zeros((ROWS, LANES), F32)
    for index, node in enumerate(INNER_NODES):
        value = result_ref[node]
        moved = value * change_ref[index] - cells_ref[node]
        change_ref[index] = moved
        crossed = crossed + value * moved
        sourced = sourced + source(index) * moved
    sums_ref[0] = energy_ref[...] + skeleton_sum(weighted * search)
    sums_ref[1] = crossed
    sums_ref[2] = start
    sums_ref[3] = sourced


def second_kernel(
    moved_ref, kept_ref, sums_ref, a0, a1, a2, a3, a4, masks_ref, shared_ref, edge_ref,
    metric_ref, penalty_ref, change_ref, message_ref, left_ref, cells_ref, first_ref, energy_ref, shift_ref,
):
    arrived_refs = [a0, a1, a2, a3, a4]
    masks = masks_ref[...]
    shared_rows = shared_ref[...]
    shift_ref[...] = helmholtz_shift()

    def load(tile):
        return select_arrived(masks, tile, [ref[tile] for ref in arrived_refs])

    local, inverse, search, applied = [kept_ref[index] for index in range(4)]
    full = applied + scatter_slots(load, shared_rows, left_ref, slot_selectors(shared_rows))
    change = full * inverse - search
    change_ref[...] = change
    crossed = sums_ref[1] + skeleton_sum(applied * change)
    sourced = sums_ref[3] + skeleton_sum(local * change)
    for index, node in enumerate(INNER_NODES):
        cells_ref[node] = moved_ref[index]

    def store(slot, value):
        cells_ref[CYCLE_NODES[slot]] = value

    gather_cycle(change, edge_ref[...], store)
    apply_energy(cells_ref, first_ref, energy_ref, metric_ref, shift_ref)
    energy = energy_ref[...] + skeleton_sum(per_tile(penalty_ref) * change * change)
    sublanes = lax.broadcasted_iota(jnp.int32, (ROWS, LANES), 0)
    lanes = lax.broadcasted_iota(jnp.int32, (ROWS, LANES), 1)
    spread = jnp.zeros((ROWS, LANES), F32)
    for index, value in enumerate([sums_ref[0], crossed, energy, sums_ref[2], sourced]):
        column = jnp.sum(value, axis=1, keepdims=True)
        spread = jnp.where(lanes == sublanes + index * ROWS, column, spread)
    message = jnp.sum(spread, axis=0, keepdims=True)
    message_ref[...] = jnp.broadcast_to(message, message_ref.shape)


def scale_kernel(
    scalars_ref, inner_ref, moved_ref, kept_ref, change_ref, o0, o1, o2, o3, o4, o5, o6, o7, packed_ref
):
    sublanes = lax.broadcasted_iota(jnp.int32, (ROWS, LANES), 0)
    lanes = lax.broadcasted_iota(jnp.int32, (ROWS, LANES), 1)
    total = jnp.sum(scalars_ref[...], axis=0, keepdims=True)
    g00, g01, g11, h0, h1 = [
        jnp.sum(jnp.where(lanes == sublanes + index * ROWS, total, 0.0), axis=1, keepdims=True)
        for index in range(SCALARS)
    ]
    ratio = g01 / g00
    pivot = g11 - ratio * g01
    second = jnp.where(pivot > 0.0, (h1 - ratio * h0) / pivot, 0.0)
    first = jnp.broadcast_to(h0 / g00 - ratio * second, (ROWS, LANES))
    second = jnp.broadcast_to(second, (ROWS, LANES))
    store = write_place(packed_ref, sent_place)
    for index in range(INNER):
        store(index, first * inner_ref[index] + second * moved_ref[index])
    for high in range(HIGH):
        for part in range(2):
            place = (row_block(high), lane_block(part))
            value = first * kept_ref[(2,) + place] + second * change_ref[place]
            store(INNER + 2 * high + part, value)
    for index in range(INNER + TILES, MODES * BLOCK):
        store(index, jnp.zeros((ROWS, LANES), F32))
    mode = lax.axis_index("mode")
    for step, out_ref in enumerate([o0, o1, o2, o3, o4, o5, o6, o7]):
        out_ref[...] = packed_ref[jnp.bitwise_xor(mode, step)]


def combine_kernel(
    matrix_ref, i4, i5, i7, i2, i6, i3, i1, i0, o0, o1, o2, o3, o4, o5, o6, o7, block_ref
):
    mode = lax.axis_index("mode")
    for step, in_ref in enumerate([i0, i1, i2, i3, i4, i5, i6, i7]):
        block_ref[:, place(jnp.bitwise_xor(mode, step)), :] = in_ref[...]
    matrix = relative_rows(matrix_ref, mode)
    for index in range(BLOCK):
        mixed = jnp.dot(matrix, block_ref[index], precision=HIGHEST, preferred_element_type=F32)
        for step, out_ref in enumerate([o0, o1, o2, o3, o4, o5, o6, o7]):
            out_ref[index] = mixed[row_block(step), :]


def unpack_kernel(i4, i5, i7, i2, i6, i3, i1, i0, edge_ref, out_ref, packed_ref):
    mode = lax.axis_index("mode")
    for step, in_ref in enumerate([i0, i1, i2, i3, i4, i5, i6, i7]):
        packed_ref[jnp.bitwise_xor(mode, step)] = in_ref[...]

    def load(index):
        block, row = sent_place(index)
        return packed_ref[block, row]

    for index, node in enumerate(INNER_NODES):
        out_ref[node] = load(index)

    def store(slot, value):
        out_ref[CYCLE_NODES[slot]] = value

    gather_cycle(read_skeleton(lambda index: load(INNER + index)), edge_ref[...], store)


def call(kernel, out_shapes, scratch, *operands, limit=VMEM_LIMIT, **options):
    return pl.pallas_call(
        kernel,
        out_shape=out_shapes,
        scratch_shapes=scratch,
        compiler_params=pltpu.CompilerParams(vmem_limit_bytes=limit),
        **options,
    )(*operands)


def shape(*dims, dtype=F32):
    return jax.ShapeDtypeStruct(dims, dtype)


def swap_blocks(blocks, axis):
    return lax.all_to_all(blocks, axis, split_axis=0, concat_axis=0, tiled=True)


def permute(value, axis, flip):
    return lax.ppermute(value, axis, [(i, i ^ flip) for i in range(lax.axis_size(axis))])


def swap_steps(blocks):
    return [permute(blocks[step], "mode", step) for step in STEP_ORDER] + [blocks[0]]


def exchange(slots):
    levels = lax.axis_size("elem").bit_length() - 1
    return [permute(slots, "elem", 1 << level) for level in range(levels)]


def body(forcing, metric, edge_map, shared_rows, partner_masks, penalty):
    forward, backward = [jnp.asarray(part) for part in fourier_tables()]
    table, cross = [jnp.asarray(part) for part in diagonal_tables()]
    metric = metric.transpose(1, 0, 2)
    edge_rows = edge_map.T
    shared = shared_rows.reshape(SLOT_TILES, LANES)
    masks = partner_masks.reshape(SLOT_TILES, LANES)
    left = pltpu.VMEM((2 * HIGH * ROWS, CYCLE * LANES), BF16)
    right = pltpu.VMEM((LOW, CYCLE * LANES), BF16)
    left_slots = pltpu.VMEM((2 * HIGH * ROWS, SLOTS), BF16)
    cells = pltpu.VMEM((NODES, ROWS, LANES), F32)
    first = pltpu.VMEM((NODES, 8, LANES), F32)
    energy = pltpu.VMEM((ROWS, LANES), F32)
    packing = pltpu.VMEM((MODES, BLOCK, ROWS, LANES), F32)
    wide = (HIGH * ROWS, LOW)
    blocks = [shape(BLOCK, ROWS, LANES)] * MODES

    hbm = pl.BlockSpec(memory_space=pltpu.HBM)
    packed_shapes = [
        shape(MODES * BLOCK, ROWS, LANES), shape(SLOT_TILES, ROWS + 8, LANES),
        shape(2, INNER, LANES), shape(2, HIGH, LOW), shape(HIGH, LOW),
    ]
    operands = [forcing.transpose(1, 0, 2), edge_rows, shared, metric, penalty, table, cross]
    packed, message, inner, diagonal, penalties = call(
        pack_kernel, packed_shapes,
        [pltpu.VMEM(operand.shape, operand.dtype) for operand in operands]
        + [pltpu.VMEM((MODES * BLOCK - INNER, ROWS, LANES), F32)]
        + [pltpu.VMEM(part.shape, part.dtype) for part in packed_shapes[1:]]
        + [
            pltpu.VMEM((2, NODES, LANES), F32), left, right,
            pltpu.SemaphoreType.DMA((len(operands),)), pltpu.SemaphoreType.DMA((ORDER + 4,)),
        ],
        *operands,
        in_specs=[hbm] * len(operands), out_specs=[hbm] * len(packed_shapes), limit=FIRST_LIMIT,
    )
    gathered = swap_blocks(packed.reshape(MODES, BLOCK, ROWS, LANES), "mode")
    *mixed, extra = call(
        transform_kernel, [shape(SHARE, ROWS, LANES)] * MODES + [shape(SLOT_TILES, 8, LANES)],
        [pltpu.VMEM((SLOT_TILES, PLANES, LANES), F32)], forward, gathered, *exchange(message), masks,
    )
    search, moved, kept, slots, sums = call(
        first_kernel,
        [
            shape(INNER, ROWS, LANES), shape(INNER, ROWS, LANES), shape(4, *wide),
            shape(SLOT_TILES, ROWS, LANES), shape(4, ROWS, LANES),
        ],
        [left, right, packing, cells, cells, first, energy, energy],
        *swap_steps(mixed), extra, shared, edge_rows, metric, inner, diagonal, penalties,
    )
    change, message = call(
        second_kernel,
        [shape(*wide), shape(ELEMS_AXIS, LANES)],
        [left_slots, cells, first, energy, energy],
        moved, kept, sums, *exchange(slots), masks, shared, edge_rows, metric, penalties,
    )
    scalars = swap_blocks(message, "elem")
    scaled = call(scale_kernel, blocks, [packing], scalars, search, moved, kept, change)
    mixed = call(
        combine_kernel, blocks, [pltpu.VMEM((BLOCK, PLANES, LANES), F32)], backward, *swap_steps(scaled)
    )
    result = call(unpack_kernel, shape(NODES, ROWS, LANES), [packing], *swap_steps(mixed), edge_rows)
    return result.transpose(1, 0, 2)


def solution(mesh):
    placed = (
        P("mode", None, "elem"),
        P(None, None, "elem"),
        P("elem", None),
        P("elem"),
        P("elem"),
        P("elem"),
    )
    return jax.shard_map(
        body, mesh=mesh, in_specs=placed, out_specs=P("mode", None, "elem"), check_vma=False
    )
```

```python
import functools
import math

import jax
import jax.numpy as jnp
import numpy as np
from jax import lax
from jax.experimental import pallas as pl
from jax.experimental.pallas import tpu as pltpu
from jax.sharding import PartitionSpec as P

ORDER = 8
SIDE = ORDER + 1
NODES = SIDE * SIDE
CYCLE = 32
INNER = (ORDER - 1) ** 2
ROWS = 16
LANES = 128
PLANES = 128
MODES = 8
ELEMS_AXIS = 32
SKEL = 2113
LOW = 256
HIGH = 9
TILES = 2 * HIGH
SLOTS = 384
SLOT_TILES = SLOTS // LANES
BLOCK = 9
SHARE = BLOCK + SLOT_TILES
SCALARS = 5
STEP_ORDER = [4, 5, 7, 2, 6, 3, 1]
LEVEL_ORDER = [0, 2, 1, 3, 4]
SPACING = 0.25
F32 = jnp.float32
BF16 = jnp.bfloat16
HIGHEST = lax.Precision.HIGHEST
VMEM_LIMIT = 32 * 1024 * 1024
FIRST_LIMIT = 56 * 1024 * 1024


def legendre_table(points, poly_order):
    table = np.zeros((points.shape[0], poly_order + 1))
    table[:, 0] = 1.0
    table[:, 1] = points
    for degree in range(2, poly_order + 1):
        table[:, degree] = (
            (2 * degree - 1) * points * table[:, degree - 1] - (degree - 1) * table[:, degree - 2]
        ) / degree
    return table


def lobatto_derivative(poly_order):
    node_count = poly_order + 1
    points = np.cos(np.pi * np.arange(node_count) / poly_order)
    for newton_step in range(100):
        table = legendre_table(points, poly_order)
        points = points - (points * table[:, poly_order] - table[:, poly_order - 1]) / (
            node_count * table[:, poly_order]
        )
    points = np.sort(points)
    top_values = legendre_table(points, poly_order)[:, poly_order]
    identity = np.eye(node_count)
    differ = points[:, None] - points[None, :] + identity
    matrix = top_values[:, None] / (top_values[None, :] * differ)
    matrix = matrix * (1.0 - identity)
    matrix[0, 0] = -poly_order * node_count / 4.0
    matrix[poly_order, poly_order] = poly_order * node_count / 4.0
    return matrix


def fourier_tables():
    positions = np.arange(PLANES)
    phases = ((positions // 2)[:, None] * positions[None, :] % PLANES) * (2.0 * np.pi / PLANES)
    cosine, sine = np.cos(phases), np.sin(phases)
    even = (positions % 2 == 0)[:, None]
    nyquist = (positions == 1)[:, None]
    alternate = (1.0 - 2.0 * (positions % 2))[None, :]
    forward = np.where(nyquist, alternate, np.where(even, cosine, -sine)) / PLANES
    backward = np.where(nyquist, alternate, np.where(even, 2.0 * cosine, -2.0 * sine))
    backward = np.where((positions == 0)[:, None], 1.0, backward)
    return forward.astype(np.float32), backward.T.astype(np.float32)


DERIVATIVE64 = lobatto_derivative(ORDER)
DERIVATIVE = DERIVATIVE64.astype(np.float32)
CYCLE_NODES = (
    [i * SIDE for i in range(SIDE)]
    + [i * SIDE + ORDER for i in range(SIDE)]
    + [j for j in range(1, ORDER)]
    + [ORDER * SIDE + j for j in range(1, ORDER)]
)
INNER_NODES = [i * SIDE + j for i in range(1, ORDER) for j in range(1, ORDER)]


def diagonal_tables():
    squared = (DERIVATIVE * DERIVATIVE).astype(np.float64)
    first = np.kron(squared.T, np.eye(SIDE))
    second = np.kron(np.eye(SIDE), squared.T)
    corner = np.diagonal(DERIVATIVE)
    cross = 2.0 * np.outer(corner, corner).reshape(NODES, 1)
    cross = np.broadcast_to(cross, (NODES, LANES))
    return np.concatenate([first, second], axis=1).astype(np.float32), cross.astype(np.float32)


def helmholtz_shift():
    rows_global = lax.axis_index("mode") * ROWS + lax.broadcasted_iota(jnp.int32, (ROWS, LANES), 0)
    wavenumber = jnp.right_shift(rows_global, 1).astype(F32)
    spanwise = wavenumber * (2.0 * math.pi / (PLANES * SPACING))
    spanwise = jnp.where(rows_global == 1, math.pi / SPACING, spanwise)
    return spanwise * spanwise


def row_block(index):
    return slice(index * ROWS, (index + 1) * ROWS)


def lane_block(index):
    return slice(index * LANES, (index + 1) * LANES)


def pieces(value):
    top = value.astype(BF16).astype(F32)
    return top, value - top


def one_hot_rows(low_rows):
    sublanes = lax.broadcasted_iota(jnp.int32, (LOW, low_rows.shape[1]), 0)
    return jnp.where(low_rows == sublanes, 1.0, 0.0).astype(BF16)


def masked_store(value, high_row, left_ref, column):
    top, rest = pieces(value)
    for high in range(HIGH):
        here = high_row == high
        left_ref[row_block(high), lane_block(column)] = jnp.where(here, top, 0.0).astype(BF16)
        left_ref[row_block(HIGH + high), lane_block(column)] = jnp.where(here, rest, 0.0).astype(BF16)


def contract_lanes(left, right):
    return lax.dot_general(left, right, (((1,), (1,)), ((), ())), preferred_element_type=F32)


def scatter_sum(left, selectors):
    both = contract_lanes(left, selectors)
    return both[: HIGH * ROWS] + both[HIGH * ROWS :]


def one_hot_cycle(edge_rows, selectors_ref):
    low = jnp.bitwise_and(edge_rows, LOW - 1)
    for slot in range(CYCLE):
        selectors_ref[:, lane_block(slot)] = one_hot_rows(low[slot : slot + 1, :])


def scatter_cycle(load, edge_rows, left_ref, selectors_ref):
    high_rows = jnp.right_shift(edge_rows, 8)
    for slot in range(CYCLE):
        masked_store(load(slot), high_rows[slot : slot + 1, :], left_ref, slot)
    return scatter_sum(left_ref[...], selectors_ref[...])


def slot_selectors(shared_rows):
    low = jnp.bitwise_and(shared_rows, LOW - 1)
    return jnp.concatenate(
        [one_hot_rows(low[tile : tile + 1, :]) for tile in range(SLOT_TILES)], axis=1
    )


def four_pieces(first, second):
    sublanes = lax.broadcasted_iota(jnp.int32, (ROWS, first.shape[1]), 0)
    first_top, first_rest = pieces(first)
    second_top, second_rest = pieces(second)
    rest = jnp.where(sublanes == 2, first_rest, jnp.where(sublanes == 3, second_rest, 0.0))
    return jnp.where(sublanes == 0, first_top, jnp.where(sublanes == 1, second_top, rest))


def masked_store_four(value, high_row, left_ref, column):
    for high in range(HIGH):
        part = jnp.where(high_row == high, value, 0.0).astype(BF16)
        left_ref[row_block(high), lane_block(column)] = part


def two_rows(total, high):
    base = high * ROWS
    first = total[base : base + 1, :] + total[base + 2 : base + 3, :]
    second = total[base + 1 : base + 2, :] + total[base + 3 : base + 4, :]
    return first, second


def scatter_slots(load, shared_rows, left_ref, right):
    high_rows = jnp.right_shift(shared_rows, 8)
    for tile in range(SLOT_TILES):
        masked_store(load(tile), high_rows[tile : tile + 1, :], left_ref, tile)
    return scatter_sum(left_ref[:, :SLOTS], right)


def stack_pieces(skeleton):
    top, rest = pieces(skeleton)
    return jnp.concatenate([top.astype(BF16), rest.astype(BF16)], axis=0)


def gather_tile(stacked, rows, keep=None):
    low = jnp.bitwise_and(rows, LOW - 1)
    high = jnp.right_shift(rows, 8)
    selector = one_hot_rows(low)
    if keep is not None:
        keep(selector)
    found = jnp.dot(stacked, selector, preferred_element_type=F32)
    total = None
    for index in range(HIGH):
        part = found[row_block(index), :] + found[row_block(HIGH + index), :]
        part = jnp.where(high == index, part, 0.0)
        total = part if total is None else total + part
    return total


def keep_columns(selectors_ref, column, selector):
    selectors_ref[:, column * LANES : (column + 2) * LANES] = selector


def gather_cycle(skeleton, edge_rows, store, selectors_ref=None):
    stacked = stack_pieces(skeleton)
    for pair in range(CYCLE // 2):
        rows = jnp.concatenate(
            [edge_rows[2 * pair : 2 * pair + 1, :], edge_rows[2 * pair + 1 : 2 * pair + 2, :]], axis=1
        )
        keep = None
        if selectors_ref is not None:
            keep = functools.partial(keep_columns, selectors_ref, 2 * pair)
        total = gather_tile(stacked, rows, keep)
        store(2 * pair, total[:, :LANES])
        store(2 * pair + 1, total[:, LANES:])


def gather_slots(skeleton, shared_rows):
    stacked = stack_pieces(skeleton)
    return [gather_tile(stacked, shared_rows[tile : tile + 1, :]) for tile in range(SLOT_TILES)]


def sent_place(index):
    return index // BLOCK, index % BLOCK


def read_skeleton(load):
    return jnp.concatenate(
        [jnp.concatenate([load(2 * high), load(2 * high + 1)], axis=1) for high in range(HIGH)], axis=0
    )


def write_skeleton(skeleton, store):
    for high in range(HIGH):
        store(2 * high, skeleton[row_block(high), :LANES])
        store(2 * high + 1, skeleton[row_block(high), LANES:])


def write_place(ref, place):
    def store(index, value):
        block, row = place(index)
        ref[block, row] = value

    return store


def fold(value):
    return value[:, :LANES] + value[:, LANES:]


def per_tile(penalty_ref):
    return jnp.concatenate(
        [jnp.broadcast_to(penalty_ref[high : high + 1, :], (ROWS, LOW)) for high in range(HIGH)], axis=0
    )


def skeleton_sum(product):
    total = None
    for high in range(HIGH):
        part = fold(product[row_block(high), :])
        total = part if total is None else total + part
    return total


def select_arrived(masks, tile, arrived):
    chosen = arrived[0]
    row = masks[tile : tile + 1, :]
    for level in range(1, len(arrived)):
        moving = jnp.bitwise_and(jnp.right_shift(row, level), 1) == 1
        chosen = jnp.where(moving, arrived[level], chosen)
    return chosen


def weighted_sum(weights, values):
    total = None
    for weight, value in zip(weights, values):
        if weight == 0.0:
            continue
        part = float(weight) * value
        total = part if total is None else total + part
    return total


def derivative_line(values, transposed):
    matrix = DERIVATIVE64.T if transposed else DERIVATIVE64
    half = SIDE // 2
    evens = [values[k] + values[ORDER - k] for k in range(half)] + [values[half]]
    odds = [values[k] - values[ORDER - k] for k in range(half)]
    results = [None] * SIDE
    for out in range(half):
        near, far = matrix[out, :half], matrix[out, :half:-1]
        even = weighted_sum(np.float32(np.append(0.5 * (near + far), matrix[out, half])), evens)
        odd = weighted_sum(np.float32(0.5 * (near - far)), odds)
        results[out] = odd + even
        results[ORDER - out] = odd - even
    results[half] = weighted_sum(np.float32(matrix[half, :half]), odds)
    return results


def grid_load(inner_ref, cycle_ref, rows):
    def load(node):
        if node in CYCLE_NODES:
            return cycle_ref[CYCLE_NODES.index(node), rows, :]
        return inner_ref[INNER_NODES.index(node), rows, :]

    return load


def gradients(load, first_ref, metric_ref, visit):
    for j in range(SIDE):
        line = derivative_line([load(k * SIDE + j) for k in range(SIDE)], False)
        for i in range(SIDE):
            first_ref[i * SIDE + j] = line[i]
    for i in range(SIDE):
        line = derivative_line([load(i * SIDE + k) for k in range(SIDE)], False)
        seconds = []
        for j in range(SIDE):
            node = i * SIDE + j
            m0, m1, m2 = [metric_ref[node, c : c + 1, :] for c in range(3)]
            g1, g2 = first_ref[node], line[j]
            p1 = m0 * g1 + m2 * g2
            p2 = m2 * g1 + m1 * g2
            visit(node, g1, g2, p1, p2)
            seconds.append(p2)
        yield i, seconds


def apply_operator(inner_ref, cycle_ref, result_ref, first_ref, energy_ref, metric_ref, shift_ref):
    @pl.loop(0, 2)
    def half(part):
        rows = pl.ds(pl.multiple_of(part * 8, 8), 8)
        shift = shift_ref[rows, :]
        load = grid_load(inner_ref, cycle_ref, rows)

        def visit(node, g1, g2, p1, p2):
            first_ref[node] = p1

        for i, seconds in gradients(load, first_ref, metric_ref, visit):
            line = derivative_line(seconds, True)
            for j in range(SIDE):
                node = i * SIDE + j
                mass = shift * metric_ref[node, 3:4, :]
                result_ref[node, rows, :] = line[j] + mass * load(node)
        energy = jnp.zeros((8, LANES), F32)
        for j in range(SIDE):
            line = derivative_line([first_ref[k * SIDE + j] for k in range(SIDE)], True)
            for i in range(SIDE):
                node = i * SIDE + j
                value = result_ref[node, rows, :] + line[i]
                result_ref[node, rows, :] = value
                energy = energy + value * load(node)
        energy_ref[rows, :] = energy


def apply_energy(inner_ref, cycle_ref, first_ref, energy_ref, metric_ref, shift_ref):
    @pl.loop(0, 2)
    def half(part):
        rows = pl.ds(pl.multiple_of(part * 8, 8), 8)
        shift = shift_ref[rows, :]
        load = grid_load(inner_ref, cycle_ref, rows)
        sums = [jnp.zeros((8, LANES), F32)]

        def visit(node, g1, g2, p1, p2):
            value = load(node)
            mass = shift * metric_ref[node, 3:4, :]
            sums[0] = sums[0] + (g1 * p1 + g2 * p2 + mass * value * value)

        for i, seconds in gradients(load, first_ref, metric_ref, visit):
            pass
        energy_ref[rows, :] = sums[0]


def diagonal_cells(metric_ref, table_ref, cross_ref, penalty_ref, inner_ref, padded_ref, cells_ref):
    both = jnp.concatenate([metric_ref[:, 0, :], metric_ref[:, 1, :]], axis=0)
    terms = jnp.dot(table_ref[...], both, precision=HIGHEST, preferred_element_type=F32)
    cells_ref[0] = terms + cross_ref[...] * metric_ref[:, 2, :]
    cells_ref[1] = metric_ref[:, 3, :]
    padded_ref[...] = jnp.ones((HIGH, LOW), F32)
    for high in range(HIGH):
        count = min(LOW, SKEL - high * LOW)
        line = penalty_ref[pl.ds(high * LOW, count)]
        padded_ref[high : high + 1, :count] = line.reshape(1, count)
    for index, node in enumerate(INNER_NODES):
        inner_ref[0, index : index + 1, :] = cells_ref[0, node : node + 1, :]
        inner_ref[1, index : index + 1, :] = cells_ref[1, node : node + 1, :]


def diagonal_slots(total, shared_rows, selectors, padded_ref, skeleton_ref):
    stacked = []
    for high in range(HIGH):
        laplace, mass = two_rows(total, high)
        laplace = laplace + padded_ref[high : high + 1, :]
        skeleton_ref[0, high : high + 1, :] = laplace
        skeleton_ref[1, high : high + 1, :] = mass
        stacked.append(four_pieces(laplace, mass).astype(BF16))
    stacked = jnp.concatenate(stacked, axis=0)
    results = []
    for tile in range(SLOT_TILES):
        high_row = jnp.right_shift(shared_rows[tile : tile + 1, :], 8)
        found = jnp.dot(stacked, selectors[:, lane_block(tile)], preferred_element_type=F32)
        value = jnp.zeros((ROWS, LANES), F32)
        for high in range(HIGH):
            value = value + jnp.where(high_row == high, found[row_block(high), :], 0.0)
        results.append(two_rows(value, 0))
    return results


def pack_kernel(
    forcing_hbm, edge_hbm, shared_hbm, masks_hbm, metric_hbm, penalty_hbm, table_hbm, cross_hbm,
    out_hbm, message_hbm, inner_hbm, skeleton_hbm, padded_hbm, lists_hbm,
    forcing_ref, edge_ref, shared_ref, masks_ref, metric_ref, penalty_ref, table_ref, cross_ref,
    packed_ref, message_ref, inner_ref, skeleton_ref, padded_ref, lists_ref,
    cells_ref, left_ref, selectors_ref, in_semaphores, out_semaphores,
):
    ins = [
        pltpu.make_async_copy(source, target, in_semaphores.at[index])
        for index, (source, target) in enumerate(
            [
                (edge_hbm, edge_ref), (metric_hbm, metric_ref), (table_hbm, table_ref), (cross_hbm, cross_ref),
                (penalty_hbm, penalty_ref), (shared_hbm, shared_ref), (masks_hbm, masks_ref),
                (forcing_hbm, forcing_ref),
            ]
        )
    ]
    for copy in ins:
        copy.start()
    outs = []

    def send(source, target):
        copy = pltpu.make_async_copy(source, target, out_semaphores.at[len(outs)])
        copy.start()
        outs.append(copy)

    width = ORDER - 1
    base = 2 * HIGH * ROWS
    for index in range(TILES, MODES * BLOCK - INNER):
        packed_ref[index] = jnp.zeros((ROWS, LANES), F32)
    ins[0].wait()
    edge_rows = edge_ref[...]
    one_hot_cycle(edge_rows, selectors_ref)
    for copy in ins[1:7]:
        copy.wait()
    shared_rows = shared_ref[...]
    lists_ref[:SLOT_TILES, :] = shared_rows
    lists_ref[SLOT_TILES : 2 * SLOT_TILES, :] = masks_ref[...]
    lists_ref[2 * SLOT_TILES :, :] = jnp.zeros((8 - 2 * SLOT_TILES, LANES), jnp.int32)
    send(lists_ref, lists_hbm)
    diagonal_cells(metric_ref, table_ref, cross_ref, penalty_ref, inner_ref, padded_ref, cells_ref)
    send(inner_ref, inner_hbm)
    send(padded_ref, padded_hbm)
    ins[7].wait()
    for line in range(width):
        send(forcing_ref.at[pl.ds((line + 1) * SIDE + 1, width)], out_hbm.at[pl.ds(line * width, width)])
    high_rows = jnp.right_shift(edge_rows, 8)
    for slot in range(CYCLE):
        node = CYCLE_NODES[slot]
        high_row = high_rows[slot : slot + 1, :]
        masked_store(forcing_ref[node], high_row, left_ref, slot)
        value = four_pieces(cells_ref[0, node : node + 1, :], cells_ref[1, node : node + 1, :])
        masked_store_four(value, high_row, left_ref.at[pl.ds(base, HIGH * ROWS)], slot)
    total = contract_lanes(left_ref[...], selectors_ref[...])
    skeleton = total[: HIGH * ROWS] + total[HIGH * ROWS : base]

    def store(index, value):
        packed_ref[index] = value

    write_skeleton(skeleton, store)
    send(packed_ref, out_hbm.at[pl.ds(INNER, MODES * BLOCK - INNER)])
    selectors = slot_selectors(shared_rows)
    pairs = diagonal_slots(total[base:], shared_rows, selectors, padded_ref, skeleton_ref)
    send(skeleton_ref, skeleton_hbm)
    for tile, value in enumerate(gather_slots(skeleton, shared_rows)):
        laplace, mass = pairs[tile]
        message_ref[tile, :ROWS, :] = value
        message_ref[tile, ROWS:, :] = jnp.zeros((8, LANES), F32)
        message_ref[tile, ROWS : ROWS + 1, :] = laplace
        message_ref[tile, ROWS + 1 : ROWS + 2, :] = mass
    send(message_ref, message_hbm)
    for copy in outs:
        copy.wait()


def place(index):
    return pl.ds(pl.multiple_of(index * ROWS, ROWS), ROWS)


def relative_rows(matrix_ref, mode):
    parts = [matrix_ref[place(jnp.bitwise_xor(mode, step)), :] for step in range(MODES)]
    return jnp.concatenate(parts, axis=0)


def transform_kernel(
    matrix_ref, in_ref, a0, a2, a1, a3, a4, lists_ref, o0, o1, o2, o3, o4, o5, o6, o7, extra_ref, slots_ref
):
    mode = lax.axis_index("mode")
    outs = [o0, o1, o2, o3, o4, o5, o6, o7]
    matrix = relative_rows(matrix_ref, mode)
    slots_ref[...] = jnp.zeros(slots_ref.shape, F32)
    arrived_refs = [a0, a1, a2, a3, a4]
    masks = lists_ref[SLOT_TILES : 2 * SLOT_TILES, :]
    for index in range(BLOCK):
        block = in_ref[:, index].reshape(PLANES, LANES)
        mixed = jnp.dot(matrix, block, precision=HIGHEST, preferred_element_type=F32)
        for step, out_ref in enumerate(outs):
            out_ref[index] = mixed[row_block(step), :]
    for tile in range(SLOT_TILES):
        chosen = select_arrived(masks, tile, [ref[tile] for ref in arrived_refs])
        slots_ref[tile, place(mode), :] = chosen[:ROWS]
        mixed = jnp.dot(matrix, slots_ref[tile], precision=HIGHEST, preferred_element_type=F32)
        for step, out_ref in enumerate(outs):
            out_ref[BLOCK + tile] = mixed[row_block(step), :]
        extra_ref[tile] = chosen[ROWS:]


def first_kernel(
    i4, i5, i7, i2, i6, i3, i1, i0, extra_ref, lists_ref, edge_ref, metric_ref,
    inner_ref, diagonal_ref, penalty_ref, search_ref, inverse_ref, result_ref, source_ref, kept_ref, slots_ref,
    sums_ref, left_ref, right_ref, cycle_ref, first_ref, energy_ref, shift_ref,
):
    mode = lax.axis_index("mode")
    ins = [i0, i1, i2, i3, i4, i5, i6, i7]
    for step, in_ref in enumerate(ins):
        source_ref[jnp.bitwise_xor(mode, step)] = in_ref[:BLOCK]
    shared_rows = lists_ref[:SLOT_TILES, :]
    right_slots = slot_selectors(shared_rows)
    shift = helmholtz_shift()
    shift_ref[...] = shift
    edge_rows = edge_ref[...]

    def load_right(tile):
        total = ins[0][BLOCK + tile]
        for in_ref in ins[1:]:
            total = total + in_ref[BLOCK + tile]
        return total

    def source(index):
        block, row = sent_place(index)
        return source_ref[block, row]

    high_rows = jnp.right_shift(shared_rows, 8)
    for tile in range(SLOT_TILES):
        value = four_pieces(extra_ref[tile, 0:1, :], extra_ref[tile, 1:2, :])
        masked_store_four(value, high_rows[tile : tile + 1, :], left_ref, tile)
    added = contract_lanes(left_ref[: HIGH * ROWS, :SLOTS], right_slots)
    wide_shift = jnp.concatenate([shift, shift], axis=1)
    parts = []
    for high in range(HIGH):
        laplace, mass = two_rows(added, high)
        laplace = laplace + diagonal_ref[0, high : high + 1, :]
        mass = mass + diagonal_ref[1, high : high + 1, :]
        parts.append(1.0 / (laplace + wide_shift * mass))
    inverse = jnp.concatenate(parts, axis=0)
    local = read_skeleton(lambda index: source(INNER + index))
    right_side = local + scatter_slots(load_right, shared_rows, left_ref, right_slots)
    search = right_side * inverse
    kept_ref[0] = local
    kept_ref[1] = inverse
    kept_ref[2] = search
    start = skeleton_sum(local * search)
    for index, node in enumerate(INNER_NODES):
        value = source(index)
        inverted = 1.0 / (inner_ref[0, index : index + 1, :] + shift * inner_ref[1, index : index + 1, :])
        scaled = value * inverted
        search_ref[index] = scaled
        inverse_ref[index] = inverted
        start = start + value * scaled

    def store(slot, value):
        cycle_ref[slot] = value

    gather_cycle(search, edge_rows, store, right_ref)
    apply_operator(search_ref, cycle_ref, result_ref, first_ref, energy_ref, metric_ref, shift_ref)
    weighted = per_tile(penalty_ref) * search
    applied = weighted + scatter_cycle(
        lambda slot: result_ref[CYCLE_NODES[slot]], edge_rows, left_ref, right_ref
    )
    kept_ref[3] = applied
    for tile, value in enumerate(gather_slots(applied, shared_rows)):
        slots_ref[tile] = value
    sums_ref[0] = energy_ref[...] + skeleton_sum(weighted * search)
    sums_ref[1] = start


def change_kernel(search_ref, inverse_ref, result_ref, source_ref, moved_ref, sums_ref):
    crossed = jnp.zeros((ROWS, LANES), F32)
    sourced = jnp.zeros((ROWS, LANES), F32)
    for index, node in enumerate(INNER_NODES):
        value = result_ref[node]
        moved = value * inverse_ref[index] - search_ref[index]
        moved_ref[index] = moved
        crossed = crossed + value * moved
        sourced = sourced + source_ref[index // BLOCK, index % BLOCK] * moved
    sums_ref[0] = crossed
    sums_ref[1] = sourced


def second_kernel(
    moved_ref, kept_ref, sums_ref, moved_sums_ref, a0, a2, a1, a3, a4, lists_ref, edge_ref,
    metric_ref, penalty_ref, change_ref, message_ref, left_ref, cycle_ref, first_ref, energy_ref, shift_ref,
):
    arrived_refs = [a0, a1, a2, a3, a4]
    masks = lists_ref[SLOT_TILES : 2 * SLOT_TILES, :]
    shared_rows = lists_ref[:SLOT_TILES, :]
    shift_ref[...] = helmholtz_shift()

    def load(tile):
        return select_arrived(masks, tile, [ref[tile] for ref in arrived_refs])

    local, inverse, search, applied = [kept_ref[index] for index in range(4)]
    full = applied + scatter_slots(load, shared_rows, left_ref, slot_selectors(shared_rows))
    change = full * inverse - search
    change_ref[...] = change
    crossed = moved_sums_ref[0] + skeleton_sum(applied * change)
    sourced = moved_sums_ref[1] + skeleton_sum(local * change)

    def store(slot, value):
        cycle_ref[slot] = value

    gather_cycle(change, edge_ref[...], store)
    apply_energy(moved_ref, cycle_ref, first_ref, energy_ref, metric_ref, shift_ref)
    energy = energy_ref[...] + skeleton_sum(per_tile(penalty_ref) * change * change)
    sublanes = lax.broadcasted_iota(jnp.int32, (ROWS, LANES), 0)
    lanes = lax.broadcasted_iota(jnp.int32, (ROWS, LANES), 1)
    spread = jnp.zeros((ROWS, LANES), F32)
    for index, value in enumerate([sums_ref[0], crossed, energy, sums_ref[1], sourced]):
        column = jnp.sum(value, axis=1, keepdims=True)
        spread = jnp.where(lanes == sublanes + index * ROWS, column, spread)
    message = jnp.sum(spread, axis=0, keepdims=True)
    message_ref[...] = jnp.broadcast_to(message, message_ref.shape)


def scale_kernel(
    scalars_ref, inner_ref, moved_ref, kept_ref, change_ref, o0, o1, o2, o3, o4, o5, o6, o7, packed_ref
):
    sublanes = lax.broadcasted_iota(jnp.int32, (ROWS, LANES), 0)
    lanes = lax.broadcasted_iota(jnp.int32, (ROWS, LANES), 1)
    total = jnp.sum(scalars_ref[...], axis=0, keepdims=True)
    g00, g01, g11, h0, h1 = [
        jnp.sum(jnp.where(lanes == sublanes + index * ROWS, total, 0.0), axis=1, keepdims=True)
        for index in range(SCALARS)
    ]
    ratio = g01 / g00
    pivot = g11 - ratio * g01
    second = jnp.where(pivot > 0.0, (h1 - ratio * h0) / pivot, 0.0)
    first = jnp.broadcast_to(h0 / g00 - ratio * second, (ROWS, LANES))
    second = jnp.broadcast_to(second, (ROWS, LANES))
    store = write_place(packed_ref, sent_place)
    for index in range(INNER):
        store(index, first * inner_ref[index] + second * moved_ref[index])
    for high in range(HIGH):
        for part in range(2):
            place = (row_block(high), lane_block(part))
            value = first * kept_ref[(2,) + place] + second * change_ref[place]
            store(INNER + 2 * high + part, value)
    for index in range(INNER + TILES, MODES * BLOCK):
        store(index, jnp.zeros((ROWS, LANES), F32))
    mode = lax.axis_index("mode")
    for step, out_ref in enumerate([o0, o1, o2, o3, o4, o5, o6, o7]):
        out_ref[...] = packed_ref[jnp.bitwise_xor(mode, step)]


def combine_kernel(
    matrix_ref, i4, i5, i7, i2, i6, i3, i1, i0, o0, o1, o2, o3, o4, o5, o6, o7, block_ref
):
    mode = lax.axis_index("mode")
    for step, in_ref in enumerate([i0, i1, i2, i3, i4, i5, i6, i7]):
        block_ref[:, place(jnp.bitwise_xor(mode, step)), :] = in_ref[...]
    matrix = relative_rows(matrix_ref, mode)
    for index in range(BLOCK):
        mixed = jnp.dot(matrix, block_ref[index], precision=HIGHEST, preferred_element_type=F32)
        for step, out_ref in enumerate([o0, o1, o2, o3, o4, o5, o6, o7]):
            out_ref[index] = mixed[row_block(step), :]


def unpack_kernel(
    i4, i5, i7, i2, i6, i3, i1, i0, edge_ref, out_hbm, packed_ref, out_ref, semaphores
):
    mode = lax.axis_index("mode")
    for step, in_ref in enumerate([i0, i1, i2, i3, i4, i5, i6, i7]):
        packed_ref[jnp.bitwise_xor(mode, step)] = in_ref[...]

    def load(index):
        block, row = sent_place(index)
        return packed_ref[block, row]

    for index, node in enumerate(INNER_NODES):
        out_ref[node] = load(index)
    spans = [(SIDE, (SIDE - 2) * SIDE), (0, SIDE), (ORDER * SIDE, SIDE)]
    copies = [
        pltpu.make_async_copy(out_ref.at[pl.ds(*span)], out_hbm.at[pl.ds(*span)], semaphores.at[index])
        for index, span in enumerate(spans)
    ]

    def store(slot, value):
        out_ref[CYCLE_NODES[slot]] = value
        if slot == 2 * SIDE - 1:
            copies[0].start()
        if slot == CYCLE - 1:
            copies[1].start()
            copies[2].start()

    gather_cycle(read_skeleton(lambda index: load(INNER + index)), edge_ref[...], store)
    for copy in copies:
        copy.wait()


def call(kernel, out_shapes, scratch, *operands, limit=VMEM_LIMIT, **options):
    return pl.pallas_call(
        kernel,
        out_shape=out_shapes,
        scratch_shapes=scratch,
        compiler_params=pltpu.CompilerParams(vmem_limit_bytes=limit),
        **options,
    )(*operands)


def shape(*dims, dtype=F32):
    return jax.ShapeDtypeStruct(dims, dtype)


def swap_blocks(blocks, axis):
    return lax.all_to_all(blocks, axis, split_axis=0, concat_axis=0, tiled=True)


def permute(value, axis, flip):
    return lax.ppermute(value, axis, [(i, i ^ flip) for i in range(lax.axis_size(axis))])


def swap_steps(blocks):
    return [permute(blocks[step], "mode", step) for step in STEP_ORDER] + [blocks[0]]


def exchange(slots):
    return [permute(slots, "elem", 1 << level) for level in LEVEL_ORDER]


def body(forcing, metric, edge_map, shared_rows, partner_masks, penalty):
    forward, backward = [jnp.asarray(part) for part in fourier_tables()]
    table, cross = [jnp.asarray(part) for part in diagonal_tables()]
    metric = metric.transpose(1, 0, 2)
    edge_rows = edge_map.T
    shared = shared_rows.reshape(SLOT_TILES, LANES)
    masks = partner_masks.reshape(SLOT_TILES, LANES)
    left = pltpu.VMEM((2 * HIGH * ROWS, CYCLE * LANES), BF16)
    right = pltpu.VMEM((LOW, CYCLE * LANES), BF16)
    left_slots = pltpu.VMEM((2 * HIGH * ROWS, SLOTS), BF16)
    cycle = pltpu.VMEM((CYCLE, ROWS, LANES), F32)
    first = pltpu.VMEM((NODES, 8, LANES), F32)
    energy = pltpu.VMEM((ROWS, LANES), F32)
    packing = pltpu.VMEM((MODES, BLOCK, ROWS, LANES), F32)
    wide = (HIGH * ROWS, LOW)
    blocks = [shape(BLOCK, ROWS, LANES)] * MODES

    hbm = pl.BlockSpec(memory_space=pltpu.HBM)
    packed_shapes = [
        shape(MODES * BLOCK, ROWS, LANES), shape(SLOT_TILES, ROWS + 8, LANES),
        shape(2, INNER, LANES), shape(2, HIGH, LOW), shape(HIGH, LOW), shape(8, LANES, dtype=jnp.int32),
    ]
    operands = [forcing.transpose(1, 0, 2), edge_rows, shared, masks, metric, penalty, table, cross]
    packed, message, inner, diagonal, penalties, lists = call(
        pack_kernel, packed_shapes,
        [pltpu.VMEM(operand.shape, operand.dtype) for operand in operands]
        + [pltpu.VMEM((MODES * BLOCK - INNER, ROWS, LANES), F32)]
        + [pltpu.VMEM(part.shape, part.dtype) for part in packed_shapes[1:]]
        + [
            pltpu.VMEM((2, NODES, LANES), F32), pltpu.VMEM((3 * HIGH * ROWS, CYCLE * LANES), BF16), right,
            pltpu.SemaphoreType.DMA((len(operands),)), pltpu.SemaphoreType.DMA((ORDER + 5,)),
        ],
        *operands,
        in_specs=[hbm] * len(operands), out_specs=[hbm] * len(packed_shapes), limit=FIRST_LIMIT,
    )
    gathered = swap_blocks(packed.reshape(MODES, BLOCK, ROWS, LANES), "mode")
    *mixed, extra = call(
        transform_kernel, [shape(SHARE, ROWS, LANES)] * MODES + [shape(SLOT_TILES, 8, LANES)],
        [pltpu.VMEM((SLOT_TILES, PLANES, LANES), F32)], forward, gathered, *exchange(message), lists,
    )
    inside = shape(INNER, ROWS, LANES)
    search, inverse, applied, source, kept, slots, sums = call(
        first_kernel,
        [
            inside, inside, shape(NODES, ROWS, LANES), shape(MODES, BLOCK, ROWS, LANES), shape(4, *wide),
            shape(SLOT_TILES, ROWS, LANES), shape(2, ROWS, LANES),
        ],
        [left, right, cycle, first, energy, energy],
        *swap_steps(mixed), extra, lists, edge_rows, metric, inner, diagonal, penalties,
    )
    moved, moved_sums = call(
        change_kernel, [inside, shape(2, ROWS, LANES)], [], search, inverse, applied, source
    )
    change, message = call(
        second_kernel,
        [shape(*wide), shape(ELEMS_AXIS, LANES)],
        [left_slots, cycle, first, energy, energy],
        moved, kept, sums, moved_sums, *exchange(slots), lists, edge_rows, metric, penalties,
    )
    scalars = swap_blocks(message, "elem")
    scaled = call(scale_kernel, blocks, [packing], scalars, search, moved, kept, change)
    mixed = call(
        combine_kernel, blocks, [pltpu.VMEM((BLOCK, PLANES, LANES), F32)], backward, *swap_steps(scaled)
    )
    result = call(
        unpack_kernel, shape(NODES, ROWS, LANES),
        [packing, pltpu.VMEM((NODES, ROWS, LANES), F32), pltpu.SemaphoreType.DMA((3,))],
        *swap_steps(mixed), edge_rows, out_specs=hbm,
    )
    return result.transpose(1, 0, 2)


def solution(mesh):
    placed = (
        P("mode", None, "elem"),
        P(None, None, "elem"),
        P("elem", None),
        P("elem"),
        P("elem"),
        P("elem"),
    )
    return jax.shard_map(
        body, mesh=mesh, in_specs=placed, out_specs=P("mode", None, "elem"), check_vma=False
    )
```

```python
import functools
import math

import jax
import jax.numpy as jnp
import numpy as np
from jax import lax
from jax.experimental import pallas as pl
from jax.experimental.pallas import tpu as pltpu
from jax.sharding import PartitionSpec as P

ORDER = 8
SIDE = ORDER + 1
NODES = SIDE * SIDE
CYCLE = 32
INNER = (ORDER - 1) ** 2
ROWS = 16
LANES = 128
PLANES = 128
MODES = 8
ELEMS_AXIS = 32
SKEL = 2113
LOW = 256
HIGH = 9
TILES = 2 * HIGH
QUADS = -(-HIGH // 4)
SLOTS = 384
SLOT_TILES = SLOTS // LANES
BLOCK = 9
SHARE = BLOCK + SLOT_TILES
SCALARS = 5
STEP_ORDER = [4, 5, 7, 2, 6, 3, 1]
LEVEL_ORDER = [0, 2, 1, 3, 4]
SPACING = 0.25
F32 = jnp.float32
BF16 = jnp.bfloat16
HIGHEST = lax.Precision.HIGHEST
VMEM_LIMIT = 32 * 1024 * 1024
FIRST_LIMIT = 56 * 1024 * 1024


def legendre_table(points, poly_order):
    table = np.zeros((points.shape[0], poly_order + 1))
    table[:, 0] = 1.0
    table[:, 1] = points
    for degree in range(2, poly_order + 1):
        table[:, degree] = (
            (2 * degree - 1) * points * table[:, degree - 1] - (degree - 1) * table[:, degree - 2]
        ) / degree
    return table


def lobatto_derivative(poly_order):
    node_count = poly_order + 1
    points = np.cos(np.pi * np.arange(node_count) / poly_order)
    for newton_step in range(100):
        table = legendre_table(points, poly_order)
        points = points - (points * table[:, poly_order] - table[:, poly_order - 1]) / (
            node_count * table[:, poly_order]
        )
    points = np.sort(points)
    top_values = legendre_table(points, poly_order)[:, poly_order]
    identity = np.eye(node_count)
    differ = points[:, None] - points[None, :] + identity
    matrix = top_values[:, None] / (top_values[None, :] * differ)
    matrix = matrix * (1.0 - identity)
    matrix[0, 0] = -poly_order * node_count / 4.0
    matrix[poly_order, poly_order] = poly_order * node_count / 4.0
    return matrix


def fourier_tables():
    positions = np.arange(PLANES)
    phases = ((positions // 2)[:, None] * positions[None, :] % PLANES) * (2.0 * np.pi / PLANES)
    cosine, sine = np.cos(phases), np.sin(phases)
    even = (positions % 2 == 0)[:, None]
    nyquist = (positions == 1)[:, None]
    alternate = (1.0 - 2.0 * (positions % 2))[None, :]
    forward = np.where(nyquist, alternate, np.where(even, cosine, -sine)) / PLANES
    backward = np.where(nyquist, alternate, np.where(even, 2.0 * cosine, -2.0 * sine))
    backward = np.where((positions == 0)[:, None], 1.0, backward)
    return forward.astype(np.float32), backward.T.astype(np.float32)


DERIVATIVE64 = lobatto_derivative(ORDER)
DERIVATIVE = DERIVATIVE64.astype(np.float32)
CYCLE_NODES = (
    [i * SIDE for i in range(SIDE)]
    + [i * SIDE + ORDER for i in range(SIDE)]
    + [j for j in range(1, ORDER)]
    + [ORDER * SIDE + j for j in range(1, ORDER)]
)
INNER_NODES = [i * SIDE + j for i in range(1, ORDER) for j in range(1, ORDER)]


def diagonal_tables():
    squared = (DERIVATIVE * DERIVATIVE).astype(np.float64)
    first = np.kron(squared.T, np.eye(SIDE))
    second = np.kron(np.eye(SIDE), squared.T)
    corner = np.diagonal(DERIVATIVE)
    cross = 2.0 * np.outer(corner, corner).reshape(NODES, 1)
    cross = np.broadcast_to(cross, (NODES, LANES))
    return np.concatenate([first, second], axis=1).astype(np.float32), cross.astype(np.float32)


def helmholtz_shift():
    rows_global = lax.axis_index("mode") * ROWS + lax.broadcasted_iota(jnp.int32, (ROWS, LANES), 0)
    wavenumber = jnp.right_shift(rows_global, 1).astype(F32)
    spanwise = wavenumber * (2.0 * math.pi / (PLANES * SPACING))
    spanwise = jnp.where(rows_global == 1, math.pi / SPACING, spanwise)
    return spanwise * spanwise


def row_block(index):
    return slice(index * ROWS, (index + 1) * ROWS)


def lane_block(index):
    return slice(index * LANES, (index + 1) * LANES)


def pieces(value):
    top = value.astype(BF16).astype(F32)
    return top, value - top


def one_hot_rows(low_rows):
    sublanes = lax.broadcasted_iota(jnp.int32, (LOW, low_rows.shape[1]), 0).astype(BF16)
    wanted = jnp.broadcast_to(low_rows.astype(BF16), sublanes.shape)
    return jnp.where(wanted == sublanes, BF16(1.0), BF16(0.0))


def masked_store(value, high_row, left_ref, column):
    top, rest = [part.astype(BF16) for part in pieces(value)]
    wanted = jnp.broadcast_to(high_row.astype(BF16), value.shape)
    for high in range(HIGH):
        here = wanted == BF16(high)
        left_ref[row_block(high), lane_block(column)] = jnp.where(here, top, BF16(0.0))
        left_ref[row_block(HIGH + high), lane_block(column)] = jnp.where(here, rest, BF16(0.0))


def contract_lanes(left, right):
    return lax.dot_general(left, right, (((1,), (1,)), ((), ())), preferred_element_type=F32)


def scatter_sum(left, selectors):
    both = contract_lanes(left, selectors)
    return both[: HIGH * ROWS] + both[HIGH * ROWS :]


def one_hot_cycle(edge_rows, selectors_ref):
    low = jnp.bitwise_and(edge_rows, LOW - 1)
    for slot in range(CYCLE):
        selectors_ref[:, lane_block(slot)] = one_hot_rows(low[slot : slot + 1, :])


def scatter_cycle(load, edge_rows, left_ref, selectors_ref):
    high_rows = jnp.right_shift(edge_rows, 8)
    for slot in range(CYCLE):
        masked_store(load(slot), high_rows[slot : slot + 1, :], left_ref, slot)
    return scatter_sum(left_ref[...], selectors_ref[...])


def slot_selectors(shared_rows):
    low = jnp.bitwise_and(shared_rows, LOW - 1)
    return jnp.concatenate(
        [one_hot_rows(low[tile : tile + 1, :]) for tile in range(SLOT_TILES)], axis=1
    )


def four_pieces(first, second):
    sublanes = jnp.bitwise_and(lax.broadcasted_iota(jnp.int32, (ROWS, first.shape[1]), 0), 3)
    first_top, first_rest = pieces(first)
    second_top, second_rest = pieces(second)
    tops = jnp.where(sublanes == 0, first_top, second_top)
    rests = jnp.where(sublanes == 2, first_rest, second_rest)
    return jnp.where(sublanes < 2, tops, rests)


def masked_store_four(value, high_row, left_ref, column):
    packed = value.astype(BF16)
    quarter = jnp.right_shift(lax.broadcasted_iota(jnp.int32, value.shape, 0), 2).astype(BF16)
    wanted = jnp.broadcast_to(high_row.astype(BF16), value.shape) - quarter
    for block in range(QUADS):
        here = wanted == BF16(4 * block)
        left_ref[row_block(block), lane_block(column)] = jnp.where(here, packed, BF16(0.0))


def two_rows(total, high):
    base = 4 * high
    first = total[base : base + 1, :] + total[base + 2 : base + 3, :]
    second = total[base + 1 : base + 2, :] + total[base + 3 : base + 4, :]
    return first, second


def scatter_slots(load, shared_rows, left_ref, right):
    high_rows = jnp.right_shift(shared_rows, 8)
    for tile in range(SLOT_TILES):
        masked_store(load(tile), high_rows[tile : tile + 1, :], left_ref, tile)
    return scatter_sum(left_ref[:, :SLOTS], right)


def stack_pieces(skeleton):
    top, rest = pieces(skeleton)
    return jnp.concatenate([top.astype(BF16), rest.astype(BF16)], axis=0)


def gather_tile(stacked, rows, keep=None):
    low = jnp.bitwise_and(rows, LOW - 1)
    high = jnp.right_shift(rows, 8)
    selector = one_hot_rows(low)
    if keep is not None:
        keep(selector)
    found = jnp.dot(stacked, selector, preferred_element_type=F32)
    total = None
    for index in range(HIGH):
        part = found[row_block(index), :] + found[row_block(HIGH + index), :]
        part = jnp.where(high == index, part, 0.0)
        total = part if total is None else total + part
    return total


def keep_columns(selectors_ref, column, selector):
    selectors_ref[:, column * LANES : (column + 2) * LANES] = selector


def gather_cycle(skeleton, edge_rows, store, selectors_ref=None):
    stacked = stack_pieces(skeleton)
    for pair in range(CYCLE // 2):
        rows = jnp.concatenate(
            [edge_rows[2 * pair : 2 * pair + 1, :], edge_rows[2 * pair + 1 : 2 * pair + 2, :]], axis=1
        )
        keep = None
        if selectors_ref is not None:
            keep = functools.partial(keep_columns, selectors_ref, 2 * pair)
        total = gather_tile(stacked, rows, keep)
        store(2 * pair, total[:, :LANES])
        store(2 * pair + 1, total[:, LANES:])


def gather_slots(skeleton, shared_rows):
    stacked = stack_pieces(skeleton)
    return [gather_tile(stacked, shared_rows[tile : tile + 1, :]) for tile in range(SLOT_TILES)]


def sent_place(index):
    return index // BLOCK, index % BLOCK


def read_skeleton(load):
    return jnp.concatenate(
        [jnp.concatenate([load(2 * high), load(2 * high + 1)], axis=1) for high in range(HIGH)], axis=0
    )


def write_skeleton(skeleton, store):
    for high in range(HIGH):
        store(2 * high, skeleton[row_block(high), :LANES])
        store(2 * high + 1, skeleton[row_block(high), LANES:])


def write_place(ref, place):
    def store(index, value):
        block, row = place(index)
        ref[block, row] = value

    return store


def fold(value):
    return value[:, :LANES] + value[:, LANES:]


def per_tile(penalty_ref):
    return jnp.concatenate(
        [jnp.broadcast_to(penalty_ref[high : high + 1, :], (ROWS, LOW)) for high in range(HIGH)], axis=0
    )


def skeleton_sum(product):
    total = None
    for high in range(HIGH):
        part = fold(product[row_block(high), :])
        total = part if total is None else total + part
    return total


def select_arrived(masks, tile, arrived):
    chosen = arrived[0]
    row = masks[tile : tile + 1, :]
    for level in range(1, len(arrived)):
        moving = jnp.bitwise_and(jnp.right_shift(row, level), 1) == 1
        chosen = jnp.where(moving, arrived[level], chosen)
    return chosen


def weighted_sum(weights, values):
    total = None
    for weight, value in zip(weights, values):
        if weight == 0.0:
            continue
        part = float(weight) * value
        total = part if total is None else total + part
    return total


def derivative_line(values, transposed):
    matrix = DERIVATIVE64.T if transposed else DERIVATIVE64
    half = SIDE // 2
    evens = [values[k] + values[ORDER - k] for k in range(half)] + [values[half]]
    odds = [values[k] - values[ORDER - k] for k in range(half)]
    results = [None] * SIDE
    for out in range(half):
        near, far = matrix[out, :half], matrix[out, :half:-1]
        even = weighted_sum(np.float32(np.append(0.5 * (near + far), matrix[out, half])), evens)
        odd = weighted_sum(np.float32(0.5 * (near - far)), odds)
        results[out] = odd + even
        results[ORDER - out] = odd - even
    results[half] = weighted_sum(np.float32(matrix[half, :half]), odds)
    return results


def grid_load(inner_ref, cycle_ref, rows):
    def load(node):
        if node in CYCLE_NODES:
            return cycle_ref[CYCLE_NODES.index(node), rows, :]
        return inner_ref[INNER_NODES.index(node), rows, :]

    return load


def gradients(load, first_ref, metric_ref, visit):
    for j in range(SIDE):
        line = derivative_line([load(k * SIDE + j) for k in range(SIDE)], False)
        for i in range(SIDE):
            first_ref[i * SIDE + j] = line[i]
    for i in range(SIDE):
        line = derivative_line([load(i * SIDE + k) for k in range(SIDE)], False)
        seconds = []
        for j in range(SIDE):
            node = i * SIDE + j
            m0, m1, m2 = [metric_ref[node, c : c + 1, :] for c in range(3)]
            g1, g2 = first_ref[node], line[j]
            p1 = m0 * g1 + m2 * g2
            p2 = m2 * g1 + m1 * g2
            visit(node, g1, g2, p1, p2)
            seconds.append(p2)
        yield i, seconds


def apply_operator(inner_ref, cycle_ref, result_ref, first_ref, energy_ref, metric_ref, shift_ref):
    @pl.loop(0, 2)
    def half(part):
        rows = pl.ds(pl.multiple_of(part * 8, 8), 8)
        shift = shift_ref[rows, :]
        load = grid_load(inner_ref, cycle_ref, rows)

        def visit(node, g1, g2, p1, p2):
            first_ref[node] = p1

        for i, seconds in gradients(load, first_ref, metric_ref, visit):
            line = derivative_line(seconds, True)
            for j in range(SIDE):
                node = i * SIDE + j
                mass = shift * metric_ref[node, 3:4, :]
                result_ref[node, rows, :] = line[j] + mass * load(node)
        energy = jnp.zeros((8, LANES), F32)
        for j in range(SIDE):
            line = derivative_line([first_ref[k * SIDE + j] for k in range(SIDE)], True)
            for i in range(SIDE):
                node = i * SIDE + j
                value = result_ref[node, rows, :] + line[i]
                result_ref[node, rows, :] = value
                energy = energy + value * load(node)
        energy_ref[rows, :] = energy


def apply_energy(inner_ref, cycle_ref, first_ref, energy_ref, metric_ref, shift_ref):
    @pl.loop(0, 2)
    def half(part):
        rows = pl.ds(pl.multiple_of(part * 8, 8), 8)
        shift = shift_ref[rows, :]
        load = grid_load(inner_ref, cycle_ref, rows)
        sums = [jnp.zeros((8, LANES), F32)]

        def visit(node, g1, g2, p1, p2):
            value = load(node)
            mass = shift * metric_ref[node, 3:4, :]
            sums[0] = sums[0] + (g1 * p1 + g2 * p2 + mass * value * value)

        for i, seconds in gradients(load, first_ref, metric_ref, visit):
            pass
        energy_ref[rows, :] = sums[0]


def diagonal_cells(metric_ref, table_ref, cross_ref, penalty_ref, inner_ref, padded_ref, cells_ref):
    both = jnp.concatenate([metric_ref[:, 0, :], metric_ref[:, 1, :]], axis=0)
    terms = jnp.dot(table_ref[...], both, precision=HIGHEST, preferred_element_type=F32)
    cells_ref[0] = terms + cross_ref[...] * metric_ref[:, 2, :]
    cells_ref[1] = metric_ref[:, 3, :]
    padded_ref[...] = jnp.ones((HIGH, LOW), F32)
    for high in range(HIGH):
        count = min(LOW, SKEL - high * LOW)
        line = penalty_ref[pl.ds(high * LOW, count)]
        padded_ref[high : high + 1, :count] = line.reshape(1, count)
    for index, node in enumerate(INNER_NODES):
        inner_ref[0, index : index + 1, :] = cells_ref[0, node : node + 1, :]
        inner_ref[1, index : index + 1, :] = cells_ref[1, node : node + 1, :]


def diagonal_slots(total, shared_rows, selectors, padded_ref, skeleton_ref):
    stacked = []
    for high in range(HIGH):
        laplace, mass = two_rows(total, high)
        laplace = laplace + padded_ref[high : high + 1, :]
        skeleton_ref[0, high : high + 1, :] = laplace
        skeleton_ref[1, high : high + 1, :] = mass
        stacked.append(four_pieces(laplace, mass).astype(BF16))
    stacked = jnp.concatenate(stacked, axis=0)
    results = []
    for tile in range(SLOT_TILES):
        high_row = jnp.right_shift(shared_rows[tile : tile + 1, :], 8)
        found = jnp.dot(stacked, selectors[:, lane_block(tile)], preferred_element_type=F32)
        value = jnp.zeros((ROWS, LANES), F32)
        for high in range(HIGH):
            value = value + jnp.where(high_row == high, found[row_block(high), :], 0.0)
        results.append(two_rows(value, 0))
    return results


def pack_kernel(
    forcing_hbm, edge_hbm, shared_hbm, masks_hbm, metric_hbm, penalty_hbm, table_hbm, cross_hbm,
    out_hbm, message_hbm, inner_hbm, skeleton_hbm, padded_hbm, lists_hbm,
    forcing_ref, edge_ref, shared_ref, masks_ref, metric_ref, penalty_ref, table_ref, cross_ref,
    packed_ref, message_ref, inner_ref, skeleton_ref, padded_ref, lists_ref,
    cells_ref, left_ref, selectors_ref, in_semaphores, out_semaphores,
):
    ins = [
        pltpu.make_async_copy(source, target, in_semaphores.at[index])
        for index, (source, target) in enumerate(
            [
                (edge_hbm, edge_ref), (metric_hbm, metric_ref), (table_hbm, table_ref), (cross_hbm, cross_ref),
                (penalty_hbm, penalty_ref), (shared_hbm, shared_ref), (masks_hbm, masks_ref),
                (forcing_hbm, forcing_ref),
            ]
        )
    ]
    for copy in ins:
        copy.start()
    outs = []

    def send(source, target):
        copy = pltpu.make_async_copy(source, target, out_semaphores.at[len(outs)])
        copy.start()
        outs.append(copy)

    width = ORDER - 1
    base = 2 * HIGH * ROWS
    for index in range(TILES, MODES * BLOCK - INNER):
        packed_ref[index] = jnp.zeros((ROWS, LANES), F32)
    ins[0].wait()
    edge_rows = edge_ref[...]
    one_hot_cycle(edge_rows, selectors_ref)
    for copy in ins[1:7]:
        copy.wait()
    shared_rows = shared_ref[...]
    lists_ref[:SLOT_TILES, :] = shared_rows
    lists_ref[SLOT_TILES : 2 * SLOT_TILES, :] = masks_ref[...]
    lists_ref[2 * SLOT_TILES :, :] = jnp.zeros((8 - 2 * SLOT_TILES, LANES), jnp.int32)
    send(lists_ref, lists_hbm)
    diagonal_cells(metric_ref, table_ref, cross_ref, penalty_ref, inner_ref, padded_ref, cells_ref)
    send(inner_ref, inner_hbm)
    send(padded_ref, padded_hbm)
    ins[7].wait()
    for line in range(width):
        send(forcing_ref.at[pl.ds((line + 1) * SIDE + 1, width)], out_hbm.at[pl.ds(line * width, width)])
    high_rows = jnp.right_shift(edge_rows, 8)
    for slot in range(CYCLE):
        node = CYCLE_NODES[slot]
        high_row = high_rows[slot : slot + 1, :]
        masked_store(forcing_ref[node], high_row, left_ref, slot)
        value = four_pieces(cells_ref[0, node : node + 1, :], cells_ref[1, node : node + 1, :])
        masked_store_four(value, high_row, left_ref.at[pl.ds(base, QUADS * ROWS)], slot)
    total = contract_lanes(left_ref[...], selectors_ref[...])
    skeleton = total[: HIGH * ROWS] + total[HIGH * ROWS : base]

    def store(index, value):
        packed_ref[index] = value

    write_skeleton(skeleton, store)
    send(packed_ref, out_hbm.at[pl.ds(INNER, MODES * BLOCK - INNER)])
    selectors = slot_selectors(shared_rows)
    pairs = diagonal_slots(total[base:], shared_rows, selectors, padded_ref, skeleton_ref)
    send(skeleton_ref, skeleton_hbm)
    for tile, value in enumerate(gather_slots(skeleton, shared_rows)):
        laplace, mass = pairs[tile]
        message_ref[tile, :ROWS, :] = value
        message_ref[tile, ROWS:, :] = jnp.zeros((8, LANES), F32)
        message_ref[tile, ROWS : ROWS + 1, :] = laplace
        message_ref[tile, ROWS + 1 : ROWS + 2, :] = mass
    send(message_ref, message_hbm)
    for copy in outs:
        copy.wait()


def place(index):
    return pl.ds(pl.multiple_of(index * ROWS, ROWS), ROWS)


def relative_rows(matrix_ref, mode):
    parts = [matrix_ref[place(jnp.bitwise_xor(mode, step)), :] for step in range(MODES)]
    return jnp.concatenate(parts, axis=0)


def transform_kernel(
    matrix_ref, in_ref, a0, a2, a1, a3, a4, lists_ref, o0, o1, o2, o3, o4, o5, o6, o7, extra_ref, slots_ref
):
    mode = lax.axis_index("mode")
    outs = [o0, o1, o2, o3, o4, o5, o6, o7]
    matrix = relative_rows(matrix_ref, mode)
    slots_ref[...] = jnp.zeros(slots_ref.shape, F32)
    arrived_refs = [a0, a1, a2, a3, a4]
    masks = lists_ref[SLOT_TILES : 2 * SLOT_TILES, :]
    for index in range(BLOCK):
        block = in_ref[:, index].reshape(PLANES, LANES)
        mixed = jnp.dot(matrix, block, precision=HIGHEST, preferred_element_type=F32)
        for step, out_ref in enumerate(outs):
            out_ref[index] = mixed[row_block(step), :]
    for tile in range(SLOT_TILES):
        chosen = select_arrived(masks, tile, [ref[tile] for ref in arrived_refs])
        slots_ref[tile, place(mode), :] = chosen[:ROWS]
        mixed = jnp.dot(matrix, slots_ref[tile], precision=HIGHEST, preferred_element_type=F32)
        for step, out_ref in enumerate(outs):
            out_ref[BLOCK + tile] = mixed[row_block(step), :]
        extra_ref[tile] = chosen[ROWS:]


def first_kernel(
    i4, i5, i7, i2, i6, i3, i1, i0, extra_ref, lists_ref, edge_ref, metric_ref,
    inner_ref, diagonal_ref, penalty_ref, search_ref, inverse_ref, result_ref, source_ref, kept_ref, slots_ref,
    sums_ref, left_ref, right_ref, cycle_ref, first_ref, energy_ref, shift_ref,
):
    mode = lax.axis_index("mode")
    ins = [i0, i1, i2, i3, i4, i5, i6, i7]
    for step, in_ref in enumerate(ins):
        source_ref[jnp.bitwise_xor(mode, step)] = in_ref[:BLOCK]
    shared_rows = lists_ref[:SLOT_TILES, :]
    right_slots = slot_selectors(shared_rows)
    shift = helmholtz_shift()
    shift_ref[...] = shift
    edge_rows = edge_ref[...]

    def load_right(tile):
        total = ins[0][BLOCK + tile]
        for in_ref in ins[1:]:
            total = total + in_ref[BLOCK + tile]
        return total

    def source(index):
        block, row = sent_place(index)
        return source_ref[block, row]

    high_rows = jnp.right_shift(shared_rows, 8)
    for tile in range(SLOT_TILES):
        value = four_pieces(extra_ref[tile, 0:1, :], extra_ref[tile, 1:2, :])
        masked_store_four(value, high_rows[tile : tile + 1, :], left_ref, tile)
    added = contract_lanes(left_ref[: QUADS * ROWS, :SLOTS], right_slots)
    wide_shift = jnp.concatenate([shift, shift], axis=1)
    parts = []
    for high in range(HIGH):
        laplace, mass = two_rows(added, high)
        laplace = laplace + diagonal_ref[0, high : high + 1, :]
        mass = mass + diagonal_ref[1, high : high + 1, :]
        parts.append(1.0 / (laplace + wide_shift * mass))
    inverse = jnp.concatenate(parts, axis=0)
    local = read_skeleton(lambda index: source(INNER + index))
    right_side = local + scatter_slots(load_right, shared_rows, left_ref, right_slots)
    search = right_side * inverse
    kept_ref[0] = local
    kept_ref[1] = inverse
    kept_ref[2] = search
    start = skeleton_sum(local * search)
    for index, node in enumerate(INNER_NODES):
        value = source(index)
        inverted = 1.0 / (inner_ref[0, index : index + 1, :] + shift * inner_ref[1, index : index + 1, :])
        scaled = value * inverted
        search_ref[index] = scaled
        inverse_ref[index] = inverted
        start = start + value * scaled

    def store(slot, value):
        cycle_ref[slot] = value

    gather_cycle(search, edge_rows, store, right_ref)
    apply_operator(search_ref, cycle_ref, result_ref, first_ref, energy_ref, metric_ref, shift_ref)
    weighted = per_tile(penalty_ref) * search
    applied = weighted + scatter_cycle(
        lambda slot: result_ref[CYCLE_NODES[slot]], edge_rows, left_ref, right_ref
    )
    kept_ref[3] = applied
    for tile, value in enumerate(gather_slots(applied, shared_rows)):
        slots_ref[tile] = value
    sums_ref[0] = energy_ref[...] + skeleton_sum(weighted * search)
    sums_ref[1] = start


def change_kernel(search_ref, inverse_ref, result_ref, source_ref, kept_ref, moved_ref, sums_ref, both_ref):
    crossed = jnp.zeros((ROWS, LANES), F32)
    sourced = jnp.zeros((ROWS, LANES), F32)
    for index, node in enumerate(INNER_NODES):
        block, row = sent_place(index)
        value = result_ref[node]
        search = search_ref[index]
        moved = value * inverse_ref[index] - search
        moved_ref[index] = moved
        both_ref[block, row] = search
        both_ref[block, BLOCK + row] = moved
        crossed = crossed + value * moved
        sourced = sourced + source_ref[block, row] * moved
    for high in range(HIGH):
        for part in range(2):
            block, row = sent_place(INNER + 2 * high + part)
            both_ref[block, row] = kept_ref[2, row_block(high), lane_block(part)]
    for index in range(INNER + TILES, MODES * BLOCK):
        block, row = sent_place(index)
        both_ref[block, row] = jnp.zeros((ROWS, LANES), F32)
        both_ref[block, BLOCK + row] = jnp.zeros((ROWS, LANES), F32)
    sums_ref[0] = crossed
    sums_ref[1] = sourced


def second_kernel(
    kept_ref, moved_sums_ref, filled_ref, a0, a2, a1, a3, a4, lists_ref,
    change_ref, sums_ref, both_ref, o0, o1, o2, o3, o4, o5, o6, o7, left_ref,
):
    arrived_refs = [a0, a1, a2, a3, a4]
    masks = lists_ref[SLOT_TILES : 2 * SLOT_TILES, :]
    shared_rows = lists_ref[:SLOT_TILES, :]

    def load(tile):
        return select_arrived(masks, tile, [ref[tile] for ref in arrived_refs])

    local, inverse, search, applied = [kept_ref[index] for index in range(4)]
    full = applied + scatter_slots(load, shared_rows, left_ref, slot_selectors(shared_rows))
    change = full * inverse - search
    for high in range(HIGH):
        for part in range(2):
            block, row = sent_place(INNER + 2 * high + part)
            both_ref[block, BLOCK + row] = change[row_block(high), lane_block(part)]
    mode = lax.axis_index("mode")
    for step, out_ref in enumerate([o0, o1, o2, o3, o4, o5, o6, o7]):
        out_ref[...] = both_ref[jnp.bitwise_xor(mode, step)]
    change_ref[...] = change
    sums_ref[0] = moved_sums_ref[0] + skeleton_sum(applied * change)
    sums_ref[1] = moved_sums_ref[1] + skeleton_sum(local * change)


def energy_kernel(
    moved_ref, change_ref, sums_ref, changed_sums_ref, edge_ref, metric_ref, penalty_ref, message_ref,
    cycle_ref, first_ref, energy_ref, shift_ref,
):
    shift_ref[...] = helmholtz_shift()
    change = change_ref[...]

    def store(slot, value):
        cycle_ref[slot] = value

    gather_cycle(change, edge_ref[...], store)
    apply_energy(moved_ref, cycle_ref, first_ref, energy_ref, metric_ref, shift_ref)
    energy = energy_ref[...] + skeleton_sum(per_tile(penalty_ref) * change * change)
    sublanes = lax.broadcasted_iota(jnp.int32, (ROWS, LANES), 0)
    lanes = lax.broadcasted_iota(jnp.int32, (ROWS, LANES), 1)
    spread = jnp.zeros((ROWS, LANES), F32)
    for index, value in enumerate([sums_ref[0], changed_sums_ref[0], energy, sums_ref[1], changed_sums_ref[1]]):
        column = jnp.sum(value, axis=1, keepdims=True)
        spread = jnp.where(lanes == sublanes + index * ROWS, column, spread)
    message = jnp.sum(spread, axis=0, keepdims=True)
    message_ref[...] = jnp.broadcast_to(message, message_ref.shape)


def combine_kernel(
    matrix_ref, scalars_ref, i4, i5, i7, i2, i6, i3, i1, i0, o0, o1, o2, o3, o4, o5, o6, o7, block_ref
):
    mode = lax.axis_index("mode")
    sublanes = lax.broadcasted_iota(jnp.int32, (ROWS, LANES), 0)
    lanes = lax.broadcasted_iota(jnp.int32, (ROWS, LANES), 1)
    for step, in_ref in enumerate([i0, i1, i2, i3, i4, i5, i6, i7]):
        origin = jnp.bitwise_xor(mode, step)
        total = jnp.sum(scalars_ref[origin], axis=0, keepdims=True)
        g00, g01, g11, h0, h1 = [
            jnp.sum(jnp.where(lanes == sublanes + index * ROWS, total, 0.0), axis=1, keepdims=True)
            for index in range(SCALARS)
        ]
        ratio = g01 / g00
        pivot = g11 - ratio * g01
        second = jnp.where(pivot > 0.0, (h1 - ratio * h0) / pivot, 0.0)
        first = h0 / g00 - ratio * second
        for index in range(BLOCK):
            block_ref[index, place(origin), :] = first * in_ref[index] + second * in_ref[BLOCK + index]
    matrix = relative_rows(matrix_ref, mode)
    for index in range(BLOCK):
        mixed = jnp.dot(matrix, block_ref[index], precision=HIGHEST, preferred_element_type=F32)
        for step, out_ref in enumerate([o0, o1, o2, o3, o4, o5, o6, o7]):
            out_ref[index] = mixed[row_block(step), :]


def unpack_kernel(
    i4, i5, i7, i2, i6, i3, i1, i0, edge_ref, out_hbm, packed_ref, out_ref, semaphores
):
    mode = lax.axis_index("mode")
    for step, in_ref in enumerate([i0, i1, i2, i3, i4, i5, i6, i7]):
        packed_ref[jnp.bitwise_xor(mode, step)] = in_ref[...]

    def load(index):
        block, row = sent_place(index)
        return packed_ref[block, row]

    for index, node in enumerate(INNER_NODES):
        out_ref[node] = load(index)
    spans = [(SIDE, (SIDE - 2) * SIDE), (0, SIDE), (ORDER * SIDE, SIDE)]
    copies = [
        pltpu.make_async_copy(out_ref.at[pl.ds(*span)], out_hbm.at[pl.ds(*span)], semaphores.at[index])
        for index, span in enumerate(spans)
    ]

    def store(slot, value):
        out_ref[CYCLE_NODES[slot]] = value
        if slot == 2 * SIDE - 1:
            copies[0].start()
        if slot == CYCLE - 1:
            copies[1].start()
            copies[2].start()

    gather_cycle(read_skeleton(lambda index: load(INNER + index)), edge_ref[...], store)
    for copy in copies:
        copy.wait()


def call(kernel, out_shapes, scratch, *operands, limit=VMEM_LIMIT, **options):
    return pl.pallas_call(
        kernel,
        out_shape=out_shapes,
        scratch_shapes=scratch,
        compiler_params=pltpu.CompilerParams(vmem_limit_bytes=limit),
        **options,
    )(*operands)


def shape(*dims, dtype=F32):
    return jax.ShapeDtypeStruct(dims, dtype)


def swap_blocks(blocks, axis):
    return lax.all_to_all(blocks, axis, split_axis=0, concat_axis=0, tiled=True)


def permute(value, axis, flip):
    return lax.ppermute(value, axis, [(i, i ^ flip) for i in range(lax.axis_size(axis))])


def swap_steps(blocks):
    return [permute(blocks[step], "mode", step) for step in STEP_ORDER] + [blocks[0]]


def exchange(slots):
    return [permute(slots, "elem", 1 << level) for level in LEVEL_ORDER]


def body(forcing, metric, edge_map, shared_rows, partner_masks, penalty):
    forward, backward = [jnp.asarray(part) for part in fourier_tables()]
    table, cross = [jnp.asarray(part) for part in diagonal_tables()]
    metric = metric.transpose(1, 0, 2)
    edge_rows = edge_map.T
    shared = shared_rows.reshape(SLOT_TILES, LANES)
    masks = partner_masks.reshape(SLOT_TILES, LANES)
    left = pltpu.VMEM((2 * HIGH * ROWS, CYCLE * LANES), BF16)
    right = pltpu.VMEM((LOW, CYCLE * LANES), BF16)
    left_slots = pltpu.VMEM((2 * HIGH * ROWS, SLOTS), BF16)
    cycle = pltpu.VMEM((CYCLE, ROWS, LANES), F32)
    first = pltpu.VMEM((NODES, 8, LANES), F32)
    energy = pltpu.VMEM((ROWS, LANES), F32)
    packing = pltpu.VMEM((MODES, BLOCK, ROWS, LANES), F32)
    wide = (HIGH * ROWS, LOW)
    blocks = [shape(BLOCK, ROWS, LANES)] * MODES

    hbm = pl.BlockSpec(memory_space=pltpu.HBM)
    packed_shapes = [
        shape(MODES * BLOCK, ROWS, LANES), shape(SLOT_TILES, ROWS + 8, LANES),
        shape(2, INNER, LANES), shape(2, HIGH, LOW), shape(HIGH, LOW), shape(8, LANES, dtype=jnp.int32),
    ]
    operands = [forcing.transpose(1, 0, 2), edge_rows, shared, masks, metric, penalty, table, cross]
    packed, message, inner, diagonal, penalties, lists = call(
        pack_kernel, packed_shapes,
        [pltpu.VMEM(operand.shape, operand.dtype) for operand in operands]
        + [pltpu.VMEM((MODES * BLOCK - INNER, ROWS, LANES), F32)]
        + [pltpu.VMEM(part.shape, part.dtype) for part in packed_shapes[1:]]
        + [
            pltpu.VMEM((2, NODES, LANES), F32), pltpu.VMEM(((2 * HIGH + QUADS) * ROWS, CYCLE * LANES), BF16), right,
            pltpu.SemaphoreType.DMA((len(operands),)), pltpu.SemaphoreType.DMA((ORDER + 5,)),
        ],
        *operands,
        in_specs=[hbm] * len(operands), out_specs=[hbm] * len(packed_shapes), limit=FIRST_LIMIT,
    )
    gathered = swap_blocks(packed.reshape(MODES, BLOCK, ROWS, LANES), "mode")
    *mixed, extra = call(
        transform_kernel, [shape(SHARE, ROWS, LANES)] * MODES + [shape(SLOT_TILES, 8, LANES)],
        [pltpu.VMEM((SLOT_TILES, PLANES, LANES), F32)], forward, gathered, *exchange(message), lists,
    )
    inside = shape(INNER, ROWS, LANES)
    search, inverse, applied, source, kept, slots, sums = call(
        first_kernel,
        [
            inside, inside, shape(NODES, ROWS, LANES), shape(MODES, BLOCK, ROWS, LANES), shape(4, *wide),
            shape(SLOT_TILES, ROWS, LANES), shape(2, ROWS, LANES),
        ],
        [left, right, cycle, first, energy, energy],
        *swap_steps(mixed), extra, lists, edge_rows, metric, inner, diagonal, penalties,
    )
    pair = shape(MODES, 2 * BLOCK, ROWS, LANES)
    moved, moved_sums, filled = call(
        change_kernel, [inside, shape(2, ROWS, LANES), pair], [], search, inverse, applied, source, kept
    )
    change, changed_sums, both, *pairs = call(
        second_kernel,
        [shape(*wide), shape(2, ROWS, LANES), pair] + [shape(2 * BLOCK, ROWS, LANES)] * MODES,
        [left_slots],
        kept, moved_sums, filled, *exchange(slots), lists,
        input_output_aliases={2: 2},
    )
    message = call(
        energy_kernel, shape(MODES * ELEMS_AXIS, LANES), [cycle, first, energy, energy],
        moved, change, sums, changed_sums, edge_rows, metric, penalties,
    )
    scalars = swap_blocks(message, ("mode", "elem")).reshape(MODES, ELEMS_AXIS, LANES)
    mixed = call(
        combine_kernel, blocks, [pltpu.VMEM((BLOCK, PLANES, LANES), F32)], backward, scalars, *swap_steps(pairs)
    )
    result = call(
        unpack_kernel, shape(NODES, ROWS, LANES),
        [packing, pltpu.VMEM((NODES, ROWS, LANES), F32), pltpu.SemaphoreType.DMA((3,))],
        *swap_steps(mixed), edge_rows, out_specs=hbm,
    )
    return result.transpose(1, 0, 2)


def solution(mesh):
    placed = (
        P("mode", None, "elem"),
        P(None, None, "elem"),
        P("elem", None),
        P("elem"),
        P("elem"),
        P("elem"),
    )
    return jax.shard_map(
        body, mesh=mesh, in_specs=placed, out_specs=P("mode", None, "elem"), check_vma=False
    )
```

```python
import functools
import math

import jax
import jax.numpy as jnp
import numpy as np
from jax import lax
from jax.experimental import pallas as pl
from jax.experimental.pallas import tpu as pltpu
from jax.sharding import PartitionSpec as P

ORDER = 8
SIDE = ORDER + 1
NODES = SIDE * SIDE
CYCLE = 32
INNER = (ORDER - 1) ** 2
ROWS = 16
LANES = 128
PLANES = 128
MODES = 8
ELEMS_AXIS = 32
SKEL = 2113
LOW = 256
HIGH = 9
TILES = 2 * HIGH
QUADS = -(-HIGH // 4)
SLOTS = 384
SLOT_TILES = SLOTS // LANES
BLOCK = 9
SHARE = BLOCK + SLOT_TILES
LINE = ORDER - 1
PAIRED = BLOCK + 2
SCALARS = 5
WIDTH = SCALARS * ROWS
STEP_ORDER = [4, 5, 7, 2, 6, 3, 1]
LEVEL_ORDER = [0, 2, 1, 3, 4]
SPACING = 0.25
F32 = jnp.float32
BF16 = jnp.bfloat16
HIGHEST = lax.Precision.HIGHEST
VMEM_LIMIT = 32 * 1024 * 1024
FIRST_LIMIT = 56 * 1024 * 1024


def legendre_table(points, poly_order):
    table = np.zeros((points.shape[0], poly_order + 1))
    table[:, 0] = 1.0
    table[:, 1] = points
    for degree in range(2, poly_order + 1):
        table[:, degree] = (
            (2 * degree - 1) * points * table[:, degree - 1] - (degree - 1) * table[:, degree - 2]
        ) / degree
    return table


def lobatto_derivative(poly_order):
    node_count = poly_order + 1
    points = np.cos(np.pi * np.arange(node_count) / poly_order)
    for newton_step in range(100):
        table = legendre_table(points, poly_order)
        points = points - (points * table[:, poly_order] - table[:, poly_order - 1]) / (
            node_count * table[:, poly_order]
        )
    points = np.sort(points)
    top_values = legendre_table(points, poly_order)[:, poly_order]
    identity = np.eye(node_count)
    differ = points[:, None] - points[None, :] + identity
    matrix = top_values[:, None] / (top_values[None, :] * differ)
    matrix = matrix * (1.0 - identity)
    matrix[0, 0] = -poly_order * node_count / 4.0
    matrix[poly_order, poly_order] = poly_order * node_count / 4.0
    return matrix


def fourier_tables():
    positions = np.arange(PLANES)
    phases = ((positions // 2)[:, None] * positions[None, :] % PLANES) * (2.0 * np.pi / PLANES)
    cosine, sine = np.cos(phases), np.sin(phases)
    even = (positions % 2 == 0)[:, None]
    nyquist = (positions == 1)[:, None]
    alternate = (1.0 - 2.0 * (positions % 2))[None, :]
    forward = np.where(nyquist, alternate, np.where(even, cosine, -sine)) / PLANES
    backward = np.where(nyquist, alternate, np.where(even, 2.0 * cosine, -2.0 * sine))
    backward = np.where((positions == 0)[:, None], 1.0, backward)
    return forward.astype(np.float32), backward.T.astype(np.float32)


DERIVATIVE64 = lobatto_derivative(ORDER)
DERIVATIVE = DERIVATIVE64.astype(np.float32)
CYCLE_NODES = (
    [i * SIDE for i in range(SIDE)]
    + [i * SIDE + ORDER for i in range(SIDE)]
    + [j for j in range(1, ORDER)]
    + [ORDER * SIDE + j for j in range(1, ORDER)]
)
INNER_NODES = [i * SIDE + j for i in range(1, ORDER) for j in range(1, ORDER)]


def diagonal_tables():
    squared = (DERIVATIVE * DERIVATIVE).astype(np.float64)
    first = np.kron(squared.T, np.eye(SIDE))
    second = np.kron(np.eye(SIDE), squared.T)
    corner = np.diagonal(DERIVATIVE)
    cross = 2.0 * np.outer(corner, corner).reshape(NODES, 1)
    cross = np.broadcast_to(cross, (NODES, LANES))
    return np.concatenate([first, second], axis=1).astype(np.float32), cross.astype(np.float32)


def helmholtz_shift(mode):
    rows_global = mode * ROWS + lax.broadcasted_iota(jnp.int32, (ROWS, LANES), 0)
    wavenumber = jnp.right_shift(rows_global, 1).astype(F32)
    spanwise = wavenumber * (2.0 * math.pi / (PLANES * SPACING))
    spanwise = jnp.where(rows_global == 1, math.pi / SPACING, spanwise)
    return spanwise * spanwise


def row_block(index):
    return slice(index * ROWS, (index + 1) * ROWS)


def lane_block(index):
    return slice(index * LANES, (index + 1) * LANES)


def pieces(value):
    top = value.astype(BF16).astype(F32)
    return top, value - top


def one_hot_rows(low_rows):
    sublanes = lax.broadcasted_iota(jnp.int32, (LOW, low_rows.shape[1]), 0).astype(BF16)
    wanted = jnp.broadcast_to(low_rows.astype(BF16), sublanes.shape)
    return jnp.where(wanted == sublanes, BF16(1.0), BF16(0.0))


def masked_store(value, high_row, left_ref, column):
    top, rest = [part.astype(BF16) for part in pieces(value)]
    wanted = jnp.broadcast_to(high_row.astype(BF16), value.shape)
    for high in range(HIGH):
        here = wanted == BF16(high)
        left_ref[row_block(high), lane_block(column)] = jnp.where(here, top, BF16(0.0))
        left_ref[row_block(HIGH + high), lane_block(column)] = jnp.where(here, rest, BF16(0.0))


def contract_lanes(left, right):
    return lax.dot_general(left, right, (((1,), (1,)), ((), ())), preferred_element_type=F32)


def scatter_sum(left, selectors):
    both = contract_lanes(left, selectors)
    return both[: HIGH * ROWS] + both[HIGH * ROWS :]


def one_hot_cycle(edge_rows, selectors_ref):
    low = jnp.bitwise_and(edge_rows, LOW - 1)
    for slot in range(CYCLE):
        selectors_ref[:, lane_block(slot)] = one_hot_rows(low[slot : slot + 1, :])


def scatter_cycle(load, edge_rows, left_ref, selectors_ref):
    high_rows = jnp.right_shift(edge_rows, 8)
    for slot in range(CYCLE):
        masked_store(load(slot), high_rows[slot : slot + 1, :], left_ref, slot)
    return scatter_sum(left_ref[...], selectors_ref[...])


def slot_selectors(shared_rows):
    low = jnp.bitwise_and(shared_rows, LOW - 1)
    return jnp.concatenate(
        [one_hot_rows(low[tile : tile + 1, :]) for tile in range(SLOT_TILES)], axis=1
    )


def four_pieces(first, second):
    sublanes = jnp.bitwise_and(lax.broadcasted_iota(jnp.int32, (ROWS, first.shape[1]), 0), 3)
    first_top, first_rest = pieces(first)
    second_top, second_rest = pieces(second)
    tops = jnp.where(sublanes == 0, first_top, second_top)
    rests = jnp.where(sublanes == 2, first_rest, second_rest)
    return jnp.where(sublanes < 2, tops, rests)


def masked_store_four(value, high_row, left_ref, column):
    packed = value.astype(BF16)
    quarter = jnp.right_shift(lax.broadcasted_iota(jnp.int32, value.shape, 0), 2).astype(BF16)
    wanted = jnp.broadcast_to(high_row.astype(BF16), value.shape) - quarter
    for block in range(QUADS):
        here = wanted == BF16(4 * block)
        left_ref[row_block(block), lane_block(column)] = jnp.where(here, packed, BF16(0.0))


def two_rows(total, high):
    base = 4 * high
    first = total[base : base + 1, :] + total[base + 2 : base + 3, :]
    second = total[base + 1 : base + 2, :] + total[base + 3 : base + 4, :]
    return first, second


def scatter_slots(load, shared_rows, left_ref, right):
    high_rows = jnp.right_shift(shared_rows, 8)
    for tile in range(SLOT_TILES):
        masked_store(load(tile), high_rows[tile : tile + 1, :], left_ref, tile)
    return scatter_sum(left_ref[:, :SLOTS], right)


def stack_pieces(skeleton):
    top, rest = pieces(skeleton)
    return jnp.concatenate([top.astype(BF16), rest.astype(BF16)], axis=0)


def gather_tile(stacked, rows, keep=None):
    low = jnp.bitwise_and(rows, LOW - 1)
    high = jnp.right_shift(rows, 8)
    selector = one_hot_rows(low)
    if keep is not None:
        keep(selector)
    found = jnp.dot(stacked, selector, preferred_element_type=F32)
    total = None
    for index in range(HIGH):
        part = found[row_block(index), :] + found[row_block(HIGH + index), :]
        part = jnp.where(high == index, part, 0.0)
        total = part if total is None else total + part
    return total


def keep_columns(selectors_ref, column, selector):
    selectors_ref[:, column * LANES : (column + 2) * LANES] = selector


def gather_cycle(skeleton, edge_rows, store, selectors_ref=None):
    stacked = stack_pieces(skeleton)
    for pair in range(CYCLE // 2):
        rows = jnp.concatenate(
            [edge_rows[2 * pair : 2 * pair + 1, :], edge_rows[2 * pair + 1 : 2 * pair + 2, :]], axis=1
        )
        keep = None
        if selectors_ref is not None:
            keep = functools.partial(keep_columns, selectors_ref, 2 * pair)
        total = gather_tile(stacked, rows, keep)
        store(2 * pair, total[:, :LANES])
        store(2 * pair + 1, total[:, LANES:])


def gather_slots(skeleton, shared_rows):
    stacked = stack_pieces(skeleton)
    return [gather_tile(stacked, shared_rows[tile : tile + 1, :]) for tile in range(SLOT_TILES)]


def sent_place(index):
    if index < INNER:
        return index // LINE, index % LINE
    extra = index - INNER
    block = min(extra // 2, MODES - 1)
    row = extra - 2 * block
    return block, row + LINE if row < 2 else row - 2


def kept_place(index):
    block, row = sent_place(index)
    return block, row + 2


EMPTY_PLACES = [(MODES - 1, row) for row in range(2, LINE)]


def read_skeleton(load):
    return jnp.concatenate(
        [jnp.concatenate([load(2 * high), load(2 * high + 1)], axis=1) for high in range(HIGH)], axis=0
    )


def write_skeleton(skeleton, store):
    for high in range(HIGH):
        store(2 * high, skeleton[row_block(high), :LANES])
        store(2 * high + 1, skeleton[row_block(high), LANES:])


def write_place(ref, place):
    def store(index, value):
        block, row = place(index)
        ref[block, row] = value

    return store


def fold(value):
    return value[:, :LANES] + value[:, LANES:]


def per_tile(penalty_ref):
    return jnp.concatenate(
        [jnp.broadcast_to(penalty_ref[high : high + 1, :], (ROWS, LOW)) for high in range(HIGH)], axis=0
    )


def skeleton_sum(product):
    total = None
    for high in range(HIGH):
        part = fold(product[row_block(high), :])
        total = part if total is None else total + part
    return total


def select_arrived(masks, tile, arrived):
    chosen = arrived[0]
    row = masks[tile : tile + 1, :]
    for level in range(1, len(arrived)):
        moving = jnp.bitwise_and(jnp.right_shift(row, level), 1) == 1
        chosen = jnp.where(moving, arrived[level], chosen)
    return chosen


def weighted_sum(weights, values):
    total = None
    for weight, value in zip(weights, values):
        if weight == 0.0:
            continue
        part = float(weight) * value
        total = part if total is None else total + part
    return total


def derivative_line(values, transposed):
    matrix = DERIVATIVE64.T if transposed else DERIVATIVE64
    half = SIDE // 2
    evens = [values[k] + values[ORDER - k] for k in range(half)] + [values[half]]
    odds = [values[k] - values[ORDER - k] for k in range(half)]
    results = [None] * SIDE
    for out in range(half):
        near, far = matrix[out, :half], matrix[out, :half:-1]
        even = weighted_sum(np.float32(np.append(0.5 * (near + far), matrix[out, half])), evens)
        odd = weighted_sum(np.float32(0.5 * (near - far)), odds)
        results[out] = odd + even
        results[ORDER - out] = odd - even
    results[half] = weighted_sum(np.float32(matrix[half, :half]), odds)
    return results


def grid_load(inner_ref, cycle_ref, rows):
    def load(node):
        if node in CYCLE_NODES:
            return cycle_ref[CYCLE_NODES.index(node), rows, :]
        return inner_ref[INNER_NODES.index(node), rows, :]

    return load


def gradients(load, first_ref, metric_ref, visit):
    for j in range(SIDE):
        line = derivative_line([load(k * SIDE + j) for k in range(SIDE)], False)
        for i in range(SIDE):
            first_ref[i * SIDE + j] = line[i]
    for i in range(SIDE):
        line = derivative_line([load(i * SIDE + k) for k in range(SIDE)], False)
        seconds = []
        for j in range(SIDE):
            node = i * SIDE + j
            m0, m1, m2 = [metric_ref[node, c : c + 1, :] for c in range(3)]
            g1, g2 = first_ref[node], line[j]
            p1 = m0 * g1 + m2 * g2
            p2 = m2 * g1 + m1 * g2
            visit(node, g1, g2, p1, p2)
            seconds.append(p2)
        yield i, seconds


def apply_operator(inner_ref, cycle_ref, result_ref, first_ref, energy_ref, metric_ref, shift_ref):
    @pl.loop(0, 2)
    def half(part):
        rows = pl.ds(pl.multiple_of(part * 8, 8), 8)
        shift = shift_ref[rows, :]
        load = grid_load(inner_ref, cycle_ref, rows)

        def visit(node, g1, g2, p1, p2):
            first_ref[node] = p1

        for i, seconds in gradients(load, first_ref, metric_ref, visit):
            line = derivative_line(seconds, True)
            for j in range(SIDE):
                node = i * SIDE + j
                mass = shift * metric_ref[node, 3:4, :]
                result_ref[node, rows, :] = line[j] + mass * load(node)
        energy = jnp.zeros((8, LANES), F32)
        for j in range(SIDE):
            line = derivative_line([first_ref[k * SIDE + j] for k in range(SIDE)], True)
            for i in range(SIDE):
                node = i * SIDE + j
                value = result_ref[node, rows, :] + line[i]
                result_ref[node, rows, :] = value
                energy = energy + value * load(node)
        energy_ref[rows, :] = energy


def apply_energy(inner_ref, cycle_ref, first_ref, energy_ref, metric_ref, shift_ref):
    @pl.loop(0, 2)
    def half(part):
        rows = pl.ds(pl.multiple_of(part * 8, 8), 8)
        shift = shift_ref[rows, :]
        load = grid_load(inner_ref, cycle_ref, rows)
        sums = [jnp.zeros((8, LANES), F32)]

        def visit(node, g1, g2, p1, p2):
            value = load(node)
            mass = shift * metric_ref[node, 3:4, :]
            sums[0] = sums[0] + (g1 * p1 + g2 * p2 + mass * value * value)

        for i, seconds in gradients(load, first_ref, metric_ref, visit):
            pass
        energy_ref[rows, :] = sums[0]


def diagonal_cells(metric_ref, table_ref, cross_ref, penalty_ref, inner_ref, padded_ref, cells_ref):
    both = jnp.concatenate([metric_ref[:, 0, :], metric_ref[:, 1, :]], axis=0)
    terms = jnp.dot(table_ref[...], both, precision=HIGHEST, preferred_element_type=F32)
    cells_ref[0] = terms + cross_ref[...] * metric_ref[:, 2, :]
    cells_ref[1] = metric_ref[:, 3, :]
    padded_ref[...] = jnp.ones((HIGH, LOW), F32)
    for high in range(HIGH):
        count = min(LOW, SKEL - high * LOW)
        line = penalty_ref[pl.ds(high * LOW, count)]
        padded_ref[high : high + 1, :count] = line.reshape(1, count)
    for index, node in enumerate(INNER_NODES):
        inner_ref[0, index : index + 1, :] = cells_ref[0, node : node + 1, :]
        inner_ref[1, index : index + 1, :] = cells_ref[1, node : node + 1, :]


def diagonal_slots(total, shared_rows, selectors, padded_ref, skeleton_ref):
    stacked = []
    for high in range(HIGH):
        laplace, mass = two_rows(total, high)
        laplace = laplace + padded_ref[high : high + 1, :]
        skeleton_ref[0, high : high + 1, :] = laplace
        skeleton_ref[1, high : high + 1, :] = mass
        stacked.append(four_pieces(laplace, mass).astype(BF16))
    stacked = jnp.concatenate(stacked, axis=0)
    results = []
    for tile in range(SLOT_TILES):
        high_row = jnp.right_shift(shared_rows[tile : tile + 1, :], 8)
        found = jnp.dot(stacked, selectors[:, lane_block(tile)], preferred_element_type=F32)
        value = jnp.zeros((ROWS, LANES), F32)
        for high in range(HIGH):
            value = value + jnp.where(high_row == high, found[row_block(high), :], 0.0)
        results.append(two_rows(value, 0))
    return results


def pack_kernel(
    forcing_hbm, edge_hbm, shared_hbm, masks_hbm, metric_hbm, penalty_hbm, table_hbm, cross_hbm,
    out_hbm, message_hbm, inner_hbm, skeleton_hbm, padded_hbm, lists_hbm,
    forcing_ref, edge_ref, shared_ref, masks_ref, metric_ref, penalty_ref, table_ref, cross_ref,
    packed_ref, message_ref, inner_ref, skeleton_ref, padded_ref, lists_ref,
    cells_ref, left_ref, selectors_ref, in_semaphores, out_semaphores,
):
    ins = [
        pltpu.make_async_copy(source, target, in_semaphores.at[index])
        for index, (source, target) in enumerate(
            [
                (edge_hbm, edge_ref), (metric_hbm, metric_ref), (table_hbm, table_ref), (cross_hbm, cross_ref),
                (penalty_hbm, penalty_ref), (shared_hbm, shared_ref), (masks_hbm, masks_ref),
                (forcing_hbm, forcing_ref),
            ]
        )
    ]
    for copy in ins:
        copy.start()
    outs = []

    def send(source, target):
        copy = pltpu.make_async_copy(source, target, out_semaphores.at[len(outs)])
        copy.start()
        outs.append(copy)

    base = 2 * HIGH * ROWS
    tail = list(range(TILES - 4)) + [TILES - 2, TILES - 1] + [None] * len(EMPTY_PLACES) + [TILES - 4, TILES - 3]
    for position, index in enumerate(tail):
        if index is None:
            packed_ref[position] = jnp.zeros((ROWS, LANES), F32)
    ins[0].wait()
    edge_rows = edge_ref[...]
    one_hot_cycle(edge_rows, selectors_ref)
    for copy in ins[1:7]:
        copy.wait()
    shared_rows = shared_ref[...]
    lists_ref[:SLOT_TILES, :] = shared_rows
    lists_ref[SLOT_TILES : 2 * SLOT_TILES, :] = masks_ref[...]
    lists_ref[2 * SLOT_TILES :, :] = jnp.zeros((8 - 2 * SLOT_TILES, LANES), jnp.int32)
    send(lists_ref, lists_hbm)
    diagonal_cells(metric_ref, table_ref, cross_ref, penalty_ref, inner_ref, padded_ref, cells_ref)
    send(inner_ref, inner_hbm)
    send(padded_ref, padded_hbm)
    ins[7].wait()
    for line in range(LINE):
        send(forcing_ref.at[pl.ds((line + 1) * SIDE + 1, LINE)], out_hbm.at[pl.ds(line * BLOCK, LINE)])
    high_rows = jnp.right_shift(edge_rows, 8)
    for slot in range(CYCLE):
        node = CYCLE_NODES[slot]
        high_row = high_rows[slot : slot + 1, :]
        masked_store(forcing_ref[node], high_row, left_ref, slot)
        value = four_pieces(cells_ref[0, node : node + 1, :], cells_ref[1, node : node + 1, :])
        masked_store_four(value, high_row, left_ref.at[pl.ds(base, QUADS * ROWS)], slot)
    total = contract_lanes(left_ref[...], selectors_ref[...])
    skeleton = total[: HIGH * ROWS] + total[HIGH * ROWS : base]

    def store(index, value):
        packed_ref[tail.index(index)] = value

    write_skeleton(skeleton, store)
    for line in range(LINE):
        send(packed_ref.at[pl.ds(2 * line, 2)], out_hbm.at[pl.ds(line * BLOCK + LINE, 2)])
    send(packed_ref.at[pl.ds(TILES - 4, BLOCK)], out_hbm.at[pl.ds(LINE * BLOCK, BLOCK)])
    selectors = slot_selectors(shared_rows)
    pairs = diagonal_slots(total[base:], shared_rows, selectors, padded_ref, skeleton_ref)
    send(skeleton_ref, skeleton_hbm)
    for tile, value in enumerate(gather_slots(skeleton, shared_rows)):
        laplace, mass = pairs[tile]
        message_ref[tile, :ROWS, :] = value
        message_ref[tile, ROWS:, :] = jnp.zeros((8, LANES), F32)
        message_ref[tile, ROWS : ROWS + 1, :] = laplace
        message_ref[tile, ROWS + 1 : ROWS + 2, :] = mass
    send(message_ref, message_hbm)
    for copy in outs:
        copy.wait()


def place(index):
    return pl.ds(pl.multiple_of(index * ROWS, ROWS), ROWS)


def relative_rows(matrix_ref, mode):
    parts = [matrix_ref[place(jnp.bitwise_xor(mode, step)), :] for step in range(MODES)]
    return jnp.concatenate(parts, axis=0)


def transform_kernel(
    matrix_ref, in_ref, a0, a2, a1, a3, a4, lists_ref, o0, o1, o2, o3, o4, o5, o6, o7, extra_ref, slots_ref
):
    mode = lax.axis_index("mode")
    outs = [o0, o1, o2, o3, o4, o5, o6, o7]
    matrix = relative_rows(matrix_ref, mode)
    slots_ref[...] = jnp.zeros(slots_ref.shape, F32)
    arrived_refs = [a0, a1, a2, a3, a4]
    masks = lists_ref[SLOT_TILES : 2 * SLOT_TILES, :]
    for index in range(BLOCK):
        block = in_ref[:, index].reshape(PLANES, LANES)
        mixed = jnp.dot(matrix, block, precision=HIGHEST, preferred_element_type=F32)
        for step, out_ref in enumerate(outs):
            out_ref[index] = mixed[row_block(step), :]
    for tile in range(SLOT_TILES):
        chosen = select_arrived(masks, tile, [ref[tile] for ref in arrived_refs])
        slots_ref[tile, place(mode), :] = chosen[:ROWS]
        mixed = jnp.dot(matrix, slots_ref[tile], precision=HIGHEST, preferred_element_type=F32)
        for step, out_ref in enumerate(outs):
            out_ref[BLOCK + tile] = mixed[row_block(step), :]
        extra_ref[tile] = chosen[ROWS:]


def column_kernel(inner_ref, o0, o1, o2, o3, o4, o5, o6, o7, out_ref):
    mode = lax.axis_index("mode")
    start = jnp.minimum(mode, LINE - 1) * LINE
    for step, in_ref in enumerate([o0, o1, o2, o3, o4, o5, o6, o7]):
        origin = jnp.bitwise_xor(mode, step)
        shift = helmholtz_shift(origin)
        for index in range(LINE):
            laplace = inner_ref[0, pl.ds(start + index, 1), :]
            mass = inner_ref[1, pl.ds(start + index, 1), :]
            out_ref[index, place(origin), :] = in_ref[index] * (1.0 / (laplace + shift * mass))


def first_kernel(
    i4, i5, i7, i2, i6, i3, i1, i0, extra_ref, lists_ref, edge_ref, metric_ref,
    inner_ref, diagonal_ref, penalty_ref, search_ref, inverse_ref, result_ref, source_ref, kept_ref, slots_ref,
    sums_ref, left_ref, right_ref, cycle_ref, first_ref, energy_ref, shift_ref,
):
    mode = lax.axis_index("mode")
    ins = [i0, i1, i2, i3, i4, i5, i6, i7]
    for step, in_ref in enumerate(ins):
        source_ref[jnp.bitwise_xor(mode, step)] = in_ref[:BLOCK]
    shared_rows = lists_ref[:SLOT_TILES, :]
    right_slots = slot_selectors(shared_rows)
    shift = helmholtz_shift(lax.axis_index("mode"))
    shift_ref[...] = shift
    edge_rows = edge_ref[...]

    def load_right(tile):
        total = ins[0][BLOCK + tile]
        for in_ref in ins[1:]:
            total = total + in_ref[BLOCK + tile]
        return total

    def source(index):
        block, row = sent_place(index)
        return source_ref[block, row]

    high_rows = jnp.right_shift(shared_rows, 8)
    for tile in range(SLOT_TILES):
        value = four_pieces(extra_ref[tile, 0:1, :], extra_ref[tile, 1:2, :])
        masked_store_four(value, high_rows[tile : tile + 1, :], left_ref, tile)
    added = contract_lanes(left_ref[: QUADS * ROWS, :SLOTS], right_slots)
    wide_shift = jnp.concatenate([shift, shift], axis=1)
    parts = []
    for high in range(HIGH):
        laplace, mass = two_rows(added, high)
        laplace = laplace + diagonal_ref[0, high : high + 1, :]
        mass = mass + diagonal_ref[1, high : high + 1, :]
        parts.append(1.0 / (laplace + wide_shift * mass))
    inverse = jnp.concatenate(parts, axis=0)
    local = read_skeleton(lambda index: source(INNER + index))
    right_side = local + scatter_slots(load_right, shared_rows, left_ref, right_slots)
    search = right_side * inverse
    kept_ref[0] = local
    kept_ref[1] = inverse
    kept_ref[2] = search
    start = skeleton_sum(local * search)
    for index, node in enumerate(INNER_NODES):
        value = source(index)
        inverted = 1.0 / (inner_ref[0, index : index + 1, :] + shift * inner_ref[1, index : index + 1, :])
        scaled = value * inverted
        search_ref[index] = scaled
        inverse_ref[index] = inverted
        start = start + value * scaled

    def store(slot, value):
        cycle_ref[slot] = value

    gather_cycle(search, edge_rows, store, right_ref)
    apply_operator(search_ref, cycle_ref, result_ref, first_ref, energy_ref, metric_ref, shift_ref)
    weighted = per_tile(penalty_ref) * search
    applied = weighted + scatter_cycle(
        lambda slot: result_ref[CYCLE_NODES[slot]], edge_rows, left_ref, right_ref
    )
    kept_ref[3] = applied
    for tile, value in enumerate(gather_slots(applied, shared_rows)):
        slots_ref[tile] = value
    sums_ref[0] = energy_ref[...] + skeleton_sum(weighted * search)
    sums_ref[1] = start


def change_kernel(search_ref, inverse_ref, result_ref, source_ref, kept_ref, moved_ref, sums_ref, both_ref):
    crossed = jnp.zeros((ROWS, LANES), F32)
    sourced = jnp.zeros((ROWS, LANES), F32)
    for index, node in enumerate(INNER_NODES):
        block, row = sent_place(index)
        value = result_ref[node]
        search = search_ref[index]
        moved = value * inverse_ref[index] - search
        moved_ref[index] = moved
        both_ref[block, row] = moved
        crossed = crossed + value * moved
        sourced = sourced + source_ref[block, row] * moved
    for high in range(HIGH):
        for part in range(2):
            block, row = kept_place(INNER + 2 * high + part)
            both_ref[block, row] = kept_ref[2, row_block(high), lane_block(part)]
    for block, row in EMPTY_PLACES[2:]:
        both_ref[block, row] = jnp.zeros((ROWS, LANES), F32)
    sums_ref[0] = crossed
    sums_ref[1] = sourced


def second_kernel(
    kept_ref, moved_sums_ref, filled_ref, a0, a2, a1, a3, a4, lists_ref,
    change_ref, sums_ref, both_ref, o0, o1, o2, o3, o4, o5, o6, o7, left_ref,
):
    arrived_refs = [a0, a1, a2, a3, a4]
    masks = lists_ref[SLOT_TILES : 2 * SLOT_TILES, :]
    shared_rows = lists_ref[:SLOT_TILES, :]

    def load(tile):
        return select_arrived(masks, tile, [ref[tile] for ref in arrived_refs])

    local, inverse, search, applied = [kept_ref[index] for index in range(4)]
    full = applied + scatter_slots(load, shared_rows, left_ref, slot_selectors(shared_rows))
    change = full * inverse - search
    for high in range(HIGH):
        for part in range(2):
            block, row = sent_place(INNER + 2 * high + part)
            both_ref[block, row] = change[row_block(high), lane_block(part)]
    mode = lax.axis_index("mode")
    for step, out_ref in enumerate([o0, o1, o2, o3, o4, o5, o6, o7]):
        out_ref[...] = both_ref[jnp.bitwise_xor(mode, step)]
    change_ref[...] = change
    sums_ref[0] = moved_sums_ref[0] + skeleton_sum(applied * change)
    sums_ref[1] = moved_sums_ref[1] + skeleton_sum(local * change)


def energy_kernel(
    moved_ref, change_ref, sums_ref, changed_sums_ref, edge_ref, metric_ref, penalty_ref, message_ref,
    cycle_ref, first_ref, energy_ref, shift_ref,
):
    shift_ref[...] = helmholtz_shift(lax.axis_index("mode"))
    change = change_ref[...]

    def store(slot, value):
        cycle_ref[slot] = value

    gather_cycle(change, edge_ref[...], store)
    apply_energy(moved_ref, cycle_ref, first_ref, energy_ref, metric_ref, shift_ref)
    energy = energy_ref[...] + skeleton_sum(per_tile(penalty_ref) * change * change)
    sublanes = lax.broadcasted_iota(jnp.int32, (ROWS, LANES), 0)
    lanes = lax.broadcasted_iota(jnp.int32, (ROWS, LANES), 1)
    spread = jnp.zeros((ROWS, LANES), F32)
    for index, value in enumerate([sums_ref[0], changed_sums_ref[0], energy, sums_ref[1], changed_sums_ref[1]]):
        column = jnp.sum(value, axis=1, keepdims=True)
        spread = jnp.where(lanes == sublanes + index * ROWS, column, spread)
    message = jnp.sum(spread, axis=0, keepdims=True)
    message_ref[...] = jnp.broadcast_to(message[:, :WIDTH], message_ref.shape)


def combine_kernel(
    matrix_ref, scalars_ref, column_ref, i4, i5, i7, i2, i6, i3, i1, i0, o0, o1, o2, o3, o4, o5, o6, o7, block_ref
):
    mode = lax.axis_index("mode")
    sublanes = lax.broadcasted_iota(jnp.int32, (ROWS, LANES), 0)
    lanes = lax.broadcasted_iota(jnp.int32, (ROWS, LANES), 1)
    for step, in_ref in enumerate([i0, i1, i2, i3, i4, i5, i6, i7]):
        origin = jnp.bitwise_xor(mode, step)
        total = jnp.sum(scalars_ref[origin], axis=0, keepdims=True)
        total = jnp.concatenate([total, jnp.zeros((1, LANES - WIDTH), F32)], axis=1)
        g00, g01, g11, h0, h1 = [
            jnp.sum(jnp.where(lanes == sublanes + index * ROWS, total, 0.0), axis=1, keepdims=True)
            for index in range(SCALARS)
        ]
        ratio = g01 / g00
        pivot = g11 - ratio * g01
        second = jnp.where(pivot > 0.0, (h1 - ratio * h0) / pivot, 0.0)
        first = h0 / g00 - ratio * second
        for index in range(BLOCK):
            if index < LINE:
                search = column_ref[index, place(origin), :]
                if index < 2:
                    search = jnp.where(mode == MODES - 1, in_ref[index + 2], search)
            else:
                search = in_ref[index + 2]
            block_ref[index, place(origin), :] = first * search + second * in_ref[index]
    matrix = relative_rows(matrix_ref, mode)
    for index in range(BLOCK):
        mixed = jnp.dot(matrix, block_ref[index], precision=HIGHEST, preferred_element_type=F32)
        for step, out_ref in enumerate([o0, o1, o2, o3, o4, o5, o6, o7]):
            out_ref[index] = mixed[row_block(step), :]


def unpack_kernel(
    i4, i5, i7, i2, i6, i3, i1, i0, edge_ref, out_hbm, packed_ref, out_ref, semaphores
):
    mode = lax.axis_index("mode")
    for step, in_ref in enumerate([i0, i1, i2, i3, i4, i5, i6, i7]):
        packed_ref[jnp.bitwise_xor(mode, step)] = in_ref[...]

    def load(index):
        block, row = sent_place(index)
        return packed_ref[block, row]

    for index, node in enumerate(INNER_NODES):
        out_ref[node] = load(index)
    spans = [(SIDE, (SIDE - 2) * SIDE), (0, SIDE), (ORDER * SIDE, SIDE)]
    copies = [
        pltpu.make_async_copy(out_ref.at[pl.ds(*span)], out_hbm.at[pl.ds(*span)], semaphores.at[index])
        for index, span in enumerate(spans)
    ]

    def store(slot, value):
        out_ref[CYCLE_NODES[slot]] = value
        if slot == 2 * SIDE - 1:
            copies[0].start()
        if slot == CYCLE - 1:
            copies[1].start()
            copies[2].start()

    gather_cycle(read_skeleton(lambda index: load(INNER + index)), edge_ref[...], store)
    for copy in copies:
        copy.wait()


def call(kernel, out_shapes, scratch, *operands, limit=VMEM_LIMIT, **options):
    return pl.pallas_call(
        kernel,
        out_shape=out_shapes,
        scratch_shapes=scratch,
        compiler_params=pltpu.CompilerParams(vmem_limit_bytes=limit),
        **options,
    )(*operands)


def shape(*dims, dtype=F32):
    return jax.ShapeDtypeStruct(dims, dtype)


def swap_blocks(blocks, axis):
    return lax.all_to_all(blocks, axis, split_axis=0, concat_axis=0, tiled=True)


def permute(value, axis, flip):
    return lax.ppermute(value, axis, [(i, i ^ flip) for i in range(lax.axis_size(axis))])


def swap_steps(blocks):
    return [permute(blocks[step], "mode", step) for step in STEP_ORDER] + [blocks[0]]


def exchange(slots):
    return [permute(slots, "elem", 1 << level) for level in LEVEL_ORDER]


def body(forcing, metric, edge_map, shared_rows, partner_masks, penalty):
    forward, backward = [jnp.asarray(part) for part in fourier_tables()]
    table, cross = [jnp.asarray(part) for part in diagonal_tables()]
    metric = metric.transpose(1, 0, 2)
    edge_rows = edge_map.T
    shared = shared_rows.reshape(SLOT_TILES, LANES)
    masks = partner_masks.reshape(SLOT_TILES, LANES)
    left = pltpu.VMEM((2 * HIGH * ROWS, CYCLE * LANES), BF16)
    right = pltpu.VMEM((LOW, CYCLE * LANES), BF16)
    left_slots = pltpu.VMEM((2 * HIGH * ROWS, SLOTS), BF16)
    cycle = pltpu.VMEM((CYCLE, ROWS, LANES), F32)
    first = pltpu.VMEM((NODES, 8, LANES), F32)
    energy = pltpu.VMEM((ROWS, LANES), F32)
    packing = pltpu.VMEM((MODES, BLOCK, ROWS, LANES), F32)
    wide = (HIGH * ROWS, LOW)
    blocks = [shape(BLOCK, ROWS, LANES)] * MODES

    hbm = pl.BlockSpec(memory_space=pltpu.HBM)
    packed_shapes = [
        shape(MODES * BLOCK, ROWS, LANES), shape(SLOT_TILES, ROWS + 8, LANES),
        shape(2, INNER, LANES), shape(2, HIGH, LOW), shape(HIGH, LOW), shape(8, LANES, dtype=jnp.int32),
    ]
    operands = [forcing.transpose(1, 0, 2), edge_rows, shared, masks, metric, penalty, table, cross]
    packed, message, inner, diagonal, penalties, lists = call(
        pack_kernel, packed_shapes,
        [pltpu.VMEM(operand.shape, operand.dtype) for operand in operands]
        + [pltpu.VMEM((MODES * BLOCK - INNER, ROWS, LANES), F32)]
        + [pltpu.VMEM(part.shape, part.dtype) for part in packed_shapes[1:]]
        + [
            pltpu.VMEM((2, NODES, LANES), F32), pltpu.VMEM(((2 * HIGH + QUADS) * ROWS, CYCLE * LANES), BF16), right,
            pltpu.SemaphoreType.DMA((len(operands),)), pltpu.SemaphoreType.DMA((2 * LINE + 6,)),
        ],
        *operands,
        in_specs=[hbm] * len(operands), out_specs=[hbm] * len(packed_shapes), limit=FIRST_LIMIT,
    )
    gathered = swap_blocks(packed.reshape(MODES, BLOCK, ROWS, LANES), "mode")
    *mixed, extra = call(
        transform_kernel, [shape(SHARE, ROWS, LANES)] * MODES + [shape(SLOT_TILES, 8, LANES)],
        [pltpu.VMEM((SLOT_TILES, PLANES, LANES), F32)], forward, gathered, *exchange(message), lists,
    )
    column = call(column_kernel, shape(LINE, PLANES, LANES), [], inner, *mixed)
    inside = shape(INNER, ROWS, LANES)
    search, inverse, applied, source, kept, slots, sums = call(
        first_kernel,
        [
            inside, inside, shape(NODES, ROWS, LANES), shape(MODES, BLOCK, ROWS, LANES), shape(4, *wide),
            shape(SLOT_TILES, ROWS, LANES), shape(2, ROWS, LANES),
        ],
        [left, right, cycle, first, energy, energy],
        *swap_steps(mixed), extra, lists, edge_rows, metric, inner, diagonal, penalties,
    )
    pair = shape(MODES, PAIRED, ROWS, LANES)
    moved, moved_sums, filled = call(
        change_kernel, [inside, shape(2, ROWS, LANES), pair], [], search, inverse, applied, source, kept
    )
    change, changed_sums, both, *pairs = call(
        second_kernel,
        [shape(*wide), shape(2, ROWS, LANES), pair] + [shape(PAIRED, ROWS, LANES)] * MODES,
        [left_slots],
        kept, moved_sums, filled, *exchange(slots), lists,
        input_output_aliases={2: 2},
    )
    message = call(
        energy_kernel, shape(MODES * ELEMS_AXIS, WIDTH), [cycle, first, energy, energy],
        moved, change, sums, changed_sums, edge_rows, metric, penalties,
    )
    scalars = swap_blocks(message, ("mode", "elem")).reshape(MODES, ELEMS_AXIS, WIDTH)
    mixed = call(
        combine_kernel, blocks, [pltpu.VMEM((BLOCK, PLANES, LANES), F32)], backward, scalars, column,
        *swap_steps(pairs)
    )
    result = call(
        unpack_kernel, shape(NODES, ROWS, LANES),
        [packing, pltpu.VMEM((NODES, ROWS, LANES), F32), pltpu.SemaphoreType.DMA((3,))],
        *swap_steps(mixed), edge_rows, out_specs=hbm,
    )
    return result.transpose(1, 0, 2)


def solution(mesh):
    placed = (
        P("mode", None, "elem"),
        P(None, None, "elem"),
        P("elem", None),
        P("elem"),
        P("elem"),
        P("elem"),
    )
    return jax.shard_map(
        body, mesh=mesh, in_specs=placed, out_specs=P("mode", None, "elem"), check_vma=False
    )
```

```python
import functools
import math

import jax
import jax.numpy as jnp
import numpy as np
from jax import lax
from jax.experimental import pallas as pl
from jax.experimental.pallas import tpu as pltpu
from jax.sharding import PartitionSpec as P

ORDER = 8
SIDE = ORDER + 1
NODES = SIDE * SIDE
CYCLE = 32
INNER = (ORDER - 1) ** 2
ROWS = 16
LANES = 128
PLANES = 128
MODES = 8
ELEMS_AXIS = 32
SKEL = 2113
LOW = 256
HIGH = 9
TILES = 2 * HIGH
QUADS = -(-HIGH // 4)
SLOTS = 384
SLOT_TILES = SLOTS // LANES
BLOCK = 9
SHARE = BLOCK + SLOT_TILES
LINE = ORDER - 1
PAIRED = BLOCK + 2
SCALARS = 5
STEP_ORDER = [4, 5, 7, 2, 6, 3, 1]
LEVEL_ORDER = [0, 2, 1, 3, 4]
SPACING = 0.25
F32 = jnp.float32
BF16 = jnp.bfloat16
HIGHEST = lax.Precision.HIGHEST
VMEM_LIMIT = 32 * 1024 * 1024
FIRST_LIMIT = 56 * 1024 * 1024


def legendre_table(points, poly_order):
    table = np.zeros((points.shape[0], poly_order + 1))
    table[:, 0] = 1.0
    table[:, 1] = points
    for degree in range(2, poly_order + 1):
        table[:, degree] = (
            (2 * degree - 1) * points * table[:, degree - 1] - (degree - 1) * table[:, degree - 2]
        ) / degree
    return table


def lobatto_derivative(poly_order):
    node_count = poly_order + 1
    points = np.cos(np.pi * np.arange(node_count) / poly_order)
    for newton_step in range(100):
        table = legendre_table(points, poly_order)
        points = points - (points * table[:, poly_order] - table[:, poly_order - 1]) / (
            node_count * table[:, poly_order]
        )
    points = np.sort(points)
    top_values = legendre_table(points, poly_order)[:, poly_order]
    identity = np.eye(node_count)
    differ = points[:, None] - points[None, :] + identity
    matrix = top_values[:, None] / (top_values[None, :] * differ)
    matrix = matrix * (1.0 - identity)
    matrix[0, 0] = -poly_order * node_count / 4.0
    matrix[poly_order, poly_order] = poly_order * node_count / 4.0
    return matrix


def fourier_tables():
    positions = np.arange(PLANES)
    phases = ((positions // 2)[:, None] * positions[None, :] % PLANES) * (2.0 * np.pi / PLANES)
    cosine, sine = np.cos(phases), np.sin(phases)
    even = (positions % 2 == 0)[:, None]
    nyquist = (positions == 1)[:, None]
    alternate = (1.0 - 2.0 * (positions % 2))[None, :]
    forward = np.where(nyquist, alternate, np.where(even, cosine, -sine)) / PLANES
    backward = np.where(nyquist, alternate, np.where(even, 2.0 * cosine, -2.0 * sine))
    backward = np.where((positions == 0)[:, None], 1.0, backward)
    return forward.astype(np.float32), backward.T.astype(np.float32)


DERIVATIVE64 = lobatto_derivative(ORDER)
DERIVATIVE = DERIVATIVE64.astype(np.float32)
CYCLE_NODES = (
    [i * SIDE for i in range(SIDE)]
    + [i * SIDE + ORDER for i in range(SIDE)]
    + [j for j in range(1, ORDER)]
    + [ORDER * SIDE + j for j in range(1, ORDER)]
)
INNER_NODES = [i * SIDE + j for i in range(1, ORDER) for j in range(1, ORDER)]


def diagonal_tables():
    squared = (DERIVATIVE * DERIVATIVE).astype(np.float64)
    first = np.kron(squared.T, np.eye(SIDE))
    second = np.kron(np.eye(SIDE), squared.T)
    corner = np.diagonal(DERIVATIVE)
    cross = 2.0 * np.outer(corner, corner).reshape(NODES, 1)
    cross = np.broadcast_to(cross, (NODES, LANES))
    return np.concatenate([first, second], axis=1).astype(np.float32), cross.astype(np.float32)


def helmholtz_shift(mode):
    rows_global = mode * ROWS + lax.broadcasted_iota(jnp.int32, (ROWS, LANES), 0)
    wavenumber = jnp.right_shift(rows_global, 1).astype(F32)
    spanwise = wavenumber * (2.0 * math.pi / (PLANES * SPACING))
    spanwise = jnp.where(rows_global == 1, math.pi / SPACING, spanwise)
    return spanwise * spanwise


def row_block(index):
    return slice(index * ROWS, (index + 1) * ROWS)


def lane_block(index):
    return slice(index * LANES, (index + 1) * LANES)


def pieces(value):
    top = value.astype(BF16).astype(F32)
    return top, value - top


def one_hot_rows(low_rows):
    sublanes = lax.broadcasted_iota(jnp.int32, (LOW, low_rows.shape[1]), 0).astype(BF16)
    wanted = jnp.broadcast_to(low_rows.astype(BF16), sublanes.shape)
    return jnp.where(wanted == sublanes, BF16(1.0), BF16(0.0))


def masked_store(value, high_row, left_ref, column):
    top, rest = [part.astype(BF16) for part in pieces(value)]
    wanted = jnp.broadcast_to(high_row.astype(BF16), value.shape)
    for high in range(HIGH):
        here = wanted == BF16(high)
        left_ref[row_block(high), lane_block(column)] = jnp.where(here, top, BF16(0.0))
        left_ref[row_block(HIGH + high), lane_block(column)] = jnp.where(here, rest, BF16(0.0))


def contract_lanes(left, right):
    return lax.dot_general(left, right, (((1,), (1,)), ((), ())), preferred_element_type=F32)


def scatter_sum(left, selectors):
    both = contract_lanes(left, selectors)
    return both[: HIGH * ROWS] + both[HIGH * ROWS :]


def one_hot_cycle(edge_rows, selectors_ref):
    low = jnp.bitwise_and(edge_rows, LOW - 1)
    for slot in range(CYCLE):
        selectors_ref[:, lane_block(slot)] = one_hot_rows(low[slot : slot + 1, :])


def scatter_cycle(load, edge_rows, left_ref, selectors_ref):
    high_rows = jnp.right_shift(edge_rows, 8)
    for slot in range(CYCLE):
        masked_store(load(slot), high_rows[slot : slot + 1, :], left_ref, slot)
    return scatter_sum(left_ref[...], selectors_ref[...])


def slot_selectors(shared_rows):
    low = jnp.bitwise_and(shared_rows, LOW - 1)
    return jnp.concatenate(
        [one_hot_rows(low[tile : tile + 1, :]) for tile in range(SLOT_TILES)], axis=1
    )


def four_pieces(first, second):
    sublanes = jnp.bitwise_and(lax.broadcasted_iota(jnp.int32, (ROWS, first.shape[1]), 0), 3)
    first_top, first_rest = pieces(first)
    second_top, second_rest = pieces(second)
    tops = jnp.where(sublanes == 0, first_top, second_top)
    rests = jnp.where(sublanes == 2, first_rest, second_rest)
    return jnp.where(sublanes < 2, tops, rests)


def masked_store_four(value, high_row, left_ref, column):
    packed = value.astype(BF16)
    quarter = jnp.right_shift(lax.broadcasted_iota(jnp.int32, value.shape, 0), 2).astype(BF16)
    wanted = jnp.broadcast_to(high_row.astype(BF16), value.shape) - quarter
    for block in range(QUADS):
        here = wanted == BF16(4 * block)
        left_ref[row_block(block), lane_block(column)] = jnp.where(here, packed, BF16(0.0))


def two_rows(total, high):
    base = 4 * high
    first = total[base : base + 1, :] + total[base + 2 : base + 3, :]
    second = total[base + 1 : base + 2, :] + total[base + 3 : base + 4, :]
    return first, second


def scatter_slots(load, shared_rows, left_ref, right):
    high_rows = jnp.right_shift(shared_rows, 8)
    for tile in range(SLOT_TILES):
        masked_store(load(tile), high_rows[tile : tile + 1, :], left_ref, tile)
    return scatter_sum(left_ref[:, :SLOTS], right)


def stack_pieces(skeleton):
    top, rest = pieces(skeleton)
    return jnp.concatenate([top.astype(BF16), rest.astype(BF16)], axis=0)


def gather_tile(stacked, rows, keep=None):
    low = jnp.bitwise_and(rows, LOW - 1)
    high = jnp.right_shift(rows, 8)
    selector = one_hot_rows(low)
    if keep is not None:
        keep(selector)
    found = jnp.dot(stacked, selector, preferred_element_type=F32)
    total = None
    for index in range(HIGH):
        part = found[row_block(index), :] + found[row_block(HIGH + index), :]
        part = jnp.where(high == index, part, 0.0)
        total = part if total is None else total + part
    return total


def keep_columns(selectors_ref, column, selector):
    selectors_ref[:, column * LANES : (column + 2) * LANES] = selector


def gather_cycle(skeleton, edge_rows, store, selectors_ref=None):
    stacked = stack_pieces(skeleton)
    for pair in range(CYCLE // 2):
        rows = jnp.concatenate(
            [edge_rows[2 * pair : 2 * pair + 1, :], edge_rows[2 * pair + 1 : 2 * pair + 2, :]], axis=1
        )
        keep = None
        if selectors_ref is not None:
            keep = functools.partial(keep_columns, selectors_ref, 2 * pair)
        total = gather_tile(stacked, rows, keep)
        store(2 * pair, total[:, :LANES])
        store(2 * pair + 1, total[:, LANES:])


def gather_slots(skeleton, shared_rows):
    stacked = stack_pieces(skeleton)
    return [gather_tile(stacked, shared_rows[tile : tile + 1, :]) for tile in range(SLOT_TILES)]


def sent_place(index):
    if index < INNER:
        return index // LINE, index % LINE
    extra = index - INNER
    block = min(extra // 2, MODES - 1)
    row = extra - 2 * block
    return block, row + LINE if row < 2 else row - 2


def kept_place(index):
    block, row = sent_place(index)
    return block, row + 2


EMPTY_PLACES = [(MODES - 1, row) for row in range(2, LINE)]


def read_skeleton(load):
    return jnp.concatenate(
        [jnp.concatenate([load(2 * high), load(2 * high + 1)], axis=1) for high in range(HIGH)], axis=0
    )


def write_skeleton(skeleton, store):
    for high in range(HIGH):
        store(2 * high, skeleton[row_block(high), :LANES])
        store(2 * high + 1, skeleton[row_block(high), LANES:])


def write_place(ref, place):
    def store(index, value):
        block, row = place(index)
        ref[block, row] = value

    return store


def fold(value):
    return value[:, :LANES] + value[:, LANES:]


def per_tile(penalty_ref):
    return jnp.concatenate(
        [jnp.broadcast_to(penalty_ref[high : high + 1, :], (ROWS, LOW)) for high in range(HIGH)], axis=0
    )


def skeleton_sum(product):
    total = None
    for high in range(HIGH):
        part = fold(product[row_block(high), :])
        total = part if total is None else total + part
    return total


def select_arrived(masks, tile, arrived):
    chosen = arrived[0]
    row = masks[tile : tile + 1, :]
    for level in range(1, len(arrived)):
        moving = jnp.bitwise_and(jnp.right_shift(row, level), 1) == 1
        chosen = jnp.where(moving, arrived[level], chosen)
    return chosen


def weighted_sum(weights, values):
    total = None
    for weight, value in zip(weights, values):
        if weight == 0.0:
            continue
        part = float(weight) * value
        total = part if total is None else total + part
    return total


def derivative_line(values, transposed):
    matrix = DERIVATIVE64.T if transposed else DERIVATIVE64
    half = SIDE // 2
    evens = [values[k] + values[ORDER - k] for k in range(half)] + [values[half]]
    odds = [values[k] - values[ORDER - k] for k in range(half)]
    results = [None] * SIDE
    for out in range(half):
        near, far = matrix[out, :half], matrix[out, :half:-1]
        even = weighted_sum(np.float32(np.append(0.5 * (near + far), matrix[out, half])), evens)
        odd = weighted_sum(np.float32(0.5 * (near - far)), odds)
        results[out] = odd + even
        results[ORDER - out] = odd - even
    results[half] = weighted_sum(np.float32(matrix[half, :half]), odds)
    return results


def grid_load(inner_ref, cycle_ref, rows):
    def load(node):
        if node in CYCLE_NODES:
            return cycle_ref[CYCLE_NODES.index(node), rows, :]
        return inner_ref[INNER_NODES.index(node), rows, :]

    return load


def gradients(load, first_ref, metric_ref, rows, visit):
    for j in range(SIDE):
        line = derivative_line([load(k * SIDE + j) for k in range(SIDE)], False)
        for i in range(SIDE):
            first_ref[i * SIDE + j, rows, :] = line[i]
    for i in range(SIDE):
        line = derivative_line([load(i * SIDE + k) for k in range(SIDE)], False)
        seconds = []
        for j in range(SIDE):
            node = i * SIDE + j
            m0, m1, m2 = [metric_ref[node, c : c + 1, :] for c in range(3)]
            g1, g2 = first_ref[node, rows, :], line[j]
            p1 = m0 * g1 + m2 * g2
            p2 = m2 * g1 + m1 * g2
            visit(node, g1, g2, p1, p2)
            seconds.append(p2)
        yield i, seconds


def apply_operator(inner_ref, cycle_ref, result_ref, first_ref, energy_ref, metric_ref, shift_ref):
    for part in range(2):
        rows = slice(part * 8, part * 8 + 8)
        shift = shift_ref[rows, :]
        load = grid_load(inner_ref, cycle_ref, rows)

        def visit(node, g1, g2, p1, p2):
            first_ref[node, rows, :] = p1

        for i, seconds in gradients(load, first_ref, metric_ref, rows, visit):
            line = derivative_line(seconds, True)
            for j in range(SIDE):
                node = i * SIDE + j
                mass = shift * metric_ref[node, 3:4, :]
                result_ref[node, rows, :] = line[j] + mass * load(node)
        energy = jnp.zeros((8, LANES), F32)
        for j in range(SIDE):
            line = derivative_line([first_ref[k * SIDE + j, rows, :] for k in range(SIDE)], True)
            for i in range(SIDE):
                node = i * SIDE + j
                value = result_ref[node, rows, :] + line[i]
                result_ref[node, rows, :] = value
                energy = energy + value * load(node)
        energy_ref[rows, :] = energy


def apply_energy(inner_ref, cycle_ref, first_ref, energy_ref, metric_ref, shift_ref):
    for part in range(2):
        rows = slice(part * 8, part * 8 + 8)
        shift = shift_ref[rows, :]
        load = grid_load(inner_ref, cycle_ref, rows)
        sums = [jnp.zeros((8, LANES), F32)]

        def visit(node, g1, g2, p1, p2):
            value = load(node)
            mass = shift * metric_ref[node, 3:4, :]
            sums[0] = sums[0] + (g1 * p1 + g2 * p2 + mass * value * value)

        for i, seconds in gradients(load, first_ref, metric_ref, rows, visit):
            pass
        energy_ref[rows, :] = sums[0]


def diagonal_cells(metric_ref, table_ref, cross_ref, penalty_ref, inner_ref, padded_ref, cells_ref):
    both = jnp.concatenate([metric_ref[:, 0, :], metric_ref[:, 1, :]], axis=0)
    terms = jnp.dot(table_ref[...], both, precision=HIGHEST, preferred_element_type=F32)
    cells_ref[0] = terms + cross_ref[...] * metric_ref[:, 2, :]
    cells_ref[1] = metric_ref[:, 3, :]
    padded_ref[...] = jnp.ones((HIGH, LOW), F32)
    for high in range(HIGH):
        count = min(LOW, SKEL - high * LOW)
        line = penalty_ref[pl.ds(high * LOW, count)]
        padded_ref[high : high + 1, :count] = line.reshape(1, count)
    for index, node in enumerate(INNER_NODES):
        inner_ref[0, index : index + 1, :] = cells_ref[0, node : node + 1, :]
        inner_ref[1, index : index + 1, :] = cells_ref[1, node : node + 1, :]


def diagonal_slots(total, shared_rows, selectors, padded_ref, skeleton_ref):
    stacked = []
    for high in range(HIGH):
        laplace, mass = two_rows(total, high)
        laplace = laplace + padded_ref[high : high + 1, :]
        skeleton_ref[0, high : high + 1, :] = laplace
        skeleton_ref[1, high : high + 1, :] = mass
        stacked.append(four_pieces(laplace, mass).astype(BF16))
    stacked = jnp.concatenate(stacked, axis=0)
    results = []
    for tile in range(SLOT_TILES):
        high_row = jnp.right_shift(shared_rows[tile : tile + 1, :], 8)
        found = jnp.dot(stacked, selectors[:, lane_block(tile)], preferred_element_type=F32)
        value = jnp.zeros((ROWS, LANES), F32)
        for high in range(HIGH):
            value = value + jnp.where(high_row == high, found[row_block(high), :], 0.0)
        results.append(two_rows(value, 0))
    return results


def pack_kernel(
    forcing_hbm, edge_hbm, shared_hbm, masks_hbm, metric_hbm, penalty_hbm, table_hbm, cross_hbm,
    out_hbm, message_hbm, inner_hbm, skeleton_hbm, padded_hbm, lists_hbm,
    forcing_ref, edge_ref, shared_ref, masks_ref, metric_ref, penalty_ref, table_ref, cross_ref,
    packed_ref, message_ref, inner_ref, skeleton_ref, padded_ref, lists_ref,
    cells_ref, left_ref, selectors_ref, in_semaphores, out_semaphores,
):
    ins = [
        pltpu.make_async_copy(source, target, in_semaphores.at[index])
        for index, (source, target) in enumerate(
            [
                (edge_hbm, edge_ref), (metric_hbm, metric_ref), (table_hbm, table_ref), (cross_hbm, cross_ref),
                (penalty_hbm, penalty_ref), (shared_hbm, shared_ref), (masks_hbm, masks_ref),
                (forcing_hbm, forcing_ref),
            ]
        )
    ]
    for copy in ins:
        copy.start()
    outs = []

    def send(source, target):
        copy = pltpu.make_async_copy(source, target, out_semaphores.at[len(outs)])
        copy.start()
        outs.append(copy)

    base = 2 * HIGH * ROWS
    tail = list(range(TILES - 4)) + [TILES - 2, TILES - 1] + [None] * len(EMPTY_PLACES) + [TILES - 4, TILES - 3]
    for position, index in enumerate(tail):
        if index is None:
            packed_ref[position] = jnp.zeros((ROWS, LANES), F32)
    ins[0].wait()
    edge_rows = edge_ref[...]
    one_hot_cycle(edge_rows, selectors_ref)
    for copy in ins[1:7]:
        copy.wait()
    shared_rows = shared_ref[...]
    lists_ref[:SLOT_TILES, :] = shared_rows
    lists_ref[SLOT_TILES : 2 * SLOT_TILES, :] = masks_ref[...]
    lists_ref[2 * SLOT_TILES :, :] = jnp.zeros((8 - 2 * SLOT_TILES, LANES), jnp.int32)
    send(lists_ref, lists_hbm)
    diagonal_cells(metric_ref, table_ref, cross_ref, penalty_ref, inner_ref, padded_ref, cells_ref)
    send(inner_ref, inner_hbm)
    send(padded_ref, padded_hbm)
    ins[7].wait()
    for line in range(LINE):
        send(forcing_ref.at[pl.ds((line + 1) * SIDE + 1, LINE)], out_hbm.at[pl.ds(line * BLOCK, LINE)])
    high_rows = jnp.right_shift(edge_rows, 8)
    for slot in range(CYCLE):
        node = CYCLE_NODES[slot]
        high_row = high_rows[slot : slot + 1, :]
        masked_store(forcing_ref[node], high_row, left_ref, slot)
        value = four_pieces(cells_ref[0, node : node + 1, :], cells_ref[1, node : node + 1, :])
        masked_store_four(value, high_row, left_ref.at[pl.ds(base, QUADS * ROWS)], slot)
    total = contract_lanes(left_ref[...], selectors_ref[...])
    skeleton = total[: HIGH * ROWS] + total[HIGH * ROWS : base]

    def store(index, value):
        packed_ref[tail.index(index)] = value

    write_skeleton(skeleton, store)
    for line in range(LINE):
        send(packed_ref.at[pl.ds(2 * line, 2)], out_hbm.at[pl.ds(line * BLOCK + LINE, 2)])
    send(packed_ref.at[pl.ds(TILES - 4, BLOCK)], out_hbm.at[pl.ds(LINE * BLOCK, BLOCK)])
    selectors = slot_selectors(shared_rows)
    pairs = diagonal_slots(total[base:], shared_rows, selectors, padded_ref, skeleton_ref)
    send(skeleton_ref, skeleton_hbm)
    for tile, value in enumerate(gather_slots(skeleton, shared_rows)):
        laplace, mass = pairs[tile]
        message_ref[tile, :ROWS, :] = value
        message_ref[tile, ROWS:, :] = jnp.zeros((8, LANES), F32)
        message_ref[tile, ROWS : ROWS + 1, :] = laplace
        message_ref[tile, ROWS + 1 : ROWS + 2, :] = mass
    send(message_ref, message_hbm)
    for copy in outs:
        copy.wait()


def place(index):
    return pl.ds(pl.multiple_of(index * ROWS, ROWS), ROWS)


def relative_rows(matrix_ref, mode):
    parts = [matrix_ref[place(jnp.bitwise_xor(mode, step)), :] for step in range(MODES)]
    return jnp.concatenate(parts, axis=0)


def transform_kernel(
    matrix_ref, in_ref, a0, a2, a1, a3, a4, lists_ref, o0, o1, o2, o3, o4, o5, o6, o7, extra_ref, slots_ref
):
    mode = lax.axis_index("mode")
    outs = [o0, o1, o2, o3, o4, o5, o6, o7]
    matrix = relative_rows(matrix_ref, mode)
    slots_ref[...] = jnp.zeros(slots_ref.shape, F32)
    arrived_refs = [a0, a1, a2, a3, a4]
    masks = lists_ref[SLOT_TILES : 2 * SLOT_TILES, :]
    for index in range(BLOCK):
        block = in_ref[:, index].reshape(PLANES, LANES)
        mixed = jnp.dot(matrix, block, precision=HIGHEST, preferred_element_type=F32)
        for step, out_ref in enumerate(outs):
            out_ref[index] = mixed[row_block(step), :]
    for tile in range(SLOT_TILES):
        chosen = select_arrived(masks, tile, [ref[tile] for ref in arrived_refs])
        slots_ref[tile, place(mode), :] = chosen[:ROWS]
        mixed = jnp.dot(matrix, slots_ref[tile], precision=HIGHEST, preferred_element_type=F32)
        for step, out_ref in enumerate(outs):
            out_ref[BLOCK + tile] = mixed[row_block(step), :]
        extra_ref[tile] = chosen[ROWS:]


def column_kernel(inner_ref, o0, o1, o2, o3, o4, o5, o6, o7, out_ref):
    mode = lax.axis_index("mode")
    start = jnp.minimum(mode, LINE - 1) * LINE
    for step, in_ref in enumerate([o0, o1, o2, o3, o4, o5, o6, o7]):
        origin = jnp.bitwise_xor(mode, step)
        shift = helmholtz_shift(origin)
        for index in range(LINE):
            laplace = inner_ref[0, pl.ds(start + index, 1), :]
            mass = inner_ref[1, pl.ds(start + index, 1), :]
            out_ref[index, place(origin), :] = in_ref[index] * (1.0 / (laplace + shift * mass))


def first_kernel(
    i4, i5, i7, i2, i6, i3, i1, i0, extra_ref, lists_ref, edge_ref, metric_ref,
    inner_ref, diagonal_ref, penalty_ref, search_ref, inverse_ref, result_ref, source_ref, kept_ref, slots_ref,
    sums_ref, left_ref, right_ref, cycle_ref, first_ref, energy_ref, shift_ref,
):
    mode = lax.axis_index("mode")
    ins = [i0, i1, i2, i3, i4, i5, i6, i7]
    for step, in_ref in enumerate(ins):
        source_ref[jnp.bitwise_xor(mode, step)] = in_ref[:BLOCK]
    shared_rows = lists_ref[:SLOT_TILES, :]
    right_slots = slot_selectors(shared_rows)
    shift = helmholtz_shift(lax.axis_index("mode"))
    shift_ref[...] = shift
    edge_rows = edge_ref[...]

    def load_right(tile):
        total = ins[0][BLOCK + tile]
        for in_ref in ins[1:]:
            total = total + in_ref[BLOCK + tile]
        return total

    def source(index):
        block, row = sent_place(index)
        return source_ref[block, row]

    high_rows = jnp.right_shift(shared_rows, 8)
    for tile in range(SLOT_TILES):
        value = four_pieces(extra_ref[tile, 0:1, :], extra_ref[tile, 1:2, :])
        masked_store_four(value, high_rows[tile : tile + 1, :], left_ref, tile)
    added = contract_lanes(left_ref[: QUADS * ROWS, :SLOTS], right_slots)
    wide_shift = jnp.concatenate([shift, shift], axis=1)
    parts = []
    for high in range(HIGH):
        laplace, mass = two_rows(added, high)
        laplace = laplace + diagonal_ref[0, high : high + 1, :]
        mass = mass + diagonal_ref[1, high : high + 1, :]
        parts.append(1.0 / (laplace + wide_shift * mass))
    inverse = jnp.concatenate(parts, axis=0)
    local = read_skeleton(lambda index: source(INNER + index))
    right_side = local + scatter_slots(load_right, shared_rows, left_ref, right_slots)
    search = right_side * inverse
    kept_ref[0] = local
    kept_ref[1] = inverse
    kept_ref[2] = search
    start = skeleton_sum(local * search)
    for index, node in enumerate(INNER_NODES):
        value = source(index)
        inverted = 1.0 / (inner_ref[0, index : index + 1, :] + shift * inner_ref[1, index : index + 1, :])
        scaled = value * inverted
        search_ref[index] = scaled
        inverse_ref[index] = inverted
        start = start + value * scaled

    def store(slot, value):
        cycle_ref[slot] = value

    gather_cycle(search, edge_rows, store, right_ref)
    apply_operator(search_ref, cycle_ref, result_ref, first_ref, energy_ref, metric_ref, shift_ref)
    weighted = per_tile(penalty_ref) * search
    applied = weighted + scatter_cycle(
        lambda slot: result_ref[CYCLE_NODES[slot]], edge_rows, left_ref, right_ref
    )
    kept_ref[3] = applied
    for tile, value in enumerate(gather_slots(applied, shared_rows)):
        slots_ref[tile] = value
    sums_ref[0] = energy_ref[...] + skeleton_sum(weighted * search)
    sums_ref[1] = start


def change_kernel(search_ref, inverse_ref, result_ref, source_ref, kept_ref, moved_ref, sums_ref, both_ref):
    crossed = jnp.zeros((ROWS, LANES), F32)
    sourced = jnp.zeros((ROWS, LANES), F32)
    for index, node in enumerate(INNER_NODES):
        block, row = sent_place(index)
        value = result_ref[node]
        search = search_ref[index]
        moved = value * inverse_ref[index] - search
        moved_ref[index] = moved
        both_ref[block, row] = moved
        crossed = crossed + value * moved
        sourced = sourced + source_ref[block, row] * moved
    for high in range(HIGH):
        for part in range(2):
            block, row = kept_place(INNER + 2 * high + part)
            both_ref[block, row] = kept_ref[2, row_block(high), lane_block(part)]
    for block, row in EMPTY_PLACES[2:]:
        both_ref[block, row] = jnp.zeros((ROWS, LANES), F32)
    sums_ref[0] = crossed
    sums_ref[1] = sourced


def second_kernel(
    kept_ref, moved_sums_ref, filled_ref, a0, a2, a1, a3, a4, lists_ref,
    change_ref, sums_ref, both_ref, o0, o1, o2, o3, o4, o5, o6, o7, left_ref,
):
    arrived_refs = [a0, a1, a2, a3, a4]
    masks = lists_ref[SLOT_TILES : 2 * SLOT_TILES, :]
    shared_rows = lists_ref[:SLOT_TILES, :]

    def load(tile):
        return select_arrived(masks, tile, [ref[tile] for ref in arrived_refs])

    local, inverse, search, applied = [kept_ref[index] for index in range(4)]
    full = applied + scatter_slots(load, shared_rows, left_ref, slot_selectors(shared_rows))
    change = full * inverse - search
    for high in range(HIGH):
        for part in range(2):
            block, row = sent_place(INNER + 2 * high + part)
            both_ref[block, row] = change[row_block(high), lane_block(part)]
    mode = lax.axis_index("mode")
    for step, out_ref in enumerate([o0, o1, o2, o3, o4, o5, o6, o7]):
        out_ref[...] = both_ref[jnp.bitwise_xor(mode, step)]
    change_ref[...] = change
    sums_ref[0] = moved_sums_ref[0] + skeleton_sum(applied * change)
    sums_ref[1] = moved_sums_ref[1] + skeleton_sum(local * change)


def energy_kernel(
    moved_ref, change_ref, sums_ref, changed_sums_ref, edge_ref, metric_ref, penalty_ref, message_ref,
    cycle_ref, first_ref, energy_ref, shift_ref,
):
    shift_ref[...] = helmholtz_shift(lax.axis_index("mode"))
    change = change_ref[...]

    def store(slot, value):
        cycle_ref[slot] = value

    gather_cycle(change, edge_ref[...], store)
    apply_energy(moved_ref, cycle_ref, first_ref, energy_ref, metric_ref, shift_ref)
    energy = energy_ref[...] + skeleton_sum(per_tile(penalty_ref) * change * change)
    sublanes = lax.broadcasted_iota(jnp.int32, (ROWS, LANES), 0)
    lanes = lax.broadcasted_iota(jnp.int32, (ROWS, LANES), 1)
    spread = jnp.zeros((ROWS, LANES), F32)
    for index, value in enumerate([sums_ref[0], changed_sums_ref[0], energy, sums_ref[1], changed_sums_ref[1]]):
        column = jnp.sum(value, axis=1, keepdims=True)
        spread = jnp.where(lanes == sublanes + index * ROWS, column, spread)
    message = jnp.sum(spread, axis=0, keepdims=True)
    message_ref[...] = jnp.broadcast_to(message, message_ref.shape)


def combine_kernel(
    matrix_ref, scalars_ref, column_ref, i4, i5, i7, i2, i6, i3, i1, i0, o0, o1, o2, o3, o4, o5, o6, o7, block_ref
):
    mode = lax.axis_index("mode")
    sublanes = lax.broadcasted_iota(jnp.int32, (ROWS, LANES), 0)
    lanes = lax.broadcasted_iota(jnp.int32, (ROWS, LANES), 1)
    for step, in_ref in enumerate([i0, i1, i2, i3, i4, i5, i6, i7]):
        origin = jnp.bitwise_xor(mode, step)
        total = jnp.sum(scalars_ref[origin], axis=0, keepdims=True)
        g00, g01, g11, h0, h1 = [
            jnp.sum(jnp.where(lanes == sublanes + index * ROWS, total, 0.0), axis=1, keepdims=True)
            for index in range(SCALARS)
        ]
        ratio = g01 / g00
        pivot = g11 - ratio * g01
        second = jnp.where(pivot > 0.0, (h1 - ratio * h0) / pivot, 0.0)
        first = h0 / g00 - ratio * second
        for index in range(BLOCK):
            if index < LINE:
                search = column_ref[index, place(origin), :]
                if index < 2:
                    search = jnp.where(mode == MODES - 1, in_ref[index + 2], search)
            else:
                search = in_ref[index + 2]
            block_ref[index, place(origin), :] = first * search + second * in_ref[index]
    matrix = relative_rows(matrix_ref, mode)
    for index in range(BLOCK):
        mixed = jnp.dot(matrix, block_ref[index], precision=HIGHEST, preferred_element_type=F32)
        for step, out_ref in enumerate([o0, o1, o2, o3, o4, o5, o6, o7]):
            out_ref[index] = mixed[row_block(step), :]


def unpack_kernel(
    i4, i5, i7, i2, i6, i3, i1, i0, edge_ref, out_hbm, packed_ref, out_ref, semaphores
):
    mode = lax.axis_index("mode")
    for step, in_ref in enumerate([i0, i1, i2, i3, i4, i5, i6, i7]):
        packed_ref[jnp.bitwise_xor(mode, step)] = in_ref[...]

    def load(index):
        block, row = sent_place(index)
        return packed_ref[block, row]

    for index, node in enumerate(INNER_NODES):
        out_ref[node] = load(index)
    spans = [(SIDE, (SIDE - 2) * SIDE), (0, SIDE), (ORDER * SIDE, SIDE)]
    copies = [
        pltpu.make_async_copy(out_ref.at[pl.ds(*span)], out_hbm.at[pl.ds(*span)], semaphores.at[index])
        for index, span in enumerate(spans)
    ]

    def store(slot, value):
        out_ref[CYCLE_NODES[slot]] = value
        if slot == 2 * SIDE - 1:
            copies[0].start()
        if slot == CYCLE - 1:
            copies[1].start()
            copies[2].start()

    gather_cycle(read_skeleton(lambda index: load(INNER + index)), edge_ref[...], store)
    for copy in copies:
        copy.wait()


def call(kernel, out_shapes, scratch, *operands, limit=VMEM_LIMIT, **options):
    return pl.pallas_call(
        kernel,
        out_shape=out_shapes,
        scratch_shapes=scratch,
        compiler_params=pltpu.CompilerParams(vmem_limit_bytes=limit),
        **options,
    )(*operands)


def shape(*dims, dtype=F32):
    return jax.ShapeDtypeStruct(dims, dtype)


def swap_blocks(blocks, axis):
    return lax.all_to_all(blocks, axis, split_axis=0, concat_axis=0, tiled=True)


def permute(value, axis, flip):
    return lax.ppermute(value, axis, [(i, i ^ flip) for i in range(lax.axis_size(axis))])


def swap_steps(blocks):
    return [permute(blocks[step], "mode", step) for step in STEP_ORDER] + [blocks[0]]


def exchange(slots):
    return [permute(slots, "elem", 1 << level) for level in LEVEL_ORDER]


def body(forcing, metric, edge_map, shared_rows, partner_masks, penalty):
    forward, backward = [jnp.asarray(part) for part in fourier_tables()]
    table, cross = [jnp.asarray(part) for part in diagonal_tables()]
    metric = metric.transpose(1, 0, 2)
    edge_rows = edge_map.T
    shared = shared_rows.reshape(SLOT_TILES, LANES)
    masks = partner_masks.reshape(SLOT_TILES, LANES)
    left = pltpu.VMEM((2 * HIGH * ROWS, CYCLE * LANES), BF16)
    right = pltpu.VMEM((LOW, CYCLE * LANES), BF16)
    left_slots = pltpu.VMEM((2 * HIGH * ROWS, SLOTS), BF16)
    cycle = pltpu.VMEM((CYCLE, ROWS, LANES), F32)
    first = pltpu.VMEM((NODES, ROWS, LANES), F32)
    energy = pltpu.VMEM((ROWS, LANES), F32)
    packing = pltpu.VMEM((MODES, BLOCK, ROWS, LANES), F32)
    wide = (HIGH * ROWS, LOW)
    blocks = [shape(BLOCK, ROWS, LANES)] * MODES

    hbm = pl.BlockSpec(memory_space=pltpu.HBM)
    packed_shapes = [
        shape(MODES * BLOCK, ROWS, LANES), shape(SLOT_TILES, ROWS + 8, LANES),
        shape(2, INNER, LANES), shape(2, HIGH, LOW), shape(HIGH, LOW), shape(8, LANES, dtype=jnp.int32),
    ]
    operands = [forcing.transpose(1, 0, 2), edge_rows, shared, masks, metric, penalty, table, cross]
    packed, message, inner, diagonal, penalties, lists = call(
        pack_kernel, packed_shapes,
        [pltpu.VMEM(operand.shape, operand.dtype) for operand in operands]
        + [pltpu.VMEM((MODES * BLOCK - INNER, ROWS, LANES), F32)]
        + [pltpu.VMEM(part.shape, part.dtype) for part in packed_shapes[1:]]
        + [
            pltpu.VMEM((2, NODES, LANES), F32), pltpu.VMEM(((2 * HIGH + QUADS) * ROWS, CYCLE * LANES), BF16), right,
            pltpu.SemaphoreType.DMA((len(operands),)), pltpu.SemaphoreType.DMA((2 * LINE + 6,)),
        ],
        *operands,
        in_specs=[hbm] * len(operands), out_specs=[hbm] * len(packed_shapes), limit=FIRST_LIMIT,
    )
    gathered = swap_blocks(packed.reshape(MODES, BLOCK, ROWS, LANES), "mode")
    *mixed, extra = call(
        transform_kernel, [shape(SHARE, ROWS, LANES)] * MODES + [shape(SLOT_TILES, 8, LANES)],
        [pltpu.VMEM((SLOT_TILES, PLANES, LANES), F32)], forward, gathered, *exchange(message), lists,
    )
    column = call(column_kernel, shape(LINE, PLANES, LANES), [], inner, *mixed)
    inside = shape(INNER, ROWS, LANES)
    search, inverse, applied, source, kept, slots, sums = call(
        first_kernel,
        [
            inside, inside, shape(NODES, ROWS, LANES), shape(MODES, BLOCK, ROWS, LANES), shape(4, *wide),
            shape(SLOT_TILES, ROWS, LANES), shape(2, ROWS, LANES),
        ],
        [left, right, cycle, first, energy, energy],
        *swap_steps(mixed), extra, lists, edge_rows, metric, inner, diagonal, penalties,
    )
    pair = shape(MODES, PAIRED, ROWS, LANES)
    moved, moved_sums, filled = call(
        change_kernel, [inside, shape(2, ROWS, LANES), pair], [], search, inverse, applied, source, kept
    )
    change, changed_sums, both, *pairs = call(
        second_kernel,
        [shape(*wide), shape(2, ROWS, LANES), pair] + [shape(PAIRED, ROWS, LANES)] * MODES,
        [left_slots],
        kept, moved_sums, filled, *exchange(slots), lists,
        input_output_aliases={2: 2},
    )
    message = call(
        energy_kernel, shape(MODES * ELEMS_AXIS, LANES), [cycle, first, energy, energy],
        moved, change, sums, changed_sums, edge_rows, metric, penalties,
    )
    scalars = swap_blocks(message, ("mode", "elem")).reshape(MODES, ELEMS_AXIS, LANES)
    mixed = call(
        combine_kernel, blocks, [pltpu.VMEM((BLOCK, PLANES, LANES), F32)], backward, scalars, column,
        *swap_steps(pairs)
    )
    result = call(
        unpack_kernel, shape(NODES, ROWS, LANES),
        [packing, pltpu.VMEM((NODES, ROWS, LANES), F32), pltpu.SemaphoreType.DMA((3,))],
        *swap_steps(mixed), edge_rows, out_specs=hbm,
    )
    return result.transpose(1, 0, 2)


def solution(mesh):
    placed = (
        P("mode", None, "elem"),
        P(None, None, "elem"),
        P("elem", None),
        P("elem"),
        P("elem"),
        P("elem"),
    )
    return jax.shard_map(
        body, mesh=mesh, in_specs=placed, out_specs=P("mode", None, "elem"), check_vma=False
    )
```

```python
import functools
import math

import jax
import jax.numpy as jnp
import numpy as np
from jax import lax
from jax.experimental import pallas as pl
from jax.experimental.pallas import tpu as pltpu
from jax.sharding import PartitionSpec as P

ORDER = 8
SIDE = ORDER + 1
NODES = SIDE * SIDE
CYCLE = 32
INNER = (ORDER - 1) ** 2
ROWS = 16
LANES = 128
PLANES = 128
MODES = 8
ELEMS_AXIS = 32
SKEL = 2113
LOW = 256
HIGH = 9
TILES = 2 * HIGH
QUADS = -(-HIGH // 4)
SLOTS = 384
SLOT_TILES = SLOTS // LANES
BLOCK = 9
SHARE = BLOCK + SLOT_TILES
LINE = ORDER - 1
PAIRED = BLOCK + 2
SCALARS = 5
STEP_ORDER = [4, 7, 5, 2, 6, 3, 1]
LEVEL_ORDER = [0, 2, 1, 3, 4]
SPACING = 0.25
F32 = jnp.float32
BF16 = jnp.bfloat16
HIGHEST = lax.Precision.HIGHEST
VMEM_LIMIT = 32 * 1024 * 1024
FIRST_LIMIT = 56 * 1024 * 1024


def legendre_table(points, poly_order):
    table = np.zeros((points.shape[0], poly_order + 1))
    table[:, 0] = 1.0
    table[:, 1] = points
    for degree in range(2, poly_order + 1):
        table[:, degree] = (
            (2 * degree - 1) * points * table[:, degree - 1] - (degree - 1) * table[:, degree - 2]
        ) / degree
    return table


def lobatto_derivative(poly_order):
    node_count = poly_order + 1
    points = np.cos(np.pi * np.arange(node_count) / poly_order)
    for newton_step in range(100):
        table = legendre_table(points, poly_order)
        points = points - (points * table[:, poly_order] - table[:, poly_order - 1]) / (
            node_count * table[:, poly_order]
        )
    points = np.sort(points)
    top_values = legendre_table(points, poly_order)[:, poly_order]
    identity = np.eye(node_count)
    differ = points[:, None] - points[None, :] + identity
    matrix = top_values[:, None] / (top_values[None, :] * differ)
    matrix = matrix * (1.0 - identity)
    matrix[0, 0] = -poly_order * node_count / 4.0
    matrix[poly_order, poly_order] = poly_order * node_count / 4.0
    return matrix


def fourier_tables():
    positions = np.arange(PLANES)
    phases = ((positions // 2)[:, None] * positions[None, :] % PLANES) * (2.0 * np.pi / PLANES)
    cosine, sine = np.cos(phases), np.sin(phases)
    even = (positions % 2 == 0)[:, None]
    nyquist = (positions == 1)[:, None]
    alternate = (1.0 - 2.0 * (positions % 2))[None, :]
    forward = np.where(nyquist, alternate, np.where(even, cosine, -sine)) / PLANES
    backward = np.where(nyquist, alternate, np.where(even, 2.0 * cosine, -2.0 * sine))
    backward = np.where((positions == 0)[:, None], 1.0, backward)
    return forward.astype(np.float32), backward.T.astype(np.float32)


DERIVATIVE64 = lobatto_derivative(ORDER)
DERIVATIVE = DERIVATIVE64.astype(np.float32)
CYCLE_NODES = (
    [i * SIDE for i in range(SIDE)]
    + [i * SIDE + ORDER for i in range(SIDE)]
    + [j for j in range(1, ORDER)]
    + [ORDER * SIDE + j for j in range(1, ORDER)]
)
INNER_NODES = [i * SIDE + j for i in range(1, ORDER) for j in range(1, ORDER)]


def diagonal_tables():
    squared = (DERIVATIVE * DERIVATIVE).astype(np.float64)
    first = np.kron(squared.T, np.eye(SIDE))
    second = np.kron(np.eye(SIDE), squared.T)
    corner = np.diagonal(DERIVATIVE)
    cross = 2.0 * np.outer(corner, corner).reshape(NODES, 1)
    cross = np.broadcast_to(cross, (NODES, LANES))
    return np.concatenate([first, second], axis=1).astype(np.float32), cross.astype(np.float32)


def helmholtz_shift(mode):
    rows_global = mode * ROWS + lax.broadcasted_iota(jnp.int32, (ROWS, LANES), 0)
    wavenumber = jnp.right_shift(rows_global, 1).astype(F32)
    spanwise = wavenumber * (2.0 * math.pi / (PLANES * SPACING))
    spanwise = jnp.where(rows_global == 1, math.pi / SPACING, spanwise)
    return spanwise * spanwise


def row_block(index):
    return slice(index * ROWS, (index + 1) * ROWS)


def lane_block(index):
    return slice(index * LANES, (index + 1) * LANES)


def pieces(value):
    top = value.astype(BF16).astype(F32)
    return top, value - top


def one_hot_rows(low_rows):
    sublanes = lax.broadcasted_iota(jnp.int32, (LOW, low_rows.shape[1]), 0).astype(BF16)
    wanted = jnp.broadcast_to(low_rows.astype(BF16), sublanes.shape)
    return jnp.where(wanted == sublanes, BF16(1.0), BF16(0.0))


def masked_store(value, high_row, left_ref, column):
    top, rest = [part.astype(BF16) for part in pieces(value)]
    wanted = jnp.broadcast_to(high_row.astype(BF16), value.shape)
    for high in range(HIGH):
        here = wanted == BF16(high)
        left_ref[row_block(high), lane_block(column)] = jnp.where(here, top, BF16(0.0))
        left_ref[row_block(HIGH + high), lane_block(column)] = jnp.where(here, rest, BF16(0.0))


def contract_lanes(left, right):
    return lax.dot_general(left, right, (((1,), (1,)), ((), ())), preferred_element_type=F32)


def scatter_sum(left, selectors):
    both = contract_lanes(left, selectors)
    return both[: HIGH * ROWS] + both[HIGH * ROWS :]


def one_hot_cycle(edge_rows, selectors_ref):
    low = jnp.bitwise_and(edge_rows, LOW - 1)
    for slot in range(CYCLE):
        selectors_ref[:, lane_block(slot)] = one_hot_rows(low[slot : slot + 1, :])


def scatter_cycle(load, edge_rows, left_ref, selectors_ref):
    high_rows = jnp.right_shift(edge_rows, 8)
    for slot in range(CYCLE):
        masked_store(load(slot), high_rows[slot : slot + 1, :], left_ref, slot)
    return scatter_sum(left_ref[...], selectors_ref[...])


def slot_selectors(shared_rows):
    low = jnp.bitwise_and(shared_rows, LOW - 1)
    return jnp.concatenate(
        [one_hot_rows(low[tile : tile + 1, :]) for tile in range(SLOT_TILES)], axis=1
    )


def four_pieces(first, second):
    sublanes = jnp.bitwise_and(lax.broadcasted_iota(jnp.int32, (ROWS, first.shape[1]), 0), 3)
    first_top, first_rest = pieces(first)
    second_top, second_rest = pieces(second)
    tops = jnp.where(sublanes == 0, first_top, second_top)
    rests = jnp.where(sublanes == 2, first_rest, second_rest)
    return jnp.where(sublanes < 2, tops, rests)


def masked_store_four(value, high_row, left_ref, column):
    packed = value.astype(BF16)
    quarter = jnp.right_shift(lax.broadcasted_iota(jnp.int32, value.shape, 0), 2).astype(BF16)
    wanted = jnp.broadcast_to(high_row.astype(BF16), value.shape) - quarter
    for block in range(QUADS):
        here = wanted == BF16(4 * block)
        left_ref[row_block(block), lane_block(column)] = jnp.where(here, packed, BF16(0.0))


def two_rows(total, high):
    base = 4 * high
    first = total[base : base + 1, :] + total[base + 2 : base + 3, :]
    second = total[base + 1 : base + 2, :] + total[base + 3 : base + 4, :]
    return first, second


def scatter_slots(load, shared_rows, left_ref, right):
    high_rows = jnp.right_shift(shared_rows, 8)
    for tile in range(SLOT_TILES):
        masked_store(load(tile), high_rows[tile : tile + 1, :], left_ref, tile)
    return scatter_sum(left_ref[:, :SLOTS], right)


def stack_pieces(skeleton):
    top, rest = pieces(skeleton)
    return jnp.concatenate([top.astype(BF16), rest.astype(BF16)], axis=0)


def gather_tile(stacked, rows, keep=None):
    low = jnp.bitwise_and(rows, LOW - 1)
    high = jnp.right_shift(rows, 8)
    selector = one_hot_rows(low)
    if keep is not None:
        keep(selector)
    found = jnp.dot(stacked, selector, preferred_element_type=F32)
    total = None
    for index in range(HIGH):
        part = found[row_block(index), :] + found[row_block(HIGH + index), :]
        part = jnp.where(high == index, part, 0.0)
        total = part if total is None else total + part
    return total


def keep_columns(selectors_ref, column, selector):
    selectors_ref[:, column * LANES : (column + 2) * LANES] = selector


def gather_cycle(skeleton, edge_rows, store, selectors_ref=None):
    stacked = stack_pieces(skeleton)
    for pair in range(CYCLE // 2):
        rows = jnp.concatenate(
            [edge_rows[2 * pair : 2 * pair + 1, :], edge_rows[2 * pair + 1 : 2 * pair + 2, :]], axis=1
        )
        keep = None
        if selectors_ref is not None:
            keep = functools.partial(keep_columns, selectors_ref, 2 * pair)
        total = gather_tile(stacked, rows, keep)
        store(2 * pair, total[:, :LANES])
        store(2 * pair + 1, total[:, LANES:])


def gather_slots(skeleton, shared_rows):
    stacked = stack_pieces(skeleton)
    return [gather_tile(stacked, shared_rows[tile : tile + 1, :]) for tile in range(SLOT_TILES)]


def sent_place(index):
    if index < INNER:
        return index // LINE, index % LINE
    extra = index - INNER
    block = min(extra // 2, MODES - 1)
    row = extra - 2 * block
    return block, row + LINE if row < 2 else row - 2


def kept_place(index):
    block, row = sent_place(index)
    return block, row + 2


EMPTY_PLACES = [(MODES - 1, row) for row in range(2, LINE)]


def read_skeleton(load):
    return jnp.concatenate(
        [jnp.concatenate([load(2 * high), load(2 * high + 1)], axis=1) for high in range(HIGH)], axis=0
    )


def write_skeleton(skeleton, store):
    for high in range(HIGH):
        store(2 * high, skeleton[row_block(high), :LANES])
        store(2 * high + 1, skeleton[row_block(high), LANES:])


def write_place(ref, place):
    def store(index, value):
        block, row = place(index)
        ref[block, row] = value

    return store


def fold(value):
    return value[:, :LANES] + value[:, LANES:]


def per_tile(penalty_ref):
    return jnp.concatenate(
        [jnp.broadcast_to(penalty_ref[high : high + 1, :], (ROWS, LOW)) for high in range(HIGH)], axis=0
    )


def skeleton_sum(product):
    total = None
    for high in range(HIGH):
        part = fold(product[row_block(high), :])
        total = part if total is None else total + part
    return total


def select_arrived(masks, tile, arrived):
    chosen = arrived[0]
    row = masks[tile : tile + 1, :]
    for level in range(1, len(arrived)):
        moving = jnp.bitwise_and(jnp.right_shift(row, level), 1) == 1
        chosen = jnp.where(moving, arrived[level], chosen)
    return chosen


def weighted_sum(weights, values):
    total = None
    for weight, value in zip(weights, values):
        if weight == 0.0:
            continue
        part = float(weight) * value
        total = part if total is None else total + part
    return total


def derivative_line(values, transposed):
    matrix = DERIVATIVE64.T if transposed else DERIVATIVE64
    half = SIDE // 2
    evens = [values[k] + values[ORDER - k] for k in range(half)] + [values[half]]
    odds = [values[k] - values[ORDER - k] for k in range(half)]
    results = [None] * SIDE
    for out in range(half):
        near, far = matrix[out, :half], matrix[out, :half:-1]
        even = weighted_sum(np.float32(np.append(0.5 * (near + far), matrix[out, half])), evens)
        odd = weighted_sum(np.float32(0.5 * (near - far)), odds)
        results[out] = odd + even
        results[ORDER - out] = odd - even
    results[half] = weighted_sum(np.float32(matrix[half, :half]), odds)
    return results


def grid_load(inner_ref, cycle_ref, rows):
    def load(node):
        if node in CYCLE_NODES:
            return cycle_ref[CYCLE_NODES.index(node), rows, :]
        return inner_ref[INNER_NODES.index(node), rows, :]

    return load


def gradients(load, first_ref, metric_ref, rows, visit):
    for j in range(SIDE):
        line = derivative_line([load(k * SIDE + j) for k in range(SIDE)], False)
        for i in range(SIDE):
            first_ref[i * SIDE + j, rows, :] = line[i]
    for i in range(SIDE):
        line = derivative_line([load(i * SIDE + k) for k in range(SIDE)], False)
        seconds = []
        for j in range(SIDE):
            node = i * SIDE + j
            m0, m1, m2 = [metric_ref[node, c : c + 1, :] for c in range(3)]
            g1, g2 = first_ref[node, rows, :], line[j]
            p1 = m0 * g1 + m2 * g2
            p2 = m2 * g1 + m1 * g2
            visit(node, g1, g2, p1, p2)
            seconds.append(p2)
        yield i, seconds


def apply_operator(inner_ref, cycle_ref, result_ref, first_ref, energy_ref, metric_ref, shift_ref):
    for part in range(2):
        rows = slice(part * 8, part * 8 + 8)
        shift = shift_ref[rows, :]
        load = grid_load(inner_ref, cycle_ref, rows)

        def visit(node, g1, g2, p1, p2):
            first_ref[node, rows, :] = p1

        for i, seconds in gradients(load, first_ref, metric_ref, rows, visit):
            line = derivative_line(seconds, True)
            for j in range(SIDE):
                node = i * SIDE + j
                mass = shift * metric_ref[node, 3:4, :]
                result_ref[node, rows, :] = line[j] + mass * load(node)
        energy = jnp.zeros((8, LANES), F32)
        for j in range(SIDE):
            line = derivative_line([first_ref[k * SIDE + j, rows, :] for k in range(SIDE)], True)
            for i in range(SIDE):
                node = i * SIDE + j
                value = result_ref[node, rows, :] + line[i]
                result_ref[node, rows, :] = value
                energy = energy + value * load(node)
        energy_ref[rows, :] = energy


def apply_energy(inner_ref, cycle_ref, first_ref, energy_ref, metric_ref, shift_ref):
    for part in range(2):
        rows = slice(part * 8, part * 8 + 8)
        shift = shift_ref[rows, :]
        load = grid_load(inner_ref, cycle_ref, rows)
        sums = [jnp.zeros((8, LANES), F32)]

        def visit(node, g1, g2, p1, p2):
            value = load(node)
            mass = shift * metric_ref[node, 3:4, :]
            sums[0] = sums[0] + (g1 * p1 + g2 * p2 + mass * value * value)

        for i, seconds in gradients(load, first_ref, metric_ref, rows, visit):
            pass
        energy_ref[rows, :] = sums[0]


def diagonal_cells(metric_ref, table_ref, cross_ref, penalty_ref, inner_ref, padded_ref, cells_ref):
    both = jnp.concatenate([metric_ref[:, 0, :], metric_ref[:, 1, :]], axis=0)
    terms = jnp.dot(table_ref[...], both, precision=HIGHEST, preferred_element_type=F32)
    cells_ref[0] = terms + cross_ref[...] * metric_ref[:, 2, :]
    cells_ref[1] = metric_ref[:, 3, :]
    padded_ref[...] = jnp.ones((HIGH, LOW), F32)
    for high in range(HIGH):
        count = min(LOW, SKEL - high * LOW)
        line = penalty_ref[pl.ds(high * LOW, count)]
        padded_ref[high : high + 1, :count] = line.reshape(1, count)
    for index, node in enumerate(INNER_NODES):
        inner_ref[0, index : index + 1, :] = cells_ref[0, node : node + 1, :]
        inner_ref[1, index : index + 1, :] = cells_ref[1, node : node + 1, :]


def diagonal_slots(total, shared_rows, selectors, padded_ref, skeleton_ref):
    stacked = []
    for high in range(HIGH):
        laplace, mass = two_rows(total, high)
        laplace = laplace + padded_ref[high : high + 1, :]
        skeleton_ref[0, high : high + 1, :] = laplace
        skeleton_ref[1, high : high + 1, :] = mass
        stacked.append(four_pieces(laplace, mass).astype(BF16))
    stacked = jnp.concatenate(stacked, axis=0)
    results = []
    for tile in range(SLOT_TILES):
        high_row = jnp.right_shift(shared_rows[tile : tile + 1, :], 8)
        found = jnp.dot(stacked, selectors[:, lane_block(tile)], preferred_element_type=F32)
        value = jnp.zeros((ROWS, LANES), F32)
        for high in range(HIGH):
            value = value + jnp.where(high_row == high, found[row_block(high), :], 0.0)
        results.append(two_rows(value, 0))
    return results


def pack_kernel(
    forcing_hbm, edge_hbm, shared_hbm, masks_hbm, metric_hbm, penalty_hbm, table_hbm, cross_hbm,
    out_hbm, message_hbm, inner_hbm, skeleton_hbm, padded_hbm, lists_hbm,
    forcing_ref, edge_ref, shared_ref, masks_ref, metric_ref, penalty_ref, table_ref, cross_ref,
    packed_ref, message_ref, inner_ref, skeleton_ref, padded_ref, lists_ref,
    cells_ref, left_ref, selectors_ref, in_semaphores, out_semaphores,
):
    ins = [
        pltpu.make_async_copy(source, target, in_semaphores.at[index])
        for index, (source, target) in enumerate(
            [
                (edge_hbm, edge_ref), (metric_hbm, metric_ref), (table_hbm, table_ref), (cross_hbm, cross_ref),
                (penalty_hbm, penalty_ref), (shared_hbm, shared_ref), (masks_hbm, masks_ref),
                (forcing_hbm, forcing_ref),
            ]
        )
    ]
    for copy in ins:
        copy.start()
    outs = []

    def send(source, target):
        copy = pltpu.make_async_copy(source, target, out_semaphores.at[len(outs)])
        copy.start()
        outs.append(copy)

    base = 2 * HIGH * ROWS
    tail = list(range(TILES - 4)) + [TILES - 2, TILES - 1] + [None] * len(EMPTY_PLACES) + [TILES - 4, TILES - 3]
    for position, index in enumerate(tail):
        if index is None:
            packed_ref[position] = jnp.zeros((ROWS, LANES), F32)
    ins[0].wait()
    edge_rows = edge_ref[...]
    one_hot_cycle(edge_rows, selectors_ref)
    for copy in ins[1:7]:
        copy.wait()
    shared_rows = shared_ref[...]
    lists_ref[:SLOT_TILES, :] = shared_rows
    lists_ref[SLOT_TILES : 2 * SLOT_TILES, :] = masks_ref[...]
    lists_ref[2 * SLOT_TILES :, :] = jnp.zeros((8 - 2 * SLOT_TILES, LANES), jnp.int32)
    send(lists_ref, lists_hbm)
    diagonal_cells(metric_ref, table_ref, cross_ref, penalty_ref, inner_ref, padded_ref, cells_ref)
    send(inner_ref, inner_hbm)
    send(padded_ref, padded_hbm)
    ins[7].wait()
    for line in range(LINE):
        send(forcing_ref.at[pl.ds((line + 1) * SIDE + 1, LINE)], out_hbm.at[pl.ds(line * BLOCK, LINE)])
    high_rows = jnp.right_shift(edge_rows, 8)
    for slot in range(CYCLE):
        node = CYCLE_NODES[slot]
        high_row = high_rows[slot : slot + 1, :]
        masked_store(forcing_ref[node], high_row, left_ref, slot)
        value = four_pieces(cells_ref[0, node : node + 1, :], cells_ref[1, node : node + 1, :])
        masked_store_four(value, high_row, left_ref.at[pl.ds(base, QUADS * ROWS)], slot)
    total = contract_lanes(left_ref[...], selectors_ref[...])
    skeleton = total[: HIGH * ROWS] + total[HIGH * ROWS : base]

    def store(index, value):
        packed_ref[tail.index(index)] = value

    write_skeleton(skeleton, store)
    for line in range(LINE):
        send(packed_ref.at[pl.ds(2 * line, 2)], out_hbm.at[pl.ds(line * BLOCK + LINE, 2)])
    send(packed_ref.at[pl.ds(TILES - 4, BLOCK)], out_hbm.at[pl.ds(LINE * BLOCK, BLOCK)])
    selectors = slot_selectors(shared_rows)
    pairs = diagonal_slots(total[base:], shared_rows, selectors, padded_ref, skeleton_ref)
    send(skeleton_ref, skeleton_hbm)
    for tile, value in enumerate(gather_slots(skeleton, shared_rows)):
        laplace, mass = pairs[tile]
        message_ref[tile, :ROWS, :] = value
        message_ref[tile, ROWS:, :] = jnp.zeros((8, LANES), F32)
        message_ref[tile, ROWS : ROWS + 1, :] = laplace
        message_ref[tile, ROWS + 1 : ROWS + 2, :] = mass
    send(message_ref, message_hbm)
    for copy in outs:
        copy.wait()


def place(index):
    return pl.ds(pl.multiple_of(index * ROWS, ROWS), ROWS)


def relative_rows(matrix_ref, mode):
    parts = [matrix_ref[place(jnp.bitwise_xor(mode, step)), :] for step in range(MODES)]
    return jnp.concatenate(parts, axis=0)


def transform_kernel(
    matrix_ref, in_ref, a0, a2, a1, a3, a4, lists_ref, o0, o1, o2, o3, o4, o5, o6, o7, extra_ref, slots_ref
):
    mode = lax.axis_index("mode")
    outs = [o0, o1, o2, o3, o4, o5, o6, o7]
    matrix = relative_rows(matrix_ref, mode)
    slots_ref[...] = jnp.zeros(slots_ref.shape, F32)
    arrived_refs = [a0, a1, a2, a3, a4]
    masks = lists_ref[SLOT_TILES : 2 * SLOT_TILES, :]
    for index in range(BLOCK):
        block = in_ref[:, index].reshape(PLANES, LANES)
        mixed = jnp.dot(matrix, block, precision=HIGHEST, preferred_element_type=F32)
        for step, out_ref in enumerate(outs):
            out_ref[index] = mixed[row_block(step), :]
    for tile in range(SLOT_TILES):
        chosen = select_arrived(masks, tile, [ref[tile] for ref in arrived_refs])
        slots_ref[tile, place(mode), :] = chosen[:ROWS]
        mixed = jnp.dot(matrix, slots_ref[tile], precision=HIGHEST, preferred_element_type=F32)
        for step, out_ref in enumerate(outs):
            out_ref[BLOCK + tile] = mixed[row_block(step), :]
        extra_ref[tile] = chosen[ROWS:]


def column_kernel(inner_ref, o0, o1, o2, o3, o4, o5, o6, o7, out_ref):
    mode = lax.axis_index("mode")
    start = jnp.minimum(mode, LINE - 1) * LINE
    for step, in_ref in enumerate([o0, o1, o2, o3, o4, o5, o6, o7]):
        origin = jnp.bitwise_xor(mode, step)
        shift = helmholtz_shift(origin)
        for index in range(LINE):
            laplace = inner_ref[0, pl.ds(start + index, 1), :]
            mass = inner_ref[1, pl.ds(start + index, 1), :]
            out_ref[index, place(origin), :] = in_ref[index] * (1.0 / (laplace + shift * mass))


def first_kernel(
    i4, i7, i5, i2, i6, i3, i1, i0, extra_ref, lists_ref, edge_ref, metric_ref,
    inner_ref, diagonal_ref, penalty_ref, search_ref, inverse_ref, result_ref, source_ref, kept_ref, slots_ref,
    sums_ref, left_ref, right_ref, cycle_ref, first_ref, energy_ref, shift_ref,
):
    mode = lax.axis_index("mode")
    ins = [i0, i1, i2, i3, i4, i5, i6, i7]
    for step, in_ref in enumerate(ins):
        source_ref[jnp.bitwise_xor(mode, step)] = in_ref[:BLOCK]
    shared_rows = lists_ref[:SLOT_TILES, :]
    right_slots = slot_selectors(shared_rows)
    shift = helmholtz_shift(lax.axis_index("mode"))
    shift_ref[...] = shift
    edge_rows = edge_ref[...]

    def load_right(tile):
        total = ins[0][BLOCK + tile]
        for in_ref in ins[1:]:
            total = total + in_ref[BLOCK + tile]
        return total

    def source(index):
        block, row = sent_place(index)
        return source_ref[block, row]

    high_rows = jnp.right_shift(shared_rows, 8)
    for tile in range(SLOT_TILES):
        value = four_pieces(extra_ref[tile, 0:1, :], extra_ref[tile, 1:2, :])
        masked_store_four(value, high_rows[tile : tile + 1, :], left_ref, tile)
    added = contract_lanes(left_ref[: QUADS * ROWS, :SLOTS], right_slots)
    wide_shift = jnp.concatenate([shift, shift], axis=1)
    parts = []
    for high in range(HIGH):
        laplace, mass = two_rows(added, high)
        laplace = laplace + diagonal_ref[0, high : high + 1, :]
        mass = mass + diagonal_ref[1, high : high + 1, :]
        parts.append(1.0 / (laplace + wide_shift * mass))
    inverse = jnp.concatenate(parts, axis=0)
    local = read_skeleton(lambda index: source(INNER + index))
    right_side = local + scatter_slots(load_right, shared_rows, left_ref, right_slots)
    search = right_side * inverse
    kept_ref[0] = local
    kept_ref[1] = inverse
    kept_ref[2] = search
    start = skeleton_sum(local * search)
    for index, node in enumerate(INNER_NODES):
        value = source(index)
        inverted = 1.0 / (inner_ref[0, index : index + 1, :] + shift * inner_ref[1, index : index + 1, :])
        scaled = value * inverted
        search_ref[index] = scaled
        inverse_ref[index] = inverted
        start = start + value * scaled

    def store(slot, value):
        cycle_ref[slot] = value

    gather_cycle(search, edge_rows, store, right_ref)
    apply_operator(search_ref, cycle_ref, result_ref, first_ref, energy_ref, metric_ref, shift_ref)
    weighted = per_tile(penalty_ref) * search
    applied = weighted + scatter_cycle(
        lambda slot: result_ref[CYCLE_NODES[slot]], edge_rows, left_ref, right_ref
    )
    kept_ref[3] = applied
    for tile, value in enumerate(gather_slots(applied, shared_rows)):
        slots_ref[tile] = value
    sums_ref[0] = energy_ref[...] + skeleton_sum(weighted * search)
    sums_ref[1] = start


def change_kernel(search_ref, inverse_ref, result_ref, source_ref, kept_ref, moved_ref, sums_ref, both_ref):
    crossed = jnp.zeros((ROWS, LANES), F32)
    sourced = jnp.zeros((ROWS, LANES), F32)
    for index, node in enumerate(INNER_NODES):
        block, row = sent_place(index)
        value = result_ref[node]
        search = search_ref[index]
        moved = value * inverse_ref[index] - search
        moved_ref[index] = moved
        both_ref[block, row] = moved
        crossed = crossed + value * moved
        sourced = sourced + source_ref[block, row] * moved
    for high in range(HIGH):
        for part in range(2):
            block, row = kept_place(INNER + 2 * high + part)
            both_ref[block, row] = kept_ref[2, row_block(high), lane_block(part)]
    for block, row in EMPTY_PLACES[2:]:
        both_ref[block, row] = jnp.zeros((ROWS, LANES), F32)
    sums_ref[0] = crossed
    sums_ref[1] = sourced


def second_kernel(
    kept_ref, moved_sums_ref, filled_ref, a0, a2, a1, a3, a4, lists_ref,
    change_ref, sums_ref, both_ref, o0, o1, o2, o3, o4, o5, o6, o7, left_ref,
):
    arrived_refs = [a0, a1, a2, a3, a4]
    masks = lists_ref[SLOT_TILES : 2 * SLOT_TILES, :]
    shared_rows = lists_ref[:SLOT_TILES, :]

    def load(tile):
        return select_arrived(masks, tile, [ref[tile] for ref in arrived_refs])

    local, inverse, search, applied = [kept_ref[index] for index in range(4)]
    full = applied + scatter_slots(load, shared_rows, left_ref, slot_selectors(shared_rows))
    change = full * inverse - search
    for high in range(HIGH):
        for part in range(2):
            block, row = sent_place(INNER + 2 * high + part)
            both_ref[block, row] = change[row_block(high), lane_block(part)]
    mode = lax.axis_index("mode")
    for step, out_ref in enumerate([o0, o1, o2, o3, o4, o5, o6, o7]):
        out_ref[...] = both_ref[jnp.bitwise_xor(mode, step)]
    change_ref[...] = change
    sums_ref[0] = moved_sums_ref[0] + skeleton_sum(applied * change)
    sums_ref[1] = moved_sums_ref[1] + skeleton_sum(local * change)


def energy_kernel(
    moved_ref, change_ref, sums_ref, changed_sums_ref, edge_ref, metric_ref, penalty_ref, message_ref,
    cycle_ref, first_ref, energy_ref, shift_ref,
):
    shift_ref[...] = helmholtz_shift(lax.axis_index("mode"))
    change = change_ref[...]

    def store(slot, value):
        cycle_ref[slot] = value

    gather_cycle(change, edge_ref[...], store)
    apply_energy(moved_ref, cycle_ref, first_ref, energy_ref, metric_ref, shift_ref)
    energy = energy_ref[...] + skeleton_sum(per_tile(penalty_ref) * change * change)
    sublanes = lax.broadcasted_iota(jnp.int32, (ROWS, LANES), 0)
    lanes = lax.broadcasted_iota(jnp.int32, (ROWS, LANES), 1)
    spread = jnp.zeros((ROWS, LANES), F32)
    for index, value in enumerate([sums_ref[0], changed_sums_ref[0], energy, sums_ref[1], changed_sums_ref[1]]):
        column = jnp.sum(value, axis=1, keepdims=True)
        spread = jnp.where(lanes == sublanes + index * ROWS, column, spread)
    message = jnp.sum(spread, axis=0, keepdims=True)
    message_ref[...] = jnp.broadcast_to(message, message_ref.shape)


def combine_kernel(
    matrix_ref, scalars_ref, column_ref, i4, i7, i5, i2, i6, i3, i1, i0, o0, o1, o2, o3, o4, o5, o6, o7, block_ref
):
    mode = lax.axis_index("mode")
    sublanes = lax.broadcasted_iota(jnp.int32, (ROWS, LANES), 0)
    lanes = lax.broadcasted_iota(jnp.int32, (ROWS, LANES), 1)
    for step, in_ref in enumerate([i0, i1, i2, i3, i4, i5, i6, i7]):
        origin = jnp.bitwise_xor(mode, step)
        total = jnp.sum(scalars_ref[origin], axis=0, keepdims=True)
        g00, g01, g11, h0, h1 = [
            jnp.sum(jnp.where(lanes == sublanes + index * ROWS, total, 0.0), axis=1, keepdims=True)
            for index in range(SCALARS)
        ]
        ratio = g01 / g00
        pivot = g11 - ratio * g01
        second = jnp.where(pivot > 0.0, (h1 - ratio * h0) / pivot, 0.0)
        first = h0 / g00 - ratio * second
        for index in range(BLOCK):
            if index < LINE:
                search = column_ref[index, place(origin), :]
                if index < 2:
                    search = jnp.where(mode == MODES - 1, in_ref[index + 2], search)
            else:
                search = in_ref[index + 2]
            block_ref[index, place(origin), :] = first * search + second * in_ref[index]
    matrix = relative_rows(matrix_ref, mode)
    for index in range(BLOCK):
        mixed = jnp.dot(matrix, block_ref[index], precision=HIGHEST, preferred_element_type=F32)
        for step, out_ref in enumerate([o0, o1, o2, o3, o4, o5, o6, o7]):
            out_ref[index] = mixed[row_block(step), :]


def unpack_kernel(
    i4, i7, i5, i2, i6, i3, i1, i0, edge_ref, out_hbm, packed_ref, out_ref, semaphores
):
    mode = lax.axis_index("mode")
    for step, in_ref in enumerate([i0, i1, i2, i3, i4, i5, i6, i7]):
        packed_ref[jnp.bitwise_xor(mode, step)] = in_ref[...]

    def load(index):
        block, row = sent_place(index)
        return packed_ref[block, row]

    for index, node in enumerate(INNER_NODES):
        out_ref[node] = load(index)
    spans = [(SIDE, (SIDE - 2) * SIDE), (0, SIDE), (ORDER * SIDE, SIDE)]
    copies = [
        pltpu.make_async_copy(out_ref.at[pl.ds(*span)], out_hbm.at[pl.ds(*span)], semaphores.at[index])
        for index, span in enumerate(spans)
    ]

    def store(slot, value):
        out_ref[CYCLE_NODES[slot]] = value
        if slot == 2 * SIDE - 1:
            copies[0].start()
        if slot == CYCLE - 1:
            copies[1].start()
            copies[2].start()

    gather_cycle(read_skeleton(lambda index: load(INNER + index)), edge_ref[...], store)
    for copy in copies:
        copy.wait()


def call(kernel, out_shapes, scratch, *operands, limit=VMEM_LIMIT, **options):
    return pl.pallas_call(
        kernel,
        out_shape=out_shapes,
        scratch_shapes=scratch,
        compiler_params=pltpu.CompilerParams(vmem_limit_bytes=limit),
        **options,
    )(*operands)


def shape(*dims, dtype=F32):
    return jax.ShapeDtypeStruct(dims, dtype)


def swap_blocks(blocks, axis):
    return lax.all_to_all(blocks, axis, split_axis=0, concat_axis=0, tiled=True)


def permute(value, axis, flip):
    return lax.ppermute(value, axis, [(i, i ^ flip) for i in range(lax.axis_size(axis))])


def swap_steps(blocks):
    return [permute(blocks[step], "mode", step) for step in STEP_ORDER] + [blocks[0]]


def exchange(slots):
    return [permute(slots, "elem", 1 << level) for level in LEVEL_ORDER]


def body(forcing, metric, edge_map, shared_rows, partner_masks, penalty):
    forward, backward = [jnp.asarray(part) for part in fourier_tables()]
    table, cross = [jnp.asarray(part) for part in diagonal_tables()]
    metric = metric.transpose(1, 0, 2)
    edge_rows = edge_map.T
    shared = shared_rows.reshape(SLOT_TILES, LANES)
    masks = partner_masks.reshape(SLOT_TILES, LANES)
    left = pltpu.VMEM((2 * HIGH * ROWS, CYCLE * LANES), BF16)
    right = pltpu.VMEM((LOW, CYCLE * LANES), BF16)
    left_slots = pltpu.VMEM((2 * HIGH * ROWS, SLOTS), BF16)
    cycle = pltpu.VMEM((CYCLE, ROWS, LANES), F32)
    first = pltpu.VMEM((NODES, ROWS, LANES), F32)
    energy = pltpu.VMEM((ROWS, LANES), F32)
    packing = pltpu.VMEM((MODES, BLOCK, ROWS, LANES), F32)
    wide = (HIGH * ROWS, LOW)
    blocks = [shape(BLOCK, ROWS, LANES)] * MODES

    hbm = pl.BlockSpec(memory_space=pltpu.HBM)
    packed_shapes = [
        shape(MODES * BLOCK, ROWS, LANES), shape(SLOT_TILES, ROWS + 8, LANES),
        shape(2, INNER, LANES), shape(2, HIGH, LOW), shape(HIGH, LOW), shape(8, LANES, dtype=jnp.int32),
    ]
    operands = [forcing.transpose(1, 0, 2), edge_rows, shared, masks, metric, penalty, table, cross]
    packed, message, inner, diagonal, penalties, lists = call(
        pack_kernel, packed_shapes,
        [pltpu.VMEM(operand.shape, operand.dtype) for operand in operands]
        + [pltpu.VMEM((MODES * BLOCK - INNER, ROWS, LANES), F32)]
        + [pltpu.VMEM(part.shape, part.dtype) for part in packed_shapes[1:]]
        + [
            pltpu.VMEM((2, NODES, LANES), F32), pltpu.VMEM(((2 * HIGH + QUADS) * ROWS, CYCLE * LANES), BF16), right,
            pltpu.SemaphoreType.DMA((len(operands),)), pltpu.SemaphoreType.DMA((2 * LINE + 6,)),
        ],
        *operands,
        in_specs=[hbm] * len(operands), out_specs=[hbm] * len(packed_shapes), limit=FIRST_LIMIT,
    )
    gathered = swap_blocks(packed.reshape(MODES, BLOCK, ROWS, LANES), "mode")
    *mixed, extra = call(
        transform_kernel, [shape(SHARE, ROWS, LANES)] * MODES + [shape(SLOT_TILES, 8, LANES)],
        [pltpu.VMEM((SLOT_TILES, PLANES, LANES), F32)], forward, gathered, *exchange(message), lists,
    )
    column = call(column_kernel, shape(LINE, PLANES, LANES), [], inner, *mixed)
    inside = shape(INNER, ROWS, LANES)
    search, inverse, applied, source, kept, slots, sums = call(
        first_kernel,
        [
            inside, inside, shape(NODES, ROWS, LANES), shape(MODES, BLOCK, ROWS, LANES), shape(4, *wide),
            shape(SLOT_TILES, ROWS, LANES), shape(2, ROWS, LANES),
        ],
        [left, right, cycle, first, energy, energy],
        *swap_steps(mixed), extra, lists, edge_rows, metric, inner, diagonal, penalties,
    )
    pair = shape(MODES, PAIRED, ROWS, LANES)
    moved, moved_sums, filled = call(
        change_kernel, [inside, shape(2, ROWS, LANES), pair], [], search, inverse, applied, source, kept
    )
    change, changed_sums, both, *pairs = call(
        second_kernel,
        [shape(*wide), shape(2, ROWS, LANES), pair] + [shape(PAIRED, ROWS, LANES)] * MODES,
        [left_slots],
        kept, moved_sums, filled, *exchange(slots), lists,
        input_output_aliases={2: 2},
    )
    message = call(
        energy_kernel, shape(MODES * ELEMS_AXIS, LANES), [cycle, first, energy, energy],
        moved, change, sums, changed_sums, edge_rows, metric, penalties,
    )
    scalars = swap_blocks(message, ("mode", "elem")).reshape(MODES, ELEMS_AXIS, LANES)
    mixed = call(
        combine_kernel, blocks, [pltpu.VMEM((BLOCK, PLANES, LANES), F32)], backward, scalars, column,
        *swap_steps(pairs)
    )
    result = call(
        unpack_kernel, shape(NODES, ROWS, LANES),
        [packing, pltpu.VMEM((NODES, ROWS, LANES), F32), pltpu.SemaphoreType.DMA((3,))],
        *swap_steps(mixed), edge_rows, out_specs=hbm,
    )
    return result.transpose(1, 0, 2)


def solution(mesh):
    placed = (
        P("mode", None, "elem"),
        P(None, None, "elem"),
        P("elem", None),
        P("elem"),
        P("elem"),
        P("elem"),
    )
    return jax.shard_map(
        body, mesh=mesh, in_specs=placed, out_specs=P("mode", None, "elem"), check_vma=False
    )
```
